32 devices in a mesh: dp: 8 (over z, y), mp: 4 (over x, core).
Axes of the slice: x: 2, y: 2, z: 4, core: 2. Of those that a mesh axis runs over, the one named last changes fastest.
Arguments:
- pieces: bfloat16 [1024, 7, 512], P(('dp', 'mp')), may hold values from -6 to 6
- script_tags: int32 [1024], P(('dp', 'mp')), may hold values from 0 to 15
- counts: int32 [1024], P(('dp', 'mp')), may hold values from 1 to 7
- cotangent: bfloat16 [1024, 2048], P(('dp', 'mp')), may hold values from -6 to 6
- qkv_weight: float32 [2, 3, 512, 512], P(None, None, 'dp'), may hold values from -0.25 to 0.25
- qkv_first: float32 [2, 3, 512, 512], P(None, None, 'dp'), may hold values from -0.00061035156 to 0.00061035156
- qkv_second: float32 [2, 3, 512, 512], P(None, None, 'dp'), may hold values from 1.3599255e-10 to 5.439702e-10
- out_weight: float32 [2, 512, 512], P(None, None, 'dp'), may hold values from -0.5 to 0.5
- out_first: float32 [2, 512, 512], P(None, None, 'dp'), may hold values from -0.00061035156 to 0.00061035156
- out_second: float32 [2, 512, 512], P(None, None, 'dp'), may hold values from 1.3599255e-10 to 5.439702e-10
- up_weight: float32 [2, 512, 2048], P(None, 'dp'), may hold values from -0.25 to 0.25
- up_first: float32 [2, 512, 2048], P(None, 'dp'), may hold values from -0.00061035156 to 0.00061035156
- up_second: float32 [2, 512, 2048], P(None, 'dp'), may hold values from 1.3599255e-10 to 5.439702e-10
- down_weight: float32 [2, 2048, 512], P(None, None, 'dp'), may hold values from -0.125 to 0.125
- down_first: float32 [2, 2048, 512], P(None, None, 'dp'), may hold values from -0.00061035156 to 0.00061035156
- down_second: float32 [2, 2048, 512], P(None, None, 'dp'), may hold values from 1.3599255e-10 to 5.439702e-10
- proj_weight: float32 [512, 2048], P('dp'), may hold values from -0.25 to 0.25
- proj_first: float32 [512, 2048], P('dp'), may hold values from -0.00061035156 to 0.00061035156
- proj_second: float32 [512, 2048], P('dp'), may hold values from 1.3599255e-10 to 5.439702e-10
- norm_gain: float32 [5, 512], replicated, may hold values from 0.5 to 1.5
- gain_first: float32 [5, 512], replicated, may hold values from -0.00061035156 to 0.00061035156
- gain_second: float32 [5, 512], replicated, may hold values from 1.3599255e-10 to 5.439702e-10
- norm_bias: float32 [5, 512], replicated, may hold values from -4 to 4
- bias_first: float32 [5, 512], replicated, may hold values from -0.00061035156 to 0.00061035156
- bias_second: float32 [5, 512], replicated, may hold values from 1.3599255e-10 to 5.439702e-10
- group_table: float32 [16, 512], replicated, may hold values from -6 to 6
- table_first: float32 [16, 512], replicated, may hold values from -0.00061035156 to 0.00061035156
- table_second: float32 [16, 512], replicated, may hold values from 1.3599255e-10 to 5.439702e-10
Outputs:
- embeddings: float32 [1024, 2048], P(('dp', 'mp'))
- input_grad: float32 [1024, 7, 512], P(('dp', 'mp'))
- grad_norm: float32 [], replicated
- new_qkv: float32 [2, 3, 512, 512], P(None, None, 'dp')
- new_qkv_first: float32 [2, 3, 512, 512], P(None, None, 'dp')
- new_qkv_second: float32 [2, 3, 512, 512], P(None, None, 'dp')
- new_out: float32 [2, 512, 512], P(None, None, 'dp')
- new_out_first: float32 [2, 512, 512], P(None, None, 'dp')
- new_out_second: float32 [2, 512, 512], P(None, None, 'dp')
- new_up: float32 [2, 512, 2048], P(None, 'dp')
- new_up_first: float32 [2, 512, 2048], P(None, 'dp')
- new_up_second: float32 [2, 512, 2048], P(None, 'dp')
- new_down: float32 [2, 2048, 512], P(None, None, 'dp')
- new_down_first: float32 [2, 2048, 512], P(None, None, 'dp')
- new_down_second: float32 [2, 2048, 512], P(None, None, 'dp')
- new_proj: float32 [512, 2048], P('dp')
- new_proj_first: float32 [512, 2048], P('dp')
- new_proj_second: float32 [512, 2048], P('dp')
- new_gain: float32 [5, 512], replicated
- new_gain_first: float32 [5, 512], replicated
- new_gain_second: float32 [5, 512], replicated
- new_bias: float32 [5, 512], replicated
- new_bias_first: float32 [5, 512], replicated
- new_bias_second: float32 [5, 512], replicated
- new_table: float32 [16, 512], replicated
- new_table_first: float32 [16, 512], replicated
- new_table_second: float32 [16, 512], replicated
The draws below stay inside these ranges and needn't reach their ends.
All inputs are finite; a program needn't handle non-finite values.
Results may differ from the reference program's by a relative error of at most 0.02.
Values may be sent and summed in bfloat16 or wider, within the bound.
A program may use at most 128 MiB of HBM per device.

```python
import math
import jax
import jax.numpy as jnp
import numpy as np
from jax import lax

D = 512
H = 8
HD = 64
FF = 2048
OUT = 2048
PIECES = 7
LAYERS = 2
GROUPS = 16
STEP = 10
ENTRIES = 1024
NORMS = 5
PARAMS = 7353344


def place_ends(array, rng, least, top_value):
    longest = array.shape.index(max(array.shape))
    spots = []
    for shift in (0, 1):
        where = [jax.random.randint(jax.random.fold_in(rng, axis), (), 0, length) for axis, length in enumerate(array.shape)]
        where[longest] = (where[longest] + shift) % array.shape[longest]
        spots.append(tuple(where))
    return array.at[spots[0]].set(least).at[spots[1]].set(top_value)


def shard_levels(stream_key, extent, cuts, smallest, top_value):
    factor_of, own = 1.0, jax.random.fold_in(stream_key, 6)
    for axis_at, shards_of in cuts:
        heights = jnp.exp(jax.random.uniform(jax.random.fold_in(own, axis_at), (shards_of,), jnp.float32, smallest / len(cuts), top_value / len(cuts)))
        factor_of = factor_of * jnp.repeat(heights, extent[axis_at] // shards_of).reshape([-1 if axis == axis_at else 1 for axis in range(len(extent))])
    return factor_of


def cumulative_ranks(count, slope):
    loads = [(1 << 20) // math.isqrt(standing ** slope) + 1 for standing in range(1, count + 1)]
    deviation = 1 + sum(loads) // (1 << 30)
    return np.cumsum(np.array([max(1, weight // deviation) for weight in loads]))


def ranked(own_key, shape, number_of, skew):
    grid = cumulative_ranks(number_of, skew)
    ticket = jax.random.randint(jax.random.fold_in(own_key, 1), shape, 0, int(grid[number_of - 1]))
    grade = jnp.searchsorted(jnp.asarray(grid, jnp.int32), ticket, side="right")
    return jax.random.permutation(jax.random.fold_in(own_key, 2), number_of)[grade].astype(jnp.int32)


def normal_values(key, shape, scale, limit, cuts=(), kind=jnp.bfloat16):
    result = scale * jax.random.normal(key, shape, jnp.float32)
    if cuts:
        result = result * shard_levels(key, shape, cuts, -0.22, 0.18)
    return jnp.clip(result, -limit, limit).astype(kind)


def setup_inputs(seed: int = 0) -> dict:
    arg_keys = jax.random.split(jax.random.key(seed), 29)
    return {
        "pieces": normal_values(arg_keys[0], (ENTRIES, PIECES, D), 1.0, 6.0, ((0, 32),)),
        "script_tags": place_ends(ranked(arg_keys[1], (ENTRIES,), GROUPS, 2), jax.random.fold_in(arg_keys[1], 3), 0, GROUPS - 1).astype(jnp.int32),
        "counts": place_ends(jax.random.randint(arg_keys[2], (ENTRIES,), 1, PIECES + 1), jax.random.fold_in(arg_keys[2], 1), 1, PIECES).astype(jnp.int32),
        "cotangent": normal_values(arg_keys[3], (ENTRIES, OUT), 1.0, 6.0, ((0, 32),)),
        "qkv_weight": normal_values(arg_keys[4], (LAYERS, 3, D, D), D ** -0.5, 0.25, ((2, 8),), jnp.float32),
        "qkv_first": normal_values(arg_keys[5], (LAYERS, 3, D, D), (0.11 / PARAMS ** 0.5), 0.00061035156, ((2, 8),), jnp.float32),
        "qkv_second": jnp.clip(jnp.exp(math.log(5.439702022158599e-10) - 1.3862944 * jax.random.uniform(arg_keys[6], (LAYERS, 3, D, D), jnp.float32) ** shard_levels(arg_keys[6], (LAYERS, 3, D, D), ((2, 8),), -0.2, 0.2)), 1.3599255055396497e-10, 5.439702022158599e-10),
        "out_weight": normal_values(arg_keys[7], (LAYERS, D, D), (D // 4) ** -0.5, 0.5, ((2, 8),), jnp.float32),
        "out_first": normal_values(arg_keys[8], (LAYERS, D, D), (0.11 / PARAMS ** 0.5), 0.00061035156, ((2, 8),), jnp.float32),
        "out_second": jnp.clip(jnp.exp(math.log(5.439702022158599e-10) - 1.3862944 * jax.random.uniform(arg_keys[9], (LAYERS, D, D), jnp.float32) ** shard_levels(arg_keys[9], (LAYERS, D, D), ((2, 8),), -0.2, 0.2)), 1.3599255055396497e-10, 5.439702022158599e-10),
        "up_weight": normal_values(arg_keys[10], (LAYERS, D, FF), D ** -0.5, 0.25, ((1, 8),), jnp.float32),
        "up_first": normal_values(arg_keys[11], (LAYERS, D, FF), (0.11 / PARAMS ** 0.5), 0.00061035156, ((1, 8),), jnp.float32),
        "up_second": jnp.clip(jnp.exp(math.log(5.439702022158599e-10) - 1.3862944 * jax.random.uniform(arg_keys[12], (LAYERS, D, FF), jnp.float32) ** shard_levels(arg_keys[12], (LAYERS, D, FF), ((1, 8),), -0.2, 0.2)), 1.3599255055396497e-10, 5.439702022158599e-10),
        "down_weight": normal_values(arg_keys[13], (LAYERS, FF, D), FF ** -0.5, 0.125, ((2, 8),), jnp.float32),
        "down_first": normal_values(arg_keys[14], (LAYERS, FF, D), (0.11 / PARAMS ** 0.5), 0.00061035156, ((2, 8),), jnp.float32),
        "down_second": jnp.clip(jnp.exp(math.log(5.439702022158599e-10) - 1.3862944 * jax.random.uniform(arg_keys[15], (LAYERS, FF, D), jnp.float32) ** shard_levels(arg_keys[15], (LAYERS, FF, D), ((2, 8),), -0.2, 0.2)), 1.3599255055396497e-10, 5.439702022158599e-10),
        "proj_weight": normal_values(arg_keys[16], (D, OUT), D ** -0.5, 0.25, ((0, 8),), jnp.float32),
        "proj_first": normal_values(arg_keys[17], (D, OUT), (0.11 / PARAMS ** 0.5), 0.00061035156, ((0, 8),), jnp.float32),
        "proj_second": jnp.clip(jnp.exp(math.log(5.439702022158599e-10) - 1.3862944 * jax.random.uniform(arg_keys[18], (D, OUT), jnp.float32) ** shard_levels(arg_keys[18], (D, OUT), ((0, 8),), -0.2, 0.2)), 1.3599255055396497e-10, 5.439702022158599e-10),
        "norm_gain": jnp.clip(1.0 + 0.1 * jax.random.normal(arg_keys[19], (NORMS, D), jnp.float32), 0.5, 1.5),
        "gain_first": normal_values(arg_keys[20], (NORMS, D), (0.11 / PARAMS ** 0.5), 0.00061035156, (), jnp.float32),
        "gain_second": jnp.clip(jnp.exp(jax.random.uniform(arg_keys[21], (NORMS, D), jnp.float32, math.log(1.3599255055396497e-10), math.log(5.439702022158599e-10))), 1.3599255055396497e-10, 5.439702022158599e-10),
        "norm_bias": normal_values(arg_keys[22], (NORMS, D), 0.3, 4.0, (), jnp.float32),
        "bias_first": normal_values(arg_keys[23], (NORMS, D), (0.11 / PARAMS ** 0.5), 0.00061035156, (), jnp.float32),
        "bias_second": jnp.clip(jnp.exp(jax.random.uniform(arg_keys[24], (NORMS, D), jnp.float32, math.log(1.3599255055396497e-10), math.log(5.439702022158599e-10))), 1.3599255055396497e-10, 5.439702022158599e-10),
        "group_table": normal_values(arg_keys[25], (GROUPS, D), 0.5, 6.0, (), jnp.float32),
        "table_first": normal_values(arg_keys[26], (GROUPS, D), (0.11 / PARAMS ** 0.5), 0.00061035156, (), jnp.float32),
        "table_second": jnp.clip(jnp.exp(jax.random.uniform(arg_keys[27], (GROUPS, D), jnp.float32, math.log(1.3599255055396497e-10), math.log(5.439702022158599e-10))), 1.3599255055396497e-10, 5.439702022158599e-10),
    }


@jax.custom_vjp
def low(v):
    return lax.optimization_barrier(v.astype(jnp.bfloat16)).astype(jnp.float32)

@jax.custom_vjp
def low_back(v):
    return v

def low_keep(v):
    return (low(v), None)

def low_pass(kept, grad):
    return (grad,)

def back_keep(v):
    return (v, None)

def back_low(kept, grad):
    return (low(grad),)
low.defvjp(low_keep, low_pass)
low_back.defvjp(back_keep, back_low)
norm_eps = 1e-05
beta_first = 0.9
beta_second = 0.999
adam_eps = 1e-08
learn_rate = 0.03
small_rate = 0.5
decay_rate = 0.01
clip_level = 1.0
masked_score = -1000000000.0
highest = lax.Precision.HIGHEST

def layer_norm(values, gain_row, bias_row):
    centre = lax.optimization_barrier(jnp.mean(values, axis=-1, keepdims=True))
    offset = values - centre
    spread = lax.optimization_barrier(jnp.mean(offset * offset, axis=-1, keepdims=True))
    return offset * lax.rsqrt(spread + norm_eps) * gain_row + bias_row

def dense_dot(left_side, right_side):
    return jnp.dot(left_side, right_side, precision=highest)

def adam_update(weight, first, second, gradient, clip_scale, decay, step_rate):
    clipped = gradient * clip_scale
    first_new = beta_first * first + (1.0 - beta_first) * clipped
    second_new = beta_second * second + (1.0 - beta_second) * clipped * clipped
    first_hat = first_new / (1.0 - beta_first ** STEP)
    second_hat = second_new / (1.0 - beta_second ** STEP)
    weight_new = weight - step_rate * (first_hat / (jnp.sqrt(second_hat) + adam_eps) + decay * weight)
    return (weight_new, first_new, second_new)

def reference(pieces, script_tags, counts, cotangent, qkv_weight, qkv_first, qkv_second, out_weight, out_first, out_second, up_weight, up_first, up_second, down_weight, down_first, down_second, proj_weight, proj_first, proj_second, norm_gain, gain_first, gain_second, norm_bias, bias_first, bias_second, group_table, table_first, table_second):
    entries = pieces.shape[0]
    block_size = math.gcd(entries, 512)
    blocks_total = entries // block_size
    block_rows = block_size * PIECES
    score_scale = HD ** (-0.5)

    def forward(inputs, w_qkv, w_out, w_up, w_down, w_proj, gains, biases, table):
        low_qkv = low(w_qkv)
        low_out = low(w_out)
        low_up = low(w_up)
        low_down = low(w_down)
        low_proj = low(w_proj)

        def block_fn(inputs_block, tags_block, counts_block):
            stream = (inputs_block + table[tags_block][:, None, :]).reshape(block_rows, D)
            keymask = jnp.arange(PIECES, dtype=jnp.int32)[None, :] < counts_block[:, None]
            for layer_index in range(LAYERS):
                normed = low(layer_norm(stream, gains[2 * layer_index], biases[2 * layer_index]))
                qkv_rows = low_back(low(jnp.einsum('rd,tdc->rtc', normed, low_qkv[layer_index], precision=highest)))
                split_heads = qkv_rows.reshape(block_size, PIECES, 3, H, HD)
                scores = jnp.einsum('eqhd,ekhd->ehqk', split_heads[:, :, 0], split_heads[:, :, 1], precision=highest) * score_scale
                scores = low_back(scores)
                scores = jnp.where(keymask[:, None, None, :], scores, masked_score)
                attn_probs = jax.nn.softmax(scores, axis=-1)
                mixed_heads = jnp.einsum('ehqk,ekhd->eqhd', low(attn_probs), split_heads[:, :, 2], precision=highest)
                mixed_heads = low_back(low(mixed_heads)).reshape(block_rows, D)
                stream = stream + low_back(dense_dot(mixed_heads, low_out[layer_index]))
                normed = low(layer_norm(stream, gains[2 * layer_index + 1], biases[2 * layer_index + 1]))
                hidden_pre = low_back(dense_dot(normed, low_up[layer_index]))
                activated = low(jax.nn.gelu(hidden_pre, approximate=False))
                stream = stream + low_back(dense_dot(activated, low_down[layer_index]))
            final_normed = layer_norm(stream, gains[2 * LAYERS], biases[2 * LAYERS]).reshape(block_size, PIECES, D)
            slot_mask = keymask.astype(jnp.float32)
            pooled = lax.optimization_barrier(jnp.sum(final_normed * slot_mask[:, :, None], axis=1)) / counts_block.astype(jnp.float32)[:, None]
            return dense_dot(low(pooled), low_proj)
        checked = jax.checkpoint(block_fn)
        packed_inputs = (inputs.reshape(blocks_total, block_size, PIECES, D), script_tags.reshape(blocks_total, block_size), counts.reshape(blocks_total, block_size))
        results = lax.map(lambda packed: checked(packed[0], packed[1], packed[2]), packed_inputs)
        return results.reshape(entries, OUT)
    embeddings, pullback = jax.vjp(forward, pieces.astype(jnp.float32), qkv_weight, out_weight, up_weight, down_weight, proj_weight, norm_gain, norm_bias, group_table)
    gradients = pullback(cotangent.astype(jnp.float32))
    input_grad = gradients[0]
    weight_grads = gradients[1:]
    square_total = jnp.float32(0.0)
    for gradient in weight_grads:
        square_total = square_total + jnp.sum(gradient * gradient)
    grad_norm = jnp.sqrt(square_total)
    clip_scale = jnp.minimum(1.0, clip_level / (grad_norm + 1e-06))
    new_qkv = adam_update(qkv_weight, qkv_first, qkv_second, weight_grads[0], clip_scale, decay_rate, learn_rate)
    new_out = adam_update(out_weight, out_first, out_second, weight_grads[1], clip_scale, decay_rate, learn_rate)
    new_up = adam_update(up_weight, up_first, up_second, weight_grads[2], clip_scale, decay_rate, learn_rate)
    new_down = adam_update(down_weight, down_first, down_second, weight_grads[3], clip_scale, decay_rate, learn_rate)
    new_proj = adam_update(proj_weight, proj_first, proj_second, weight_grads[4], clip_scale, decay_rate, learn_rate)
    new_gain = adam_update(norm_gain, gain_first, gain_second, weight_grads[5], clip_scale, 0.0, small_rate)
    new_bias = adam_update(norm_bias, bias_first, bias_second, weight_grads[6], clip_scale, 0.0, small_rate)
    new_table = adam_update(group_table, table_first, table_second, weight_grads[7], clip_scale, 0.0, small_rate)
    return (embeddings, input_grad, grad_norm, new_qkv[0], new_qkv[1], new_qkv[2], new_out[0], new_out[1], new_out[2], new_up[0], new_up[1], new_up[2], new_down[0], new_down[1], new_down[2], new_proj[0], new_proj[1], new_proj[2], new_gain[0], new_gain[1], new_gain[2], new_bias[0], new_bias[1], new_bias[2], new_table[0], new_table[1], new_table[2])
```

```python
import functools
import math

import jax
import jax.numpy as jnp
from jax import lax
from jax.experimental import pallas as pl
from jax.experimental.pallas import tpu as pltpu
from jax.sharding import PartitionSpec as P

HD = 64
PIECES = 7
SLOTS = 8
STEP = 10
BLOCKS = 4
SMALL_ROWS = 32

norm_eps = 1e-05
beta_first = 0.9
beta_second = 0.999
adam_eps = 1e-08
learn_rate = 0.03
small_rate = 0.5
decay_rate = 0.01
clip_level = 1.0
masked_score = -1000000000.0
bfloat = jnp.bfloat16
single = jnp.float32
highest = lax.Precision.HIGHEST
MESH = pl.DeviceIdType.MESH
VMEM = pltpu.VMEM


def place():
    along, across = lax.axis_index("dp"), lax.axis_index("mp")
    return lax.div(along, 2), lax.rem(along, 2), lax.div(across, 2), lax.rem(across, 2)


def device(z, y, x, c):
    return (z * 2 + y, x * 2 + c)


def remote(src, dst, send_sem, recv_sem, target):
    return pltpu.make_async_remote_copy(
        src_ref=src, dst_ref=dst, send_sem=send_sem, recv_sem=recv_sem, device_id=target, device_id_type=MESH
    )


def await_arrival(dst, send_sem, recv_sem, target):
    remote(dst, dst, send_sem, recv_sem, target).wait_recv()


def greet(z_count):
    z, y, x, c = place()
    barrier = pltpu.get_barrier_semaphore()

    def signal(target):
        pl.semaphore_signal(barrier, inc=1, device_id=target, device_id_type=MESH)

    signal(device(z, 1 - y, x, c))
    signal(device(z, y, 1 - x, c))
    signal(device(z, y, x, 1 - c))

    @pl.when(z > 0)
    def _():
        signal(device(z - 1, y, x, c))

    @pl.when(z < z_count - 1)
    def _():
        signal(device(z + 1, y, x, c))

    pl.semaphore_wait(barrier, 3 + jnp.minimum(z, 1) + jnp.minimum(z_count - 1 - z, 1))


def loop(low, high, body):
    if high - low <= 8:
        for step in range(low, high):
            body(step)
    else:

        def wrapped(step, carry):
            body(step)
            return carry

        lax.fori_loop(low, high, wrapped, 0)


def shared_gather(index):
    return index % 3 == 1


def gather_kernel(dims, w_ref, out_ref, local_sem, right_sem, left_sem, y_sem, x_sem, c_sem, recv_sem, c_recv):
    mats, z_count = dims
    z, y, x, c = place()
    greet(z_count)
    home = pltpu.make_async_copy(
        w_ref.at[:, pl.ds(2 * c, 2)], out_ref.at[:, pl.ds(2 * c, 2), z, y], local_sem
    )
    home.start()

    def span(index):
        if shared_gather(index):
            return pl.ds(2 * c, 2)
        return pl.ds(2 * c + x, 1)

    def spot(index, zz, yy):
        return out_ref.at[index, span(index), zz, yy]

    def to_right(index, zz, src):
        return remote(src, spot(index, zz, y), right_sem.at[index, zz], recv_sem.at[index, 0, zz, y], device(z + 1, y, x, c))

    def to_left(index, zz, src):
        return remote(src, spot(index, zz, y), left_sem.at[index, zz], recv_sem.at[index, 0, zz, y], device(z - 1, y, x, c))

    def to_y(index, zz, src):
        return remote(src, spot(index, zz, y), y_sem.at[index, zz], recv_sem.at[index, 0, zz, y], device(z, 1 - y, x, c))

    def to_x(index, zz, yy):
        return remote(
            spot(index, zz, yy), spot(index, zz, yy), x_sem.at[index, zz, yy], recv_sem.at[index, 1, zz, yy], device(z, y, 1 - x, c)
        )

    def to_c(index):
        pair = out_ref.at[index, pl.ds(2 * c, 2)]
        return remote(pair, pair, c_sem.at[index], c_recv.at[index], device(z, y, x, 1 - c))

    def arrived(index, zz, yy):
        await_arrival(spot(index, zz, yy), y_sem.at[index, zz], recv_sem.at[index, 0, zz, yy], device(z, 1 - y, x, c))

    def own(index):
        src = w_ref.at[index, span(index)]

        @pl.when(z < z_count - 1)
        def _():
            to_right(index, z, src).start()

        @pl.when(z > 0)
        def _():
            to_left(index, z, src).start()

        to_y(index, z, src).start()

    def line(index):
        def hop(away):
            @pl.when(z - away >= 0)
            def _():
                zz = z - away
                arrived(index, zz, y)

                @pl.when(z < z_count - 1)
                def _():
                    to_right(index, zz, spot(index, zz, y)).start()

                to_y(index, zz, spot(index, zz, y)).start()
                if not shared_gather(index):
                    to_x(index, zz, y).start()

            @pl.when(z + away < z_count)
            def _():
                zz = z + away
                arrived(index, zz, y)

                @pl.when(z > 0)
                def _():
                    to_left(index, zz, spot(index, zz, y)).start()

                to_y(index, zz, spot(index, zz, y)).start()
                if not shared_gather(index):
                    to_x(index, zz, y).start()

        loop(1, z_count, hop)

    def beside(index):
        def one(zz):
            arrived(index, zz, 1 - y)
            if not shared_gather(index):
                to_x(index, zz, 1 - y).start()

        one(z)

        def hop(away):
            @pl.when(z - away >= 0)
            def _():
                one(z - away)

            @pl.when(z + away < z_count)
            def _():
                one(z + away)

        loop(1, z_count, hop)

    def opposite(index):
        if not shared_gather(index):

            def one(zz, yy):
                block = out_ref.at[index, pl.ds(2 * c + 1 - x, 1), zz, yy]
                await_arrival(block, x_sem.at[index, zz, yy], recv_sem.at[index, 1, zz, yy], device(z, y, 1 - x, c))

            def each(zz):
                @pl.when(zz != z)
                def _():
                    one(zz, y)

                one(zz, 1 - y)

            loop(0, z_count, each)
        to_c(index).start()

    def finish(index):
        pair = out_ref.at[index, pl.ds(2 * (1 - c), 2)]
        await_arrival(pair, c_sem.at[index], c_recv.at[index], device(z, y, x, 1 - c))

    for tick in range(mats + 3):
        if tick == 0:
            own(0)
            own(1)
        elif tick + 1 < mats:
            own(tick + 1)
        if tick < mats:
            line(tick)
        if tick == 0:
            home.wait()
        if 1 <= tick <= mats:
            beside(tick - 1)
        if 2 <= tick <= mats + 1:
            opposite(tick - 2)
        if 3 <= tick:
            finish(tick - 3)

    for index in range(mats):

        def each(zz):
            @pl.when(jnp.logical_and(zz <= z, z < z_count - 1))
            def _():
                to_right(index, zz, spot(index, zz, y)).wait_send()

            @pl.when(jnp.logical_and(zz >= z, z > 0))
            def _():
                to_left(index, zz, spot(index, zz, y)).wait_send()

            to_y(index, zz, spot(index, zz, y)).wait_send()
            if not shared_gather(index):

                @pl.when(zz != z)
                def _():
                    to_x(index, zz, y).wait_send()

                to_x(index, zz, 1 - y).wait_send()

        loop(0, z_count, each)
        to_c(index).wait_send()


def gather_weights(packed, dp):
    mats, blocks, rows, width = packed.shape
    z_count = dp // 2
    dma = pltpu.SemaphoreType.DMA
    return pl.pallas_call(
        functools.partial(gather_kernel, (mats, z_count)),
        out_shape=jax.ShapeDtypeStruct((mats, blocks, z_count, 2, rows, width), bfloat),
        in_specs=[pl.BlockSpec(memory_space=pl.ANY)],
        out_specs=pl.BlockSpec(memory_space=pl.ANY),
        scratch_shapes=[
            dma,
            dma((mats, z_count)),
            dma((mats, z_count)),
            dma((mats, z_count)),
            dma((mats, z_count, 2)),
            dma((mats,)),
            dma((mats, 2, z_count, 2)),
            dma((mats,)),
        ],
        compiler_params=pltpu.CompilerParams(collective_id=1, has_side_effects=True),
        name="gather_weights",
    )(packed)


def dot_nn(left_side, right_side):
    return lax.dot_general(left_side, right_side, (((1,), (0,)), ((), ())), preferred_element_type=single)


def dot_nt(left_side, right_side):
    return lax.dot_general(left_side, right_side, (((1,), (1,)), ((), ())), preferred_element_type=single)


def dot_tn(left_side, right_side):
    return lax.dot_general(left_side, right_side, (((0,), (0,)), ((), ())), preferred_element_type=single)


def normalize(values):
    centre = jnp.mean(values, axis=-1, keepdims=True)
    offset = values - centre
    spread = jnp.mean(offset * offset, axis=-1, keepdims=True)
    scale = lax.rsqrt(spread + norm_eps)
    return offset * scale, scale


def normalize_back(grad, unit, scale, gain_row):
    grad_unit = grad * gain_row
    first = jnp.mean(grad_unit, axis=-1, keepdims=True)
    second = jnp.mean(grad_unit * unit, axis=-1, keepdims=True)
    return scale * (grad_unit - first - unit * second)


def compute_kernel(
    layers, pieces_ref, meta_ref, cot_ref, w_ref, gain_ref, bias_ref, table_ref,
    emb_ref, dx_ref, grad_ref, small_ref,
    x_ref, unit_ref, scale_ref, a_ref, b_ref, qkv_ref, prob_ref, o_ref, g_ref, slope_ref, dqkv_ref, do_ref, acc_ref, turn_ref,
):
    entries, _, width = pieces_ref.shape
    rows = entries * SLOTS
    half = rows // 2
    groups = table_ref.shape[0]
    pairs = width // 128
    final = 2 * layers
    proj = 3 * layers

    tags_row = meta_ref[0:1, :]
    counts_row = meta_ref[1:2, :]
    columns = meta_ref[...].T
    tags_col = columns[:, 0:1]
    counts_col = columns[:, 1:2]

    group_col = lax.broadcasted_iota(jnp.int32, (rows, groups), 1).astype(single)
    onehot = (group_col == tags_col).astype(single)
    x_ref[0] = lax.dot_general(
        onehot, table_ref[...], (((1,), (0,)), ((), ())), precision=highest, preferred_element_type=single
    )
    for entry in range(entries):
        at = entry * SLOTS
        x_ref[0, at : at + PIECES, :] = x_ref[0, at : at + PIECES, :] + pieces_ref[entry].astype(single)

    row_at = lax.broadcasted_iota(jnp.int32, (half, 2 * half), 0)
    key_at = lax.rem(lax.broadcasted_iota(jnp.int32, (half, 2 * half), 1), half)
    same = lax.div(row_at, SLOTS) == lax.div(key_at, SLOTS)
    key_slot = lax.rem(key_at, SLOTS).astype(single)
    low_lane = lax.broadcasted_iota(jnp.int32, (half, 128), 1) < HD

    def key_mask(part):
        piece = counts_row[:, part * half : (part + 1) * half]
        counts_here = jnp.concatenate([piece, piece], axis=1)
        return jnp.logical_and(same, key_slot < counts_here)

    def split_pair(values):
        zero = jnp.zeros_like(values)
        return jnp.concatenate([jnp.where(low_lane, values, zero), jnp.where(low_lane, zero, values)], axis=0)

    def forward(layer, carry):
        values = x_ref[layer]
        unit, scale = normalize(values)
        unit_ref[2 * layer] = unit
        scale_ref[2 * layer] = scale
        a = (unit * gain_ref[2 * layer] + bias_ref[2 * layer]).astype(bfloat)
        a_ref[layer] = a
        for part in range(3):
            qkv_ref[layer, part] = dot_nn(a, w_ref[3 * layer, part]).astype(bfloat)
        for part in range(2):
            mask = key_mask(part)
            here = slice(part * half, (part + 1) * half)
            for pair in range(pairs):
                lanes = slice(pair * 128, (pair + 1) * 128)
                q = qkv_ref[layer, 0, here, lanes]
                keys = split_pair(qkv_ref[layer, 1, here, lanes])
                vals = split_pair(qkv_ref[layer, 2, here, lanes])
                scores = dot_nt(q, keys) * HD ** (-0.5)
                scores = jnp.where(mask, scores, masked_score)
                probs = []
                for head in range(2):
                    mine = scores[:, head * half : (head + 1) * half]
                    top = jnp.max(mine, axis=-1, keepdims=True)
                    raised = jnp.exp(mine - top)
                    probs.append(raised / jnp.sum(raised, axis=-1, keepdims=True))
                prob = jnp.concatenate(probs, axis=1)
                prob_ref[layer, part * pairs + pair] = prob
                o_ref[layer, here, lanes] = dot_nn(prob.astype(bfloat), vals).astype(bfloat)
        middle = values + dot_nt(o_ref[layer], w_ref[3 * layer, 3])
        unit, scale = normalize(middle)
        unit_ref[2 * layer + 1] = unit
        scale_ref[2 * layer + 1] = scale
        b_ref[layer] = (unit * gain_ref[2 * layer + 1] + bias_ref[2 * layer + 1]).astype(bfloat)
        acc_ref[...] = middle

        def hidden(block, carry):
            u = dot_nn(b_ref[layer], w_ref[3 * layer + 1, block])
            gate = 0.5 * (1.0 + lax.erf(u * math.sqrt(0.5)))
            g = (u * gate).astype(bfloat)
            g_ref[layer, block] = g
            slope_ref[layer, block] = gate + u * (jnp.exp(-0.5 * u * u) * (1.0 / math.sqrt(2.0 * math.pi)))
            acc_ref[...] += dot_nt(g, w_ref[3 * layer + 2, block])
            return carry

        lax.fori_loop(0, BLOCKS, hidden, 0)
        x_ref[layer + 1] = acc_ref[...]
        return carry

    lax.fori_loop(0, layers, forward, 0)

    unit, scale = normalize(x_ref[layers])
    normed = unit * gain_ref[final] + bias_ref[final]
    slot_col = lax.rem(lax.broadcasted_iota(jnp.int32, (rows, 1), 0), SLOTS).astype(single)
    used_col = (slot_col < counts_col).astype(single)
    pooled = jnp.sum((normed * used_col).reshape(entries, SLOTS, width), axis=1)
    counts_entry = counts_col.reshape(entries, SLOTS, 1)[:, 0, :]
    pooled_low = (pooled / counts_entry).astype(bfloat)
    grad_pooled = jnp.zeros((entries, width), single)
    for block in range(BLOCKS):
        lanes = slice(block * width, (block + 1) * width)
        emb_ref[:, lanes] = dot_nn(pooled_low, w_ref[proj, block])
        grad_ref[proj, block] = dot_tn(pooled_low, cot_ref[:, lanes]).astype(bfloat)
        grad_pooled += dot_nt(cot_ref[:, lanes], w_ref[proj, block])
    grad_pooled = grad_pooled / counts_entry
    grad_normed = jnp.broadcast_to(grad_pooled[:, None, :], (entries, SLOTS, width)).reshape(rows, width) * used_col
    small_ref[...] = jnp.zeros_like(small_ref)
    small_ref[pl.ds(final, 1), :] = jnp.sum(grad_normed * unit, axis=0, keepdims=True)
    small_ref[pl.ds(SLOTS + final, 1), :] = jnp.sum(grad_normed, axis=0, keepdims=True)
    acc_ref[...] = normalize_back(grad_normed, unit, scale, gain_ref[final])

    def backward(step, carry):
        layer = layers - 1 - step
        grad_next = acc_ref[...]
        a_ref_here = a_ref[layer]
        dz = grad_next.astype(bfloat)
        do_ref[...] = dz
        turn_ref[0] = grad_next.T.astype(bfloat)
        turn_ref[1] = b_ref[layer].astype(single).T.astype(bfloat)
        acc_ref[...] = jnp.zeros_like(acc_ref)

        def hidden(block, carry):
            grad_ref[3 * layer + 2, block] = dot_nn(turn_ref[0], g_ref[layer, block]).astype(bfloat)
            grad_act = dot_nn(do_ref[...], w_ref[3 * layer + 2, block])
            du = (grad_act * slope_ref[layer, block]).astype(bfloat)
            grad_ref[3 * layer + 1, block] = dot_nn(turn_ref[1], du).astype(bfloat)
            acc_ref[...] += dot_nt(du, w_ref[3 * layer + 1, block])
            return carry

        lax.fori_loop(0, BLOCKS, hidden, 0)
        grad_b = acc_ref[...]
        unit = unit_ref[2 * layer + 1]
        small_ref[pl.ds(2 * layer + 1, 1), :] = jnp.sum(grad_b * unit, axis=0, keepdims=True)
        small_ref[pl.ds(SLOTS + 2 * layer + 1, 1), :] = jnp.sum(grad_b, axis=0, keepdims=True)
        grad_middle = grad_next + normalize_back(grad_b, unit, scale_ref[2 * layer + 1], gain_ref[2 * layer + 1])
        acc_ref[...] = grad_middle
        dy = grad_middle.astype(bfloat)
        grad_ref[3 * layer, 3] = dot_nn(grad_middle.T.astype(bfloat), o_ref[layer]).astype(bfloat)
        do_ref[...] = dot_nn(dy, w_ref[3 * layer, 3]).astype(bfloat)
        for part in range(2):
            here = slice(part * half, (part + 1) * half)
            for pair in range(pairs):
                lanes = slice(pair * 128, (pair + 1) * 128)
                q = qkv_ref[layer, 0, here, lanes]
                keys = split_pair(qkv_ref[layer, 1, here, lanes])
                vals = split_pair(qkv_ref[layer, 2, here, lanes])
                do = do_ref[here, lanes]
                prob = prob_ref[layer, part * pairs + pair]
                grad_prob = dot_nt(do, vals)
                product = grad_prob * prob
                scored = []
                for head in range(2):
                    spans = slice(head * half, (head + 1) * half)
                    total = jnp.sum(product[:, spans], axis=-1, keepdims=True)
                    scored.append(product[:, spans] - prob[:, spans] * total)
                ds = jnp.concatenate(scored, axis=1)
                ds_low = ds.astype(bfloat)
                dv = dot_tn(prob.astype(bfloat), do)
                dk = dot_tn(ds_low, q)
                dq = dot_nn(ds_low, keys)
                dqkv_ref[0, here, lanes] = (dq * HD ** (-0.5)).astype(bfloat)
                dqkv_ref[1, here, lanes] = (jnp.where(low_lane, dk[:half], dk[half:]) * HD ** (-0.5)).astype(bfloat)
                dqkv_ref[2, here, lanes] = jnp.where(low_lane, dv[:half], dv[half:]).astype(bfloat)
        turned = a_ref_here.astype(single).T.astype(bfloat)
        grad_a = jnp.zeros((rows, width), single)
        for part in range(3):
            grad_ref[3 * layer, part] = dot_nn(turned, dqkv_ref[part]).astype(bfloat)
            grad_a += dot_nt(dqkv_ref[part], w_ref[3 * layer, part])
        unit = unit_ref[2 * layer]
        small_ref[pl.ds(2 * layer, 1), :] = jnp.sum(grad_a * unit, axis=0, keepdims=True)
        small_ref[pl.ds(SLOTS + 2 * layer, 1), :] = jnp.sum(grad_a, axis=0, keepdims=True)
        acc_ref[...] += normalize_back(grad_a, unit, scale_ref[2 * layer], gain_ref[2 * layer])
        return carry

    lax.fori_loop(0, layers, backward, 0)
    for entry in range(entries):
        at = entry * SLOTS
        dx_ref[entry] = acc_ref[at : at + PIECES, :]
    group_row = lax.broadcasted_iota(jnp.int32, (groups, rows), 0).astype(single)
    spread = (group_row == tags_row).astype(single)
    small_ref[2 * SLOTS : 2 * SLOTS + groups, :] = lax.dot_general(
        spread, acc_ref[...], (((1,), (0,)), ((), ())), precision=highest, preferred_element_type=single
    )


def compute(pieces, meta, cotangent, weights, gain, bias, table, layers):
    entries, _, width = pieces.shape
    rows = entries * SLOTS
    pairs = width // 128
    vmem = pl.BlockSpec(memory_space=VMEM)
    return pl.pallas_call(
        functools.partial(compute_kernel, layers),
        out_shape=(
            jax.ShapeDtypeStruct(cotangent.shape, single),
            jax.ShapeDtypeStruct(pieces.shape, single),
            jax.ShapeDtypeStruct(weights.shape, bfloat),
            jax.ShapeDtypeStruct((SMALL_ROWS, width), single),
        ),
        in_specs=[vmem] * 7,
        out_specs=(vmem, vmem, vmem, vmem),
        scratch_shapes=[
            VMEM((layers + 1, rows, width), single),
            VMEM((2 * layers, rows, width), single),
            VMEM((2 * layers, rows, 1), single),
            VMEM((layers, rows, width), bfloat),
            VMEM((layers, rows, width), bfloat),
            VMEM((layers, 3, rows, width), bfloat),
            VMEM((layers, 2 * pairs, rows // 2, rows), single),
            VMEM((layers, rows, width), bfloat),
            VMEM((layers, BLOCKS, rows, width), bfloat),
            VMEM((layers, BLOCKS, rows, width), single),
            VMEM((3, rows, width), bfloat),
            VMEM((rows, width), bfloat),
            VMEM((rows, width), single),
            VMEM((2, width, rows), bfloat),
        ],
        compiler_params=pltpu.CompilerParams(vmem_limit_bytes=60 * 2**20),
        name="forward_backward",
    )(pieces, meta, cotangent, weights, gain, bias, table)


def shared_reduce(index):
    return lax.rem(index, 2) == 1


def reduce_kernel(
    dims, grad_ref, small_ref,
    out_ref, total_ref, norm_ref,
    acc, c_buf, x_buf, y_buf, l_buf, r_buf, f_buf, part_ref, s_x, s_y, s_c, s_z, s_cur, n_buf,
    load_sem, c_ss, c_rs, x_ss, x_rs, y_ss, y_rs, z_ss, l_rs, r_rs, fx_ss, fx_rs, fc_ss, fc_rs, s_ss, s_rs, n_ss, n_rs,
):
    mats, z_count = dims
    z, y, x, c = place()
    units = mats * z_count
    rows = out_ref.shape[2]
    dp = 2 * z_count
    me = z * 2 + y

    barrier = pltpu.get_barrier_semaphore()

    def signal(target):
        pl.semaphore_signal(barrier, inc=1, device_id=target, device_id_type=MESH)

    def greet_dp(step, carry):
        other = lax.rem(me + step, dp)
        pl.semaphore_signal(barrier, inc=1, device_id=(other, x * 2 + c), device_id_type=MESH)
        return carry

    lax.fori_loop(1, dp, greet_dp, 0)
    signal(device(z, y, 1 - x, c))
    signal(device(z, y, x, 1 - c))
    pl.semaphore_wait(barrier, dp + 1)

    right, left = device(z + 1, y, x, c), device(z - 1, y, x, c)
    y_side, x_side, c_side = device(z, 1 - y, x, c), device(z, y, 1 - x, c), device(z, y, x, 1 - c)

    load = pltpu.make_async_copy(grad_ref.at[:, pl.ds(2 * c, 2)], acc, load_sem)
    load.start()

    def order(unit):
        index = mats - 1 - lax.div(unit, z_count)
        turn = lax.rem(unit, z_count)
        target = jnp.where(lax.rem(turn, 2) == 0, lax.div(turn, 2), z_count - 1 - lax.div(turn, 2))
        return index, target

    def to_c(unit):
        index, target = order(unit)
        return remote(
            grad_ref.at[index, pl.ds(2 * (1 - c), 2), target], c_buf.at[index, :, target], c_ss.at[index, target], c_rs.at[index, target], c_side
        )

    def to_x(index, target):
        return remote(acc.at[index, 1 - x, target], x_buf.at[index, target], x_ss.at[index, target], x_rs.at[index, target], x_side)

    def both(shared, make):
        @pl.when(shared)
        def _():
            make(pl.ds(0, 2))

        @pl.when(jnp.logical_not(shared))
        def _():
            make(pl.ds(x, 1))

    def to_y(index, target, span):
        return remote(
            acc.at[index, span, target, 1 - y], y_buf.at[index, span, target], y_ss.at[index, target], y_rs.at[index, target], y_side
        )

    def to_z(index, target, span, buf, sems, side):
        return remote(acc.at[index, span, target, y], buf.at[index, span, target], z_ss.at[index, target], sems.at[index, target], side)

    def add(ref, at, extra):
        ref[at] = (ref[at].astype(single) + extra.astype(single)).astype(bfloat)

    def stage_c(unit):
        index, target = order(unit)
        to_c(unit).wait_recv()
        for block in range(2):
            add(acc, (index, block, target), c_buf[index, block, target])
        shared = shared_reduce(index)

        @pl.when(shared)
        def _():
            to_y(index, target, pl.ds(0, 2)).start()

        @pl.when(jnp.logical_not(shared))
        def _():
            to_x(index, target).start()

    def stage_x(unit):
        index, target = order(unit)

        @pl.when(jnp.logical_not(shared_reduce(index)))
        def _():
            to_x(index, target).wait_recv()
            add(acc, (index, x, target), x_buf[index, target])
            to_y(index, target, pl.ds(x, 1)).start()

    def stage_y(unit):
        index, target = order(unit)

        def make(span):
            to_y(index, target, span).wait_recv()
            add(acc, (index, span, target, y), y_buf[index, span, target])

            @pl.when(jnp.logical_and(z == 0, target != 0))
            def _():
                to_z(index, target, span, l_buf, l_rs, right).start()

            @pl.when(jnp.logical_and(z == z_count - 1, target != z_count - 1))
            def _():
                to_z(index, target, span, r_buf, r_rs, left).start()

        both(shared_reduce(index), make)

    def stage_z(unit):
        index, target = order(unit)

        def make(span):
            at = (index, span, target, y)
            from_left = jnp.logical_and(z > 0, target >= z)
            from_right = jnp.logical_and(z < z_count - 1, target <= z)

            @pl.when(from_left)
            def _():
                to_z(index, target, span, l_buf, l_rs, right).wait_recv()

            @pl.when(from_right)
            def _():
                to_z(index, target, span, r_buf, r_rs, left).wait_recv()

            @pl.when(jnp.logical_and(from_left, target > z))
            def _():
                add(acc, at, l_buf[index, span, target])
                to_z(index, target, span, l_buf, l_rs, right).start()

            @pl.when(jnp.logical_and(from_right, target < z))
            def _():
                add(acc, at, r_buf[index, span, target])
                to_z(index, target, span, r_buf, r_rs, left).start()

            @pl.when(target == z)
            def _():
                part_ref[...] = acc[index, :, target, y].astype(single)

                @pl.when(from_left)
                def _():
                    part_ref[span] = part_ref[span] + l_buf[index, span, target].astype(single)

                @pl.when(from_right)
                def _():
                    part_ref[span] = part_ref[span] + r_buf[index, span, target].astype(single)

        both(shared_reduce(index), make)

        @pl.when(target == z)
        def _():
            @pl.when(shared_reduce(index))
            def _():
                f_buf[index, 0] = part_ref[...].astype(bfloat)

            @pl.when(jnp.logical_not(shared_reduce(index)))
            def _():
                out_ref[index, pl.ds(2 * c + x, 1)] = part_ref[pl.ds(x, 1)].astype(bfloat)

            start_final(index)

    def final_shared(index):
        return remote(f_buf.at[index, 0], f_buf.at[index, 1], fx_ss.at[index], fx_rs.at[index], x_side)

    def final_split(index):
        mine = out_ref.at[index, 2 * c + x]
        return remote(mine, mine, fx_ss.at[index], fx_rs.at[index], x_side)

    def final_c(index):
        pair = out_ref.at[index, pl.ds(2 * c, 2)]
        return remote(pair, pair, fc_ss.at[index], fc_rs.at[index], c_side)

    def on_type(index, shared_do, split_do):
        @pl.when(shared_reduce(index))
        def _():
            shared_do()

        @pl.when(jnp.logical_not(shared_reduce(index)))
        def _():
            split_do()

    def start_final(index):
        on_type(index, lambda: final_shared(index).start(), lambda: final_split(index).start())

    def stage_f(unit):
        index, target = order(unit)

        @pl.when(target == z)
        def _():
            @pl.when(shared_reduce(index))
            def _():
                final_shared(index).wait_recv()
                total = f_buf[index, 0].astype(single) + f_buf[index, 1].astype(single)
                out_ref[index, pl.ds(2 * c, 2)] = total.astype(bfloat)

            @pl.when(jnp.logical_not(shared_reduce(index)))
            def _():
                final_split(index).wait_recv()

            final_c(index).start()

    def small_step(stage):
        if stage == 0:
            remote(small_ref, s_c, s_ss.at[0], s_rs.at[0], c_side).start()
        elif stage == 1:
            remote(small_ref, s_c, s_ss.at[0], s_rs.at[0], c_side).wait_recv()
            s_cur[0] = small_ref[...] + s_c[...]
            remote(s_cur.at[0], s_x, s_ss.at[1], s_rs.at[1], x_side).start()
        elif stage == 2:
            remote(s_cur.at[0], s_x, s_ss.at[1], s_rs.at[1], x_side).wait_recv()
            s_cur[1] = s_cur[0] + s_x[...]
            remote(s_cur.at[1], s_y, s_ss.at[2], s_rs.at[2], y_side).start()
        elif stage == 3:
            remote(s_cur.at[1], s_y, s_ss.at[2], s_rs.at[2], y_side).wait_recv()
            s_z[z] = s_cur[1] + s_y[...]

            def send(step, carry):
                other = lax.rem(z + step, z_count)
                remote(s_z.at[z], s_z.at[z], s_ss.at[3 + other], s_rs.at[3 + z], device(other, y, x, c)).start()
                return carry

            lax.fori_loop(1, z_count, send, 0)
        else:

            def wait(step, carry):
                other = lax.rem(z + step, z_count)
                remote(s_z.at[other], s_z.at[other], s_ss.at[3 + other], s_rs.at[3 + other], device(other, y, x, c)).wait_recv()
                return carry

            lax.fori_loop(1, z_count, wait, 0)

            def gather(step, carry):
                return carry + s_z[step]

            total_ref[...] = lax.fori_loop(0, z_count, gather, jnp.zeros(total_ref.shape, single))

    small_step(0)

    def start_c(unit, carry):
        to_c(unit).start()
        return carry

    lax.fori_loop(0, units, start_c, 0)
    load.wait()
    small_step(1)

    lags = (0, 2, 4, 6, 8)
    stages = (stage_c, stage_x, stage_y, stage_z, stage_f)

    def tick(step, carry):
        for lag, stage in zip(lags, stages):
            unit = step - lag

            @pl.when(jnp.logical_and(unit >= 0, unit < units))
            def _():
                stage(unit)

        return carry

    lax.fori_loop(0, units, tick, 0)
    small_step(2)
    lax.fori_loop(units, units + lags[2], tick, 0)
    small_step(3)
    lax.fori_loop(units + lags[2], units + lags[-1], tick, 0)
    small_step(4)

    def arrive(index, carry):
        pair = out_ref.at[index, pl.ds(2 * (1 - c), 2)]
        remote(pair, pair, fc_ss.at[index], fc_rs.at[index], c_side).wait_recv()
        return carry

    lax.fori_loop(0, mats, arrive, 0)

    def squares(index, carry):
        values = out_ref[index].astype(single)
        return carry + jnp.sum(jnp.sum(values * values, axis=0), axis=0, keepdims=True)

    squared = lax.fori_loop(0, mats, squares, jnp.zeros((1, out_ref.shape[3]), single))
    n_buf[me] = jnp.broadcast_to(squared, n_buf.shape[1:])

    def send_norm(step, carry):
        other = lax.rem(me + step, dp)
        remote(n_buf.at[me], n_buf.at[me], n_ss.at[other], n_rs.at[me], (other, x * 2 + c)).start()
        return carry

    lax.fori_loop(1, dp, send_norm, 0)

    def wait_norm(step, carry):
        other = lax.rem(me + step, dp)
        remote(n_buf.at[other], n_buf.at[other], n_ss.at[other], n_rs.at[other], (other, x * 2 + c)).wait_recv()
        return carry

    lax.fori_loop(1, dp, wait_norm, 0)

    def sum_norm(step, carry):
        return carry + n_buf[step]

    spread = lax.fori_loop(0, dp, sum_norm, jnp.zeros(n_buf.shape[1:], single))
    smalls = total_ref[...]
    norm_ref[...] = jnp.broadcast_to(
        jnp.sum(spread[0:1], axis=1, keepdims=True) + jnp.sum(jnp.sum(smalls * smalls, axis=0, keepdims=True), axis=1, keepdims=True),
        norm_ref.shape,
    )

    def done_unit(unit, carry):
        index, target = order(unit)
        to_c(unit).wait_send()

        @pl.when(jnp.logical_not(shared_reduce(index)))
        def _():
            to_x(index, target).wait_send()

        def make(span):
            to_y(index, target, span).wait_send()

            @pl.when(target != z)
            def _():
                to_z(index, target, span, l_buf, l_rs, y_side).wait_send()

        both(shared_reduce(index), make)
        return carry

    lax.fori_loop(0, units, done_unit, 0)

    def done_mat(index, carry):
        on_type(index, lambda: final_shared(index).wait_send(), lambda: final_split(index).wait_send())
        final_c(index).wait_send()
        return carry

    lax.fori_loop(0, mats, done_mat, 0)
    remote(small_ref, s_c, s_ss.at[0], s_rs.at[0], c_side).wait_send()
    remote(s_cur.at[0], s_x, s_ss.at[1], s_rs.at[1], x_side).wait_send()
    remote(s_cur.at[1], s_y, s_ss.at[2], s_rs.at[2], y_side).wait_send()

    def done_z(step, carry):
        other = lax.rem(z + step, z_count)
        remote(s_z.at[z], s_z.at[z], s_ss.at[3 + other], s_rs.at[3 + z], device(other, y, x, c)).wait_send()
        return carry

    lax.fori_loop(1, z_count, done_z, 0)

    def done_norm(step, carry):
        other = lax.rem(me + step, dp)
        remote(n_buf.at[me], n_buf.at[me], n_ss.at[other], n_rs.at[me], (other, x * 2 + c)).wait_send()
        return carry

    lax.fori_loop(1, dp, done_norm, 0)


def reduce_gradients(grads, small, dp):
    mats, blocks, z_count, _, rows, width = grads.shape
    dma = pltpu.SemaphoreType.DMA
    vmem = pl.BlockSpec(memory_space=VMEM)
    return pl.pallas_call(
        functools.partial(reduce_kernel, (mats, z_count)),
        out_shape=(
            jax.ShapeDtypeStruct((mats, blocks, rows, width), bfloat),
            jax.ShapeDtypeStruct(small.shape, single),
            jax.ShapeDtypeStruct((8, 128), single),
        ),
        in_specs=[pl.BlockSpec(memory_space=pl.ANY), vmem],
        out_specs=(vmem, vmem, vmem),
        scratch_shapes=[
            VMEM((mats, 2, z_count, 2, rows, width), bfloat),
            VMEM((mats, 2, z_count, 2, rows, width), bfloat),
            VMEM((mats, z_count, 2, rows, width), bfloat),
            VMEM((mats, 2, z_count, rows, width), bfloat),
            VMEM((mats, 2, z_count, rows, width), bfloat),
            VMEM((mats, 2, z_count, rows, width), bfloat),
            VMEM((mats, 2, 2, rows, width), bfloat),
            VMEM((2, rows, width), single),
            VMEM(small.shape, single),
            VMEM(small.shape, single),
            VMEM(small.shape, single),
            VMEM((z_count, *small.shape), single),
            VMEM((2, *small.shape), single),
            VMEM((dp, 8, width), single),
            dma,
            dma((mats, z_count)),
            dma((mats, z_count)),
            dma((mats, z_count)),
            dma((mats, z_count)),
            dma((mats, z_count)),
            dma((mats, z_count)),
            dma((mats, z_count)),
            dma((mats, z_count)),
            dma((mats, z_count)),
            dma((mats,)),
            dma((mats,)),
            dma((mats,)),
            dma((mats,)),
            dma((3 + z_count,)),
            dma((3 + z_count,)),
            dma((dp,)),
            dma((dp,)),
        ],
        compiler_params=pltpu.CompilerParams(collective_id=2, has_side_effects=True, vmem_limit_bytes=60 * 2**20),
        name="reduce_gradients",
    )(grads, small)


def adam_update(weight, first, second, gradient, clip_scale, decay, step_rate):
    clipped = gradient * clip_scale
    first_new = beta_first * first + (1.0 - beta_first) * clipped
    second_new = beta_second * second + (1.0 - beta_second) * clipped * clipped
    first_hat = first_new / (1.0 - beta_first**STEP)
    second_hat = second_new / (1.0 - beta_second**STEP)
    weight_new = weight - step_rate * (first_hat / (jnp.sqrt(second_hat) + adam_eps) + decay * weight)
    return (weight_new, first_new, second_new)


def pack(qkv, out, up, down, proj):
    layers, _, rows, width = qkv.shape
    parts = []
    front = jnp.concatenate([qkv, jnp.swapaxes(out, 1, 2)[:, None]], axis=1)
    rise = jnp.swapaxes(up.reshape(layers, rows, BLOCKS, width), 1, 2)
    fall = jnp.swapaxes(jnp.swapaxes(down, 1, 2).reshape(layers, rows, BLOCKS, width), 1, 2)
    body = jnp.stack([front, rise, fall], axis=1).reshape(3 * layers, BLOCKS, rows, width)
    last = jnp.swapaxes(proj.reshape(rows, BLOCKS, width), 0, 1)[None]
    return jnp.concatenate([body, last], axis=0)


def unpack(packed, layers):
    _, _, rows, width = packed.shape
    body = packed[: 3 * layers].reshape(layers, 3, BLOCKS, rows, width)
    qkv = body[:, 0, :3]
    out = jnp.swapaxes(body[:, 0, 3], 1, 2)
    up = jnp.swapaxes(body[:, 1], 1, 2).reshape(layers, rows, BLOCKS * width)
    down = jnp.swapaxes(jnp.swapaxes(body[:, 2], 1, 2).reshape(layers, rows, BLOCKS * width), 1, 2)
    proj = jnp.swapaxes(packed[3 * layers], 0, 1).reshape(rows, BLOCKS * width)
    return qkv, out, up, down, proj


def per_device(
    pieces, script_tags, counts, cotangent,
    qkv_weight, qkv_first, qkv_second,
    out_weight, out_first, out_second,
    up_weight, up_first, up_second,
    down_weight, down_first, down_second,
    proj_weight, proj_first, proj_second,
    norm_gain, gain_first, gain_second,
    norm_bias, bias_first, bias_second,
    group_table, table_first, table_second,
):
    layers = qkv_weight.shape[0]
    width = pieces.shape[2]
    dp = lax.axis_size("dp")
    norms = norm_gain.shape[0]
    groups = group_table.shape[0]
    packed = pack(
        qkv_weight.astype(bfloat), out_weight.astype(bfloat), up_weight.astype(bfloat), down_weight.astype(bfloat), proj_weight.astype(bfloat)
    )
    gathered = gather_weights(packed, dp)
    mats = gathered.shape[0]
    weights = gathered.reshape(mats, BLOCKS, width, width)
    meta = jnp.stack([jnp.repeat(script_tags, SLOTS), jnp.repeat(counts, SLOTS)]).astype(single)
    meta = jnp.concatenate([meta, jnp.zeros((SLOTS - 2, meta.shape[1]), single)], axis=0)
    embeddings, input_grad, grads, small = compute(
        pieces, meta, cotangent, weights,
        norm_gain.reshape(norms, 1, width), norm_bias.reshape(norms, 1, width), group_table, layers,
    )
    reduced, small_total, square_total = reduce_gradients(grads.reshape(gathered.shape), small, dp)
    grad_norm = jnp.sqrt(square_total[0, 0])
    clip_scale = jnp.minimum(1.0, clip_level / (grad_norm + 1e-06))
    grad_qkv, grad_out, grad_up, grad_down, grad_proj = unpack(reduced.astype(single), layers)
    grad_gain = small_total[:norms]
    grad_bias = small_total[SLOTS : SLOTS + norms]
    grad_table = small_total[2 * SLOTS : 2 * SLOTS + groups]
    big = functools.partial(adam_update, clip_scale=clip_scale, decay=decay_rate, step_rate=learn_rate)
    little = functools.partial(adam_update, clip_scale=clip_scale, decay=0.0, step_rate=small_rate)
    return (
        embeddings,
        input_grad,
        grad_norm,
        *big(qkv_weight, qkv_first, qkv_second, grad_qkv),
        *big(out_weight, out_first, out_second, grad_out),
        *big(up_weight, up_first, up_second, grad_up),
        *big(down_weight, down_first, down_second, grad_down),
        *big(proj_weight, proj_first, proj_second, grad_proj),
        *little(norm_gain, gain_first, gain_second, grad_gain),
        *little(norm_bias, bias_first, bias_second, grad_bias),
        *little(group_table, table_first, table_second, grad_table),
    )


def solution(mesh):
    entry_split = ("dp", "mp")
    weight_specs = (P(None, None, "dp", None), P(None, None, "dp"), P(None, "dp", None), P(None, None, "dp"), P("dp", None))
    state = tuple(spec for spec in weight_specs for _ in range(3)) + (P(),) * 9
    return jax.shard_map(
        per_device,
        mesh=mesh,
        in_specs=(P(entry_split, None, None), P(entry_split), P(entry_split), P(entry_split, None)) + state,
        out_specs=(P(entry_split, None), P(entry_split, None, None), P()) + state,
        check_vma=False,
    )
```

```python
import functools
import math

import jax
import jax.numpy as jnp
from jax import lax
from jax.experimental import pallas as pl
from jax.experimental.pallas import tpu as pltpu
from jax.sharding import PartitionSpec as P

HD = 64
PIECES = 7
SLOTS = 8
STEP = 10
BLOCKS = 4
SMALL_ROWS = 32

norm_eps = 1e-05
beta_first = 0.9
beta_second = 0.999
adam_eps = 1e-08
learn_rate = 0.03
small_rate = 0.5
decay_rate = 0.01
clip_level = 1.0
masked_score = -1000000000.0
bfloat = jnp.bfloat16
single = jnp.float32
highest = lax.Precision.HIGHEST
MESH = pl.DeviceIdType.MESH
VMEM = pltpu.VMEM


def place():
    along, across = lax.axis_index("dp"), lax.axis_index("mp")
    return lax.div(along, 2), lax.rem(along, 2), lax.div(across, 2), lax.rem(across, 2)


def device(z, y, x, c):
    return (z * 2 + y, x * 2 + c)


def remote(src, dst, send_sem, recv_sem, target):
    return pltpu.make_async_remote_copy(
        src_ref=src, dst_ref=dst, send_sem=send_sem, recv_sem=recv_sem, device_id=target, device_id_type=MESH
    )


def await_arrival(dst, send_sem, recv_sem, target):
    remote(dst, dst, send_sem, recv_sem, target).wait_recv()


def greet(z_count, whole_dp):
    z, y, x, c = place()
    barrier = pltpu.get_barrier_semaphore()

    def signal(target):
        pl.semaphore_signal(barrier, inc=1, device_id=target, device_id_type=MESH)

    signal(device(z, y, 1 - x, c))
    signal(device(z, y, x, 1 - c))
    if whole_dp:
        dp = 2 * z_count

        def one(step):
            signal((lax.rem(z * 2 + y + step, dp), x * 2 + c))

        loop(1, dp, one)
        pl.semaphore_wait(barrier, dp + 1)
    else:
        signal(device(z, 1 - y, x, c))

        def one(step):
            signal(device(lax.rem(z + step, z_count), y, x, c))

        loop(1, z_count, one)
        pl.semaphore_wait(barrier, z_count + 2)


def when(condition, body):
    if isinstance(condition, bool):
        if condition:
            body()
    else:
        pl.when(condition)(body)


def otherwise(condition):
    return not condition if isinstance(condition, bool) else jnp.logical_not(condition)


def loop(low, high, body):
    if high - low <= 8:
        for step in range(low, high):
            body(step)
    else:

        def wrapped(step, carry):
            body(step)
            return carry

        lax.fori_loop(low, high, wrapped, 0)


def dot_nn(left_side, right_side):
    return lax.dot_general(left_side, right_side, (((1,), (0,)), ((), ())), preferred_element_type=single)


def dot_nt(left_side, right_side):
    return lax.dot_general(left_side, right_side, (((1,), (1,)), ((), ())), preferred_element_type=single)


def dot_tn(left_side, right_side):
    return lax.dot_general(left_side, right_side, (((0,), (0,)), ((), ())), preferred_element_type=single)


def normalize(values):
    centre = jnp.mean(values, axis=-1, keepdims=True)
    offset = values - centre
    spread = jnp.mean(offset * offset, axis=-1, keepdims=True)
    scale = lax.rsqrt(spread + norm_eps)
    return offset * scale, scale


def normalize_back(grad, unit, scale, gain_row):
    grad_unit = grad * gain_row
    first = jnp.mean(grad_unit, axis=-1, keepdims=True)
    second = jnp.mean(grad_unit * unit, axis=-1, keepdims=True)
    return scale * (grad_unit - first - unit * second)


def shared_gather(index, zz):
    return lax.rem(index + zz, 4) == 0


def shared_reduce(index, target):
    return lax.rem(index + target, 2) == 1


AHEAD = 2
LAGS = (1, 2, 3)
REDUCE = (0, 2, 4, 6, 8)


def step_kernel(
    layers, z_count,
    pieces_ref, meta_ref, cot_ref, shard_ref, gain_ref, bias_ref, table_ref,
    emb_ref, dx_ref, out_ref, total_ref, norm_ref,
    w_ref, grad_ref, z_buf, f_buf, part_ref,
    x_ref, unit_ref, scale_ref, a_ref, b_ref, qkv_ref, prob_ref, o_ref, g_ref, slope_ref, dqkv_ref, do_ref, acc_ref, turn_ref, dpool_ref,
    small_ref, s_c, s_x, s_y, s_z, s_cur, n_buf,
    gx_ss, gc_ss, g_rs, gc_rs,
    c_ss, c_rs, x_ss, x_rs, y_ss, y_rs, z_ss, z_rs, fx_ss, fx_rs, fc_ss, fc_rs, s_ss, s_rs, n_ss, n_rs, credit,
):
    mats = 3 * layers + 1
    proj = 3 * layers
    final = 2 * layers
    entries, _, width = pieces_ref.shape
    rows = entries * SLOTS
    half = rows // 2
    groups = table_ref.shape[0]
    pairs = width // 128
    dp = 2 * z_count
    z, y, x, c = place()
    me = z * 2 + y
    y_side, x_side, c_side = device(z, 1 - y, x, c), device(z, y, 1 - x, c), device(z, y, x, 1 - c)
    greet(z_count, True)


    def matrix_at(turn):
        early = 3 * (layers - 1)
        return jnp.where(turn < early, turn, jnp.where(turn == early, proj, turn - 1))

    def by_type(index, zz, body):
        shared = shared_gather(index, zz)
        when(shared, lambda: body(pl.ds(2 * c, 2), False))
        when(otherwise(shared), lambda: body(pl.ds(2 * c + x, 1), True))

    def gather_z(index, other, span):
        return remote(
            shard_ref.at[index, span], w_ref.at[index, span, z, y], z_ss.at[index, other], g_rs.at[index, 0, z, y], device(other, y, x, c)
        )

    def gather_y(index, zz, span, src=None):
        spot = w_ref.at[index, span, zz, y]
        return remote(spot if src is None else src, spot, y_ss.at[index, zz], g_rs.at[index, 0, zz, y], y_side)

    def gather_x(index, zz, yy, span):
        spot = w_ref.at[index, span, zz, yy]
        return remote(spot, spot, gx_ss.at[index, zz, yy], g_rs.at[index, 1, zz, yy], x_side)

    def gather_c(index):
        pair = w_ref.at[index, pl.ds(2 * c, 2)]
        return remote(pair, pair, gc_ss.at[index], gc_rs.at[index], c_side)

    def arrived(index, zz, yy, span):
        await_arrival(w_ref.at[index, span, zz, yy], y_ss.at[index, zz], g_rs.at[index, 0, zz, yy], y_side)

    def own(index):
        def send(span, cross):
            gather_y(index, z, span, shard_ref.at[index, span]).start()

            def one(other):
                pl.when(other != z)(lambda: gather_z(index, other, span).start())

            loop(0, z_count, one)

        by_type(index, z, send)

    def line(index):
        def one(zz):
            def pass_on(span, cross):
                arrived(index, zz, y, span)
                gather_y(index, zz, span).start()
                if cross:
                    gather_x(index, zz, y, span).start()

            pl.when(z != zz)(lambda: by_type(index, zz, pass_on))

        loop(0, z_count, one)

    def beside(index):
        def one(zz):
            def pass_on(span, cross):
                arrived(index, zz, 1 - y, span)
                if cross:
                    gather_x(index, zz, 1 - y, span).start()

            by_type(index, zz, pass_on)

        loop(0, z_count, one)

    def opposite(index):
        def each(zz):
            def one(yy):
                block = w_ref.at[index, pl.ds(2 * c + 1 - x, 1), zz, yy]
                await_arrival(block, gx_ss.at[index, zz, yy], g_rs.at[index, 1, zz, yy], x_side)

            def two():
                pl.when(zz != z)(lambda: one(y))
                one(1 - y)

            when(otherwise(shared_gather(index, zz)), two)

        loop(0, z_count, each)
        gather_c(index).start()

    def finish(index):
        pair = w_ref.at[index, pl.ds(2 * (1 - c), 2)]
        await_arrival(pair, gc_ss.at[index], gc_rs.at[index], c_side)

    def gather_sent(index):
        def each(zz):
            def done(span, cross):
                gather_y(index, zz, span).wait_send()
                if cross:
                    pl.when(zz != z)(lambda: gather_x(index, zz, y, span).wait_send())
                    gather_x(index, zz, 1 - y, span).wait_send()

                def one(other):
                    pl.when(other != z)(lambda: gather_z(index, other, span).wait_send())

                pl.when(zz == z)(lambda: loop(0, z_count, one))

            by_type(index, zz, done)

        loop(0, z_count, each)
        gather_c(index).wait_send()

    def block_of(index, block):
        return w_ref[index, block].reshape(width, width)

    def put_grad(index, block, values):
        grad_ref[index, block] = values.astype(bfloat).reshape(grad_ref.shape[2:])


    units = mats * z_count
    pair_c = pl.ds(2 * c, 2)

    def order(unit):
        return mats - 1 - lax.div(unit, z_count), lax.rem(unit, z_count)

    def local(span):
        return pl.ds(2 * c, 2) if span is None else pl.ds(2 * c + x, 1)

    def near(span):
        return pl.ds(0, 2) if span is None else pl.ds(x, 1)

    def to_c(index, target):
        return remote(
            grad_ref.at[index, pl.ds(2 * (1 - c), 2), target], w_ref.at[index, pl.ds(0, 2), target],
            c_ss.at[index, target], c_rs.at[index, target], c_side,
        )

    def to_x(index, target):
        return remote(
            grad_ref.at[index, 2 * c + 1 - x, target], w_ref.at[index, 2, target], x_ss.at[index, target], x_rs.at[index, target], x_side
        )

    def to_y(index, target, span):
        return remote(
            grad_ref.at[index, local(span), target, 1 - y], w_ref.at[index, 3, target, near(span)],
            y_ss.at[index, target], y_rs.at[index, target], y_side,
        )

    def to_z(index, target, span):
        return remote(
            grad_ref.at[index, local(span), target, y], z_buf.at[index, near(span), z],
            z_ss.at[index, target], z_rs.at[index, z], device(target, y, x, c),
        )

    def from_z(index, source, span):
        await_arrival(z_buf.at[index, near(span), source], z_ss.at[index, source], z_rs.at[index, source], device(source, y, x, c))

    def both(shared, body):
        when(shared, lambda: body(None))
        when(otherwise(shared), lambda: body(1))

    def add(ref, at, extra):
        ref[at] = (ref[at].astype(single) + extra.astype(single)).astype(bfloat)

    def give_credit(index):
        for kind, side in enumerate((c_side, x_side, y_side)):
            pl.semaphore_signal(credit.at[kind, index], inc=1, device_id=side, device_id_type=MESH)

    def start_matrix(index):
        give_credit(index)
        pl.semaphore_wait(credit.at[0, index], 1)
        loop(0, z_count, lambda target: to_c(index, target).start())

    def stage_c(unit):
        index, target = order(unit)
        to_c(index, target).wait_recv()
        for block in range(2):
            add(grad_ref, (index, 2 * c + block, target), w_ref[index, block, target])
        shared = shared_reduce(index, target)

        @pl.when(target == 0)
        def _():
            pl.semaphore_wait(credit.at[1, index], 1)
            pl.semaphore_wait(credit.at[2, index], 1)

        when(shared, lambda: to_y(index, target, None).start())
        when(otherwise(shared), lambda: to_x(index, target).start())

    def stage_x(unit):
        index, target = order(unit)

        @pl.when(otherwise(shared_reduce(index, target)))
        def _():
            to_x(index, target).wait_recv()
            add(grad_ref, (index, 2 * c + x, target), w_ref[index, 2, target])
            to_y(index, target, 1).start()

    def stage_y(unit):
        index, target = order(unit)

        def make(span):
            to_y(index, target, span).wait_recv()
            add(grad_ref, (index, local(span), target, y), w_ref[index, 3, target, near(span)])
            pl.when(target != z)(lambda: to_z(index, target, span).start())

        both(shared_reduce(index, target), make)

    def final_shared(index):
        return remote(f_buf.at[index, 0], f_buf.at[index, 1], fx_ss.at[index], fx_rs.at[index], x_side)

    def final_split(index):
        mine = out_ref.at[index, 2 * c + x]
        return remote(mine, mine, fx_ss.at[index], fx_rs.at[index], x_side)

    def final_c(index):
        pair = out_ref.at[index, pl.ds(2 * c, 2)]
        return remote(pair, pair, fc_ss.at[index], fc_rs.at[index], c_side)

    def stage_z(step):
        index = mats - 1 - step

        def make(span):
            def one(source):
                pl.when(source != z)(lambda: from_z(index, source, span))

            loop(0, z_count, one)
            part_ref[near(span)] = grad_ref[index, local(span), z, y].astype(single)

            def more(source):
                @pl.when(source != z)
                def _():
                    part_ref[near(span)] = part_ref[near(span)] + z_buf[index, near(span), source].astype(single)

            loop(0, z_count, more)

        shared = shared_reduce(index, z)
        both(shared, make)

        @pl.when(shared)
        def _():
            f_buf[index, 0] = part_ref[...].astype(bfloat)
            final_shared(index).start()

        @pl.when(otherwise(shared))
        def _():
            out_ref[index, pl.ds(2 * c + x, 1)] = part_ref[pl.ds(x, 1)].astype(bfloat)
            final_split(index).start()

    def stage_f(step):
        index = mats - 1 - step
        shared = shared_reduce(index, z)

        @pl.when(shared)
        def _():
            final_shared(index).wait_recv()
            total = f_buf[index, 0].astype(single) + f_buf[index, 1].astype(single)
            out_ref[index, pl.ds(2 * c, 2)] = total.astype(bfloat)

        @pl.when(otherwise(shared))
        def _():
            final_split(index).wait_recv()

        final_c(index).start()

    def reduce_tick(step):
        for lag, stage in zip(REDUCE, (stage_c, stage_x, stage_y)):
            unit = step - lag
            pl.when(jnp.logical_and(unit >= 0, unit < units))(functools.partial(stage, unit))
        for lag, stage in zip(REDUCE[3:], (stage_z, stage_f)):
            turn = step - lag
            whole = lax.div(turn, z_count)
            pl.when(jnp.logical_and(jnp.logical_and(turn >= 0, turn < units), turn == whole * z_count + z_count - 1))(
                functools.partial(stage, whole)
            )

    def spread_ticks(first, count, turn, turns):
        each = -(-count // turns)

        def one(step):
            mine = turn * each + step
            pl.when(mine < count)(lambda: reduce_tick(first + mine))

        loop(0, each, one)

    def small_step(stage):
        if stage == 0:
            remote(small_ref, s_c, s_ss.at[0], s_rs.at[0], c_side).start()
        elif stage == 1:
            remote(small_ref, s_c, s_ss.at[0], s_rs.at[0], c_side).wait_recv()
            s_cur[0] = small_ref[...] + s_c[...]
            remote(s_cur.at[0], s_x, s_ss.at[1], s_rs.at[1], x_side).start()
        elif stage == 2:
            remote(s_cur.at[0], s_x, s_ss.at[1], s_rs.at[1], x_side).wait_recv()
            s_cur[1] = s_cur[0] + s_x[...]
            remote(s_cur.at[1], s_y, s_ss.at[2], s_rs.at[2], y_side).start()
        elif stage == 3:
            remote(s_cur.at[1], s_y, s_ss.at[2], s_rs.at[2], y_side).wait_recv()
            s_z[z] = s_cur[1] + s_y[...]

            def send(step, carry):
                other = lax.rem(z + step, z_count)
                remote(s_z.at[z], s_z.at[z], s_ss.at[3 + other], s_rs.at[3 + z], device(other, y, x, c)).start()
                return carry

            lax.fori_loop(1, z_count, send, 0)
        else:

            def wait(step, carry):
                other = lax.rem(z + step, z_count)
                remote(s_z.at[other], s_z.at[other], s_ss.at[3 + other], s_rs.at[3 + other], device(other, y, x, c)).wait_recv()
                return carry

            lax.fori_loop(1, z_count, wait, 0)

            def gather(step, carry):
                return carry + s_z[step]

            total_ref[...] = lax.fori_loop(0, z_count, gather, jnp.zeros(total_ref.shape, single))


    def home(index, carry):
        for block in range(2):
            w_ref[index, 2 * c + block, z, y] = shard_ref[index, 2 * c + block]
        return carry

    lax.fori_loop(0, mats, home, 0)
    for first in range(AHEAD):
        own(matrix_at(first))

    tags_row = meta_ref[0:1, :]
    counts_row = meta_ref[1:2, :]
    columns = meta_ref[...].T
    tags_col = columns[:, 0:1]
    counts_col = columns[:, 1:2]

    group_col = lax.broadcasted_iota(jnp.int32, (rows, groups), 1).astype(single)
    onehot = (group_col == tags_col).astype(single)
    x_ref[...] = lax.dot_general(
        onehot, table_ref[...], (((1,), (0,)), ((), ())), precision=highest, preferred_element_type=single
    )
    for entry in range(entries):
        at = entry * SLOTS
        x_ref[at : at + PIECES, :] = x_ref[at : at + PIECES, :] + pieces_ref[entry].astype(single)

    row_at = lax.broadcasted_iota(jnp.int32, (half, 2 * half), 0)
    key_at = lax.rem(lax.broadcasted_iota(jnp.int32, (half, 2 * half), 1), half)
    same = lax.div(row_at, SLOTS) == lax.div(key_at, SLOTS)
    key_slot = lax.rem(key_at, SLOTS).astype(single)
    low_lane = lax.broadcasted_iota(jnp.int32, (half, 128), 1) < HD

    def key_mask(part):
        piece = counts_row[:, part * half : (part + 1) * half]
        counts_here = jnp.concatenate([piece, piece], axis=1)
        return jnp.logical_and(same, key_slot < counts_here)

    def split_pair(values):
        zero = jnp.zeros_like(values)
        return jnp.concatenate([jnp.where(low_lane, values, zero), jnp.where(low_lane, zero, values)], axis=0)

    def front(layer):
        values = x_ref[...]
        unit, scale = normalize(values)
        unit_ref[2 * layer] = unit
        scale_ref[2 * layer] = scale
        a = (unit * gain_ref[2 * layer] + bias_ref[2 * layer]).astype(bfloat)
        a_ref[layer] = a
        for part in range(3):
            qkv_ref[layer, part] = dot_nn(a, block_of(3 * layer, part)).astype(bfloat)
        for part in range(2):
            mask = key_mask(part)
            here = slice(part * half, (part + 1) * half)
            for pair in range(pairs):
                lanes = slice(pair * 128, (pair + 1) * 128)
                q = qkv_ref[layer, 0, here, lanes]
                keys = split_pair(qkv_ref[layer, 1, here, lanes])
                vals = split_pair(qkv_ref[layer, 2, here, lanes])
                scores = dot_nt(q, keys) * HD ** (-0.5)
                scores = jnp.where(mask, scores, masked_score)
                probs = []
                for head in range(2):
                    mine = scores[:, head * half : (head + 1) * half]
                    top = jnp.max(mine, axis=-1, keepdims=True)
                    raised = jnp.exp(mine - top)
                    probs.append(raised / jnp.sum(raised, axis=-1, keepdims=True))
                prob = jnp.concatenate(probs, axis=1)
                prob_ref[layer, part * pairs + pair] = prob
                o_ref[layer, here, lanes] = dot_nn(prob.astype(bfloat), vals).astype(bfloat)
        middle = values + dot_nt(o_ref[layer], block_of(3 * layer, 3))
        unit, scale = normalize(middle)
        unit_ref[2 * layer + 1] = unit
        scale_ref[2 * layer + 1] = scale
        b_ref[layer] = (unit * gain_ref[2 * layer + 1] + bias_ref[2 * layer + 1]).astype(bfloat)
        x_ref[...] = middle

    def rise(layer):
        def hidden(block, carry):
            u = dot_nn(b_ref[layer], block_of(3 * layer + 1, block))
            gate = 0.5 * (1.0 + lax.erf(u * math.sqrt(0.5)))
            g_ref[layer, block] = (u * gate).astype(bfloat)
            slope_ref[layer, block] = gate + u * (jnp.exp(-0.5 * u * u) * (1.0 / math.sqrt(2.0 * math.pi)))
            return carry

        lax.fori_loop(0, BLOCKS, hidden, 0)

    def fall(layer):
        def hidden(block, carry):
            x_ref[...] += dot_nt(g_ref[layer, block], block_of(3 * layer + 2, block))
            return carry

        lax.fori_loop(0, BLOCKS, hidden, 0)

    def project():
        total = jnp.zeros((entries, width), single)
        for block in range(BLOCKS):
            total += dot_nt(cot_ref[:, block * width : (block + 1) * width], block_of(proj, block))
        dpool_ref[...] = total

    depth = LAGS[-1]

    def gather_tick(step, carry):
        @pl.when(step + AHEAD < mats)
        def _():
            own(matrix_at(step + AHEAD))

        for lag, stage in zip((0, *LAGS), (line, beside, opposite, finish)):
            turn = step - lag
            pl.when(jnp.logical_and(turn >= 0, turn < mats))(lambda: stage(matrix_at(turn)))
        index = matrix_at(step - depth)
        layer = lax.div(index, 3)
        ready = jnp.logical_and(step >= depth, index < proj)
        for kind, work in enumerate((front, rise, fall)):
            pl.when(jnp.logical_and(ready, lax.rem(index, 3) == kind))(lambda: work(layer))
        pl.when(jnp.logical_and(step >= depth, index == proj))(project)
        return carry

    lax.fori_loop(0, mats + depth, gather_tick, 0)


    unit, scale = normalize(x_ref[...])
    normed = unit * gain_ref[final] + bias_ref[final]
    slot_col = lax.rem(lax.broadcasted_iota(jnp.int32, (rows, 1), 0), SLOTS).astype(single)
    used_col = (slot_col < counts_col).astype(single)
    pooled = jnp.sum((normed * used_col).reshape(entries, SLOTS, width), axis=1)
    counts_entry = counts_col.reshape(entries, SLOTS, 1)[:, 0, :]
    pooled_low = (pooled / counts_entry).astype(bfloat)
    for block in range(BLOCKS):
        lanes = slice(block * width, (block + 1) * width)
        emb_ref[:, lanes] = dot_nn(pooled_low, block_of(proj, block))
        put_grad(proj, block, dot_tn(pooled_low, cot_ref[:, lanes]))
    lax.fori_loop(0, mats, lambda index, carry: (gather_sent(index), carry)[1], 0)
    start_matrix(proj)
    grad_pooled = dpool_ref[...] / counts_entry
    grad_normed = jnp.broadcast_to(grad_pooled[:, None, :], (entries, SLOTS, width)).reshape(rows, width) * used_col
    small_ref[...] = jnp.zeros_like(small_ref)
    small_ref[pl.ds(final, 1), :] = jnp.sum(grad_normed * unit, axis=0, keepdims=True)
    small_ref[pl.ds(SLOTS + final, 1), :] = jnp.sum(grad_normed, axis=0, keepdims=True)
    acc_ref[...] = normalize_back(grad_normed, unit, scale, gain_ref[final])

    def backward(step, carry):
        layer = layers - 1 - step
        tick = 3 * z_count * step
        grad_next = acc_ref[...]
        do_ref[...] = grad_next.astype(bfloat)
        turn_ref[0] = grad_next.T.astype(bfloat)
        turn_ref[1] = b_ref[layer].astype(single).T.astype(bfloat)
        x_ref[...] = jnp.zeros_like(x_ref)

        def hidden(block, carry):
            put_grad(3 * layer + 2, block, dot_nn(turn_ref[0], g_ref[layer, block]))
            grad_act = dot_nn(do_ref[...], block_of(3 * layer + 2, block))
            du = (grad_act * slope_ref[layer, block]).astype(bfloat)
            put_grad(3 * layer + 1, block, dot_nn(turn_ref[1], du))
            x_ref[...] += dot_nt(du, block_of(3 * layer + 1, block))
            spread_ticks(tick, z_count, block, BLOCKS)
            return carry

        lax.fori_loop(0, BLOCKS, hidden, 0)
        start_matrix(3 * layer + 2)
        start_matrix(3 * layer + 1)
        grad_b = x_ref[...]
        unit = unit_ref[2 * layer + 1]
        small_ref[pl.ds(2 * layer + 1, 1), :] = jnp.sum(grad_b * unit, axis=0, keepdims=True)
        small_ref[pl.ds(SLOTS + 2 * layer + 1, 1), :] = jnp.sum(grad_b, axis=0, keepdims=True)
        grad_middle = grad_next + normalize_back(grad_b, unit, scale_ref[2 * layer + 1], gain_ref[2 * layer + 1])
        acc_ref[...] = grad_middle
        dy = grad_middle.astype(bfloat)
        put_grad(3 * layer, 3, dot_nn(grad_middle.T.astype(bfloat), o_ref[layer]))
        do_ref[...] = dot_nn(dy, block_of(3 * layer, 3)).astype(bfloat)

        def attend(pair, carry):
            lanes = pl.ds(pl.multiple_of(pair * 128, 128), 128)
            for part in range(2):
                here = slice(part * half, (part + 1) * half)
                q = qkv_ref[layer, 0, here, lanes]
                keys = split_pair(qkv_ref[layer, 1, here, lanes])
                vals = split_pair(qkv_ref[layer, 2, here, lanes])
                do = do_ref[here, lanes]
                prob = prob_ref[layer, part * pairs + pair]
                grad_prob = dot_nt(do, vals)
                product = grad_prob * prob
                scored = []
                for head in range(2):
                    spans = slice(head * half, (head + 1) * half)
                    total = jnp.sum(product[:, spans], axis=-1, keepdims=True)
                    scored.append(product[:, spans] - prob[:, spans] * total)
                ds_low = jnp.concatenate(scored, axis=1).astype(bfloat)
                dv = dot_tn(prob.astype(bfloat), do)
                dk = dot_tn(ds_low, q)
                dq = dot_nn(ds_low, keys)
                dqkv_ref[0, here, lanes] = (dq * HD ** (-0.5)).astype(bfloat)
                dqkv_ref[1, here, lanes] = (jnp.where(low_lane, dk[:half], dk[half:]) * HD ** (-0.5)).astype(bfloat)
                dqkv_ref[2, here, lanes] = jnp.where(low_lane, dv[:half], dv[half:]).astype(bfloat)
            spread_ticks(tick + z_count, 2 * z_count, pair, pairs)
            return carry

        lax.fori_loop(0, pairs, attend, 0)
        turned = a_ref[layer].astype(single).T.astype(bfloat)
        grad_a = jnp.zeros((rows, width), single)
        for part in range(3):
            put_grad(3 * layer, part, dot_nn(turned, dqkv_ref[part]))
            grad_a += dot_nt(dqkv_ref[part], block_of(3 * layer, part))
        start_matrix(3 * layer)
        unit = unit_ref[2 * layer]
        small_ref[pl.ds(2 * layer, 1), :] = jnp.sum(grad_a * unit, axis=0, keepdims=True)
        small_ref[pl.ds(SLOTS + 2 * layer, 1), :] = jnp.sum(grad_a, axis=0, keepdims=True)
        acc_ref[...] += normalize_back(grad_a, unit, scale_ref[2 * layer], gain_ref[2 * layer])
        return carry

    lax.fori_loop(0, layers, backward, 0)
    group_row = lax.broadcasted_iota(jnp.int32, (groups, rows), 0).astype(single)
    spread = (group_row == tags_row).astype(single)
    small_ref[2 * SLOTS : 2 * SLOTS + groups, :] = lax.dot_general(
        spread, acc_ref[...], (((1,), (0,)), ((), ())), precision=highest, preferred_element_type=single
    )
    small_step(0)
    for entry in range(entries):
        at = entry * SLOTS
        dx_ref[entry] = acc_ref[at : at + PIECES, :]

    def tail_tick(step, carry):
        reduce_tick(step)
        return carry

    last = units - z_count
    small_step(1)
    lax.fori_loop(last, last + 2, tail_tick, 0)
    small_step(2)
    lax.fori_loop(last + 2, last + 4, tail_tick, 0)
    small_step(3)
    lax.fori_loop(last + 4, units + REDUCE[-1], tail_tick, 0)
    small_step(4)

    def arrive(index, carry):
        pair = out_ref.at[index, pl.ds(2 * (1 - c), 2)]
        remote(pair, pair, fc_ss.at[index], fc_rs.at[index], c_side).wait_recv()
        return carry

    lax.fori_loop(0, mats, arrive, 0)

    def squares(index, carry):
        values = out_ref[index].astype(single)
        return carry + jnp.sum(jnp.sum(values * values, axis=0), axis=0, keepdims=True)

    squared = lax.fori_loop(0, mats, squares, jnp.zeros((1, out_ref.shape[3]), single))
    n_buf[me] = jnp.broadcast_to(squared, n_buf.shape[1:])

    def send_norm(step, carry):
        other = lax.rem(me + step, dp)
        remote(n_buf.at[me], n_buf.at[me], n_ss.at[other], n_rs.at[me], (other, x * 2 + c)).start()
        return carry

    lax.fori_loop(1, dp, send_norm, 0)

    def wait_norm(step, carry):
        other = lax.rem(me + step, dp)
        remote(n_buf.at[other], n_buf.at[other], n_ss.at[other], n_rs.at[other], (other, x * 2 + c)).wait_recv()
        return carry

    lax.fori_loop(1, dp, wait_norm, 0)

    def sum_norm(step, carry):
        return carry + n_buf[step]

    spread = lax.fori_loop(0, dp, sum_norm, jnp.zeros(n_buf.shape[1:], single))
    smalls = total_ref[...]
    norm_ref[...] = jnp.broadcast_to(
        jnp.sum(spread[0:1], axis=1, keepdims=True) + jnp.sum(jnp.sum(smalls * smalls, axis=0, keepdims=True), axis=1, keepdims=True),
        norm_ref.shape,
    )

    def done_unit(unit, carry):
        index, target = order(unit)
        to_c(index, target).wait_send()
        shared = shared_reduce(index, target)
        when(otherwise(shared), lambda: to_x(index, target).wait_send())

        def make(span):
            to_y(index, target, span).wait_send()
            pl.when(target != z)(lambda: to_z(index, target, span).wait_send())

        both(shared, make)
        return carry

    lax.fori_loop(0, units, done_unit, 0)

    def done_mat(index, carry):
        shared = shared_reduce(index, z)
        when(shared, lambda: final_shared(index).wait_send())
        when(otherwise(shared), lambda: final_split(index).wait_send())
        final_c(index).wait_send()
        return carry

    lax.fori_loop(0, mats, done_mat, 0)
    remote(small_ref, s_c, s_ss.at[0], s_rs.at[0], c_side).wait_send()
    remote(s_cur.at[0], s_x, s_ss.at[1], s_rs.at[1], x_side).wait_send()
    remote(s_cur.at[1], s_y, s_ss.at[2], s_rs.at[2], y_side).wait_send()

    def done_z(step, carry):
        other = lax.rem(z + step, z_count)
        remote(s_z.at[z], s_z.at[z], s_ss.at[3 + other], s_rs.at[3 + z], device(other, y, x, c)).wait_send()
        return carry

    lax.fori_loop(1, z_count, done_z, 0)

    def done_norm(step, carry):
        other = lax.rem(me + step, dp)
        remote(n_buf.at[me], n_buf.at[me], n_ss.at[other], n_rs.at[me], (other, x * 2 + c)).wait_send()
        return carry

    lax.fori_loop(1, dp, done_norm, 0)


def train_step(pieces, meta, cotangent, packed, gain, bias, table, layers, dp):
    entries, _, width = pieces.shape
    mats, blocks, shard_rows, _ = packed.shape
    rows = entries * SLOTS
    pairs = width // 128
    z_count = dp // 2
    small = (SMALL_ROWS, width)
    vmem = pl.BlockSpec(memory_space=VMEM)
    dma = pltpu.SemaphoreType.DMA
    whole = (mats, blocks, z_count, 2, shard_rows, width)
    return pl.pallas_call(
        functools.partial(step_kernel, layers, z_count),
        out_shape=(
            jax.ShapeDtypeStruct(cotangent.shape, single),
            jax.ShapeDtypeStruct(pieces.shape, single),
            jax.ShapeDtypeStruct(packed.shape, bfloat),
            jax.ShapeDtypeStruct(small, single),
            jax.ShapeDtypeStruct((8, 128), single),
        ),
        in_specs=[vmem] * 7,
        out_specs=(vmem,) * 5,
        scratch_shapes=[
            VMEM(whole, bfloat),
            VMEM(whole, bfloat),
            VMEM((mats, 2, z_count, shard_rows, width), bfloat),
            VMEM((mats, 2, 2, shard_rows, width), bfloat),
            VMEM((2, shard_rows, width), single),
            VMEM((rows, width), single),
            VMEM((2 * layers, rows, width), single),
            VMEM((2 * layers, rows, 1), single),
            VMEM((layers, rows, width), bfloat),
            VMEM((layers, rows, width), bfloat),
            VMEM((layers, 3, rows, width), bfloat),
            VMEM((layers, 2 * pairs, rows // 2, rows), single),
            VMEM((layers, rows, width), bfloat),
            VMEM((layers, BLOCKS, rows, width), bfloat),
            VMEM((layers, BLOCKS, rows, width), single),
            VMEM((3, rows, width), bfloat),
            VMEM((rows, width), bfloat),
            VMEM((rows, width), single),
            VMEM((2, width, rows), bfloat),
            VMEM((entries, width), single),
            VMEM(small, single),
            VMEM(small, single),
            VMEM(small, single),
            VMEM(small, single),
            VMEM((z_count, *small), single),
            VMEM((2, *small), single),
            VMEM((dp, 8, width), single),
            dma((mats, z_count, 2)),
            dma((mats,)),
            dma((mats, 2, z_count, 2)),
            dma((mats,)),
            *[dma((mats, z_count))] * 8,
            *[dma((mats,))] * 4,
            dma((3 + z_count,)),
            dma((3 + z_count,)),
            dma((dp,)),
            dma((dp,)),
            pltpu.SemaphoreType.REGULAR((3, mats)),
        ],
        compiler_params=pltpu.CompilerParams(collective_id=1, has_side_effects=True, vmem_limit_bytes=60 * 2**20),
        name="train_step",
    )(pieces, meta, cotangent, packed, gain, bias, table)


def adam_update(weight, first, second, gradient, clip_scale, decay, step_rate):
    clipped = gradient * clip_scale
    first_new = beta_first * first + (1.0 - beta_first) * clipped
    second_new = beta_second * second + (1.0 - beta_second) * clipped * clipped
    first_hat = first_new / (1.0 - beta_first**STEP)
    second_hat = second_new / (1.0 - beta_second**STEP)
    weight_new = weight - step_rate * (first_hat / (jnp.sqrt(second_hat) + adam_eps) + decay * weight)
    return (weight_new, first_new, second_new)


def pack(qkv, out, up, down, proj):
    layers, _, rows, width = qkv.shape
    parts = []
    front = jnp.concatenate([qkv, jnp.swapaxes(out, 1, 2)[:, None]], axis=1)
    rise = jnp.swapaxes(up.reshape(layers, rows, BLOCKS, width), 1, 2)
    fall = jnp.swapaxes(jnp.swapaxes(down, 1, 2).reshape(layers, rows, BLOCKS, width), 1, 2)
    body = jnp.stack([front, rise, fall], axis=1).reshape(3 * layers, BLOCKS, rows, width)
    last = jnp.swapaxes(proj.reshape(rows, BLOCKS, width), 0, 1)[None]
    return jnp.concatenate([body, last], axis=0)


def unpack(packed, layers):
    _, _, rows, width = packed.shape
    body = packed[: 3 * layers].reshape(layers, 3, BLOCKS, rows, width)
    qkv = body[:, 0, :3]
    out = jnp.swapaxes(body[:, 0, 3], 1, 2)
    up = jnp.swapaxes(body[:, 1], 1, 2).reshape(layers, rows, BLOCKS * width)
    down = jnp.swapaxes(jnp.swapaxes(body[:, 2], 1, 2).reshape(layers, rows, BLOCKS * width), 1, 2)
    proj = jnp.swapaxes(packed[3 * layers], 0, 1).reshape(rows, BLOCKS * width)
    return qkv, out, up, down, proj


def per_device(
    pieces, script_tags, counts, cotangent,
    qkv_weight, qkv_first, qkv_second,
    out_weight, out_first, out_second,
    up_weight, up_first, up_second,
    down_weight, down_first, down_second,
    proj_weight, proj_first, proj_second,
    norm_gain, gain_first, gain_second,
    norm_bias, bias_first, bias_second,
    group_table, table_first, table_second,
):
    layers = qkv_weight.shape[0]
    width = pieces.shape[2]
    dp = lax.axis_size("dp")
    norms = norm_gain.shape[0]
    groups = group_table.shape[0]
    packed = pack(
        qkv_weight.astype(bfloat), out_weight.astype(bfloat), up_weight.astype(bfloat), down_weight.astype(bfloat), proj_weight.astype(bfloat)
    )
    meta = jnp.stack([jnp.repeat(script_tags, SLOTS), jnp.repeat(counts, SLOTS)]).astype(single)
    meta = jnp.concatenate([meta, jnp.zeros((SLOTS - 2, meta.shape[1]), single)], axis=0)
    embeddings, input_grad, reduced, small_total, square_total = train_step(
        pieces, meta, cotangent, packed,
        norm_gain.reshape(norms, 1, width), norm_bias.reshape(norms, 1, width), group_table, layers, dp,
    )
    grad_norm = jnp.sqrt(square_total[0, 0])
    clip_scale = jnp.minimum(1.0, clip_level / (grad_norm + 1e-06))
    grad_qkv, grad_out, grad_up, grad_down, grad_proj = unpack(reduced.astype(single), layers)
    grad_gain = small_total[:norms]
    grad_bias = small_total[SLOTS : SLOTS + norms]
    grad_table = small_total[2 * SLOTS : 2 * SLOTS + groups]
    big = functools.partial(adam_update, clip_scale=clip_scale, decay=decay_rate, step_rate=learn_rate)
    little = functools.partial(adam_update, clip_scale=clip_scale, decay=0.0, step_rate=small_rate)
    return (
        embeddings,
        input_grad,
        grad_norm,
        *big(qkv_weight, qkv_first, qkv_second, grad_qkv),
        *big(out_weight, out_first, out_second, grad_out),
        *big(up_weight, up_first, up_second, grad_up),
        *big(down_weight, down_first, down_second, grad_down),
        *big(proj_weight, proj_first, proj_second, grad_proj),
        *little(norm_gain, gain_first, gain_second, grad_gain),
        *little(norm_bias, bias_first, bias_second, grad_bias),
        *little(group_table, table_first, table_second, grad_table),
    )


def solution(mesh):
    entry_split = ("dp", "mp")
    weight_specs = (P(None, None, "dp", None), P(None, None, "dp"), P(None, "dp", None), P(None, None, "dp"), P("dp", None))
    state = tuple(spec for spec in weight_specs for _ in range(3)) + (P(),) * 9
    return jax.shard_map(
        per_device,
        mesh=mesh,
        in_specs=(P(entry_split, None, None), P(entry_split), P(entry_split), P(entry_split, None)) + state,
        out_specs=(P(entry_split, None), P(entry_split, None, None), P()) + state,
        check_vma=False,
    )
```

```python
import functools
import math

import jax
import jax.numpy as jnp
from jax import lax
from jax.experimental import pallas as pl
from jax.experimental.pallas import tpu as pltpu
from jax.sharding import PartitionSpec as P

HD = 64
PIECES = 7
SLOTS = 8
STEP = 10
BLOCKS = 4
SMALL_ROWS = 32

norm_eps = 1e-05
beta_first = 0.9
beta_second = 0.999
adam_eps = 1e-08
learn_rate = 0.03
small_rate = 0.5
decay_rate = 0.01
clip_level = 1.0
masked_score = -1000000000.0
bfloat = jnp.bfloat16
single = jnp.float32
highest = lax.Precision.HIGHEST
MESH = pl.DeviceIdType.MESH
VMEM = pltpu.VMEM


def place():
    along, across = lax.axis_index("dp"), lax.axis_index("mp")
    return lax.div(along, 2), lax.rem(along, 2), lax.div(across, 2), lax.rem(across, 2)


def device(z, y, x, c):
    return (z * 2 + y, x * 2 + c)


def remote(src, dst, send_sem, recv_sem, target):
    return pltpu.make_async_remote_copy(
        src_ref=src, dst_ref=dst, send_sem=send_sem, recv_sem=recv_sem, device_id=target, device_id_type=MESH
    )


def await_arrival(dst, send_sem, recv_sem, target):
    remote(dst, dst, send_sem, recv_sem, target).wait_recv()


def greet(z_count):
    z, y, x, c = place()
    barrier = pltpu.get_barrier_semaphore()

    def signal(target):
        pl.semaphore_signal(barrier, inc=1, device_id=target, device_id_type=MESH)

    signal(device(z, y, 1 - x, c))
    signal(device(z, y, x, 1 - c))
    dp = 2 * z_count

    def one(step):
        other = lax.rem(z * 2 + y + step, dp)
        signal((other, x * 2 + c))
        signal((other, x * 2 + 1 - c))

    loop(1, dp, one)
    return lambda: pl.semaphore_wait(barrier, 2 * dp)


def when(condition, body):
    if isinstance(condition, bool):
        if condition:
            body()
    else:
        pl.when(condition)(body)


def otherwise(condition):
    return not condition if isinstance(condition, bool) else jnp.logical_not(condition)


def loop(low, high, body):
    if high - low <= 8:
        for step in range(low, high):
            body(step)
    else:

        def wrapped(step, carry):
            body(step)
            return carry

        lax.fori_loop(low, high, wrapped, 0)


def dot_nn(left_side, right_side):
    return lax.dot_general(left_side, right_side, (((1,), (0,)), ((), ())), preferred_element_type=single)


def dot_nt(left_side, right_side):
    return lax.dot_general(left_side, right_side, (((1,), (1,)), ((), ())), preferred_element_type=single)


def dot_tn(left_side, right_side):
    return lax.dot_general(left_side, right_side, (((0,), (0,)), ((), ())), preferred_element_type=single)


def normalize(values):
    centre = jnp.mean(values, axis=-1, keepdims=True)
    offset = values - centre
    spread = jnp.mean(offset * offset, axis=-1, keepdims=True)
    scale = lax.rsqrt(spread + norm_eps)
    return offset * scale, scale


def normalize_back(grad, unit, scale, gain_row):
    grad_unit = grad * gain_row
    first = jnp.mean(grad_unit, axis=-1, keepdims=True)
    second = jnp.mean(grad_unit * unit, axis=-1, keepdims=True)
    return scale * (grad_unit - first - unit * second)


def shared_gather(index, zz):
    return lax.rem(index + zz, 4) == 0


def shared_reduce(index, target):
    return lax.rem(index + target, 2) == 1


AHEAD = 2
LAGS = (1, 2, 3)
REDUCE = (0, 3, 6, 8, 9, 11)
SHIFT = 0
MARKS = (2, 5, 8, 11)


def step_kernel(
    layers, z_count,
    pieces_hbm, tags_hbm, counts_hbm, cot_hbm, qkv_hbm, outward_hbm, rise_hbm, fall_hbm, proj_hbm, gain_hbm, bias_hbm, table_hbm,
    emb_hbm, dx_hbm, out_ref, total_ref, norm_ref,
    pieces_ref, tags_ref, counts_ref, cot_ref, gain_ref, bias_ref, table_ref, emb_ref, dx_ref, sum_ref,
    w_ref, grad_ref, z_buf, f_buf, part_ref,
    x_ref, unit_ref, scale_ref, a_ref, b_ref, qkv_ref, prob_ref, o_ref, g_ref, slope_ref, dqkv_ref, do_ref, acc_ref, turn_ref, dpool_ref,
    small_ref, s_c, s_x, s_y, s_z, s_cur, n_buf,
    gx_ss, gc_ss, g_rs, gc_rs,
    c_ss, c_rs, x_ss, x_rs, y_ss, y_rs, z_ss, z_rs, fx_ss, fx_rs, fc_ss, fc_rs, s_ss, s_rs, n_ss, n_rs, credit,
    in_sem, load_sem, store_sem,
):
    mats = 3 * layers + 1
    proj = 3 * layers
    final = 2 * layers
    _, entries, width = pieces_ref.shape
    rows = entries * SLOTS
    half = rows // 2
    group = entries // 2
    groups = table_ref.shape[0]
    pairs = width // 128
    dp = 2 * z_count
    shard_rows = out_ref.shape[2]
    z, y, x, c = place()
    me = z * 2 + y
    y_side, x_side, c_side = device(z, 1 - y, x, c), device(z, y, 1 - x, c), device(z, y, x, 1 - c)
    all_here = greet(z_count)


    inputs = [
        pltpu.make_async_copy(src, dst, in_sem.at[at])
        for at, (src, dst) in enumerate(
            (
                (tags_hbm, tags_ref), (counts_hbm, counts_ref), (pieces_hbm, pieces_ref), (table_hbm, table_ref),
                (gain_hbm, gain_ref), (bias_hbm, bias_ref), (cot_hbm, cot_ref),
            )
        )
    ]

    def shard_slot(index, block):
        at = 2 * index + block
        return slope_ref.at[at % layers, at // layers % BLOCKS, pl.ds(at // (layers * BLOCKS) * shard_rows, shard_rows)]

    def load(index, block, src):
        return pltpu.make_async_copy(src, shard_slot(index, block), load_sem.at[index, block])

    def each_load(act):
        for first in range(mats):
            index = gather_order[first]
            layer, kind = divmod(index, 3)
            for block in range(2):
                if index == proj or kind:
                    source = proj_hbm if index == proj else (rise_hbm, fall_hbm)[kind - 1].at[layer]
                    act(index, block, load(index, block, source.at[:, pl.ds(pl.multiple_of((2 * c + block) * width, width), width)]))
                else:
                    choice = (qkv_hbm.at[layer, block], qkv_hbm.at[layer, 2] if block == 0 else outward_hbm.at[layer])
                    for core in range(2):
                        pl.when(c == core)(functools.partial(act, index, block, load(index, block, choice[core])))

    gather_order = [*range(3 * (layers - 1)), proj, *range(3 * (layers - 1), proj)]

    def place_block(index, block, copy):
        copy.wait()
        w_ref[index, 2 * c + block, z, y] = shard_slot(index, block)[...].astype(bfloat)

    each_load(lambda index, block, copy: copy.start())
    for copy in inputs:
        copy.start()
    each_load(place_block)
    all_here()


    def matrix_at(turn):
        early = 3 * (layers - 1)
        return jnp.where(turn < early, turn, jnp.where(turn == early, proj, turn - 1))

    def by_type(index, zz, body):
        shared = shared_gather(index, zz)
        when(shared, lambda: body(pl.ds(2 * c, 2), False))
        when(otherwise(shared), lambda: body(pl.ds(2 * c + x, 1), True))

    def gather_z(index, other, span):
        return remote(
            w_ref.at[index, span, z, y], w_ref.at[index, span, z, y], z_ss.at[index, other], g_rs.at[index, 0, z, y], device(other, y, x, c)
        )

    def gather_y(index, zz, span):
        spot = w_ref.at[index, span, zz, y]
        return remote(spot, spot, y_ss.at[index, zz], g_rs.at[index, 0, zz, y], y_side)

    def gather_x(index, zz, yy, span):
        spot = w_ref.at[index, span, zz, yy]
        return remote(spot, spot, gx_ss.at[index, zz, yy], g_rs.at[index, 1, zz, yy], x_side)

    def gather_c(index):
        pair = w_ref.at[index, pl.ds(2 * c, 2)]
        return remote(pair, pair, gc_ss.at[index], gc_rs.at[index], c_side)

    def arrived(index, zz, yy, span):
        await_arrival(w_ref.at[index, span, zz, yy], y_ss.at[index, zz], g_rs.at[index, 0, zz, yy], y_side)

    def own(index):
        def send(span, cross):
            gather_y(index, z, span).start()

            def one(other):
                pl.when(other != z)(lambda: gather_z(index, other, span).start())

            loop(0, z_count, one)

        by_type(index, z, send)

    def line(index):
        def one(zz):
            def pass_on(span, cross):
                arrived(index, zz, y, span)
                gather_y(index, zz, span).start()
                if cross:
                    gather_x(index, zz, y, span).start()

            pl.when(z != zz)(lambda: by_type(index, zz, pass_on))

        loop(0, z_count, one)

    def beside(index):
        def one(zz):
            def pass_on(span, cross):
                arrived(index, zz, 1 - y, span)
                if cross:
                    gather_x(index, zz, 1 - y, span).start()

            by_type(index, zz, pass_on)

        loop(0, z_count, one)

    def opposite(index):
        def each(zz):
            def one(yy):
                block = w_ref.at[index, pl.ds(2 * c + 1 - x, 1), zz, yy]
                await_arrival(block, gx_ss.at[index, zz, yy], g_rs.at[index, 1, zz, yy], x_side)

            def two():
                pl.when(zz != z)(lambda: one(y))
                one(1 - y)

            when(otherwise(shared_gather(index, zz)), two)

        loop(0, z_count, each)
        gather_c(index).start()

    def finish(index):
        pair = w_ref.at[index, pl.ds(2 * (1 - c), 2)]
        await_arrival(pair, gc_ss.at[index], gc_rs.at[index], c_side)

    def gather_sent(index):
        def each(zz):
            def done(span, cross):
                gather_y(index, zz, span).wait_send()
                if cross:
                    pl.when(zz != z)(lambda: gather_x(index, zz, y, span).wait_send())
                    gather_x(index, zz, 1 - y, span).wait_send()

                def one(other):
                    pl.when(other != z)(lambda: gather_z(index, other, span).wait_send())

                pl.when(zz == z)(lambda: loop(0, z_count, one))

            by_type(index, zz, done)

        loop(0, z_count, each)
        gather_c(index).wait_send()

    def block_of(index, block):
        return w_ref[index, block].reshape(width, width)

    def put_grad(index, block, values):
        grad_ref[index, block] = values.astype(bfloat).reshape(grad_ref.shape[2:])


    units = mats * z_count
    pair_c = pl.ds(2 * c, 2)

    def order(unit):
        return mats - 1 - lax.div(unit, z_count), lax.rem(unit, z_count)

    def local(span):
        return pl.ds(2 * c, 2) if span is None else pl.ds(2 * c + x, 1)

    def near(span):
        return pl.ds(0, 2) if span is None else pl.ds(x, 1)

    def to_c(index, target):
        return remote(
            grad_ref.at[index, pl.ds(2 * (1 - c), 2), target], w_ref.at[index, pl.ds(2 * c, 2), target],
            c_ss.at[index, target], c_rs.at[index, target], c_side,
        )

    def from_c(index, target):
        await_arrival(w_ref.at[index, pl.ds(2 * (1 - c), 2), target], c_ss.at[index, target], c_rs.at[index, target], c_side)

    def to_x(index, target):
        return remote(
            grad_ref.at[index, 2 * c + 1 - x, target], w_ref.at[index, 2 * c, target], x_ss.at[index, target], x_rs.at[index, target], x_side
        )

    def to_y(index, target, span):
        return remote(
            grad_ref.at[index, local(span), target, 1 - y], w_ref.at[index, 2 * c + 1, target, near(span)],
            y_ss.at[index, target], y_rs.at[index, target], y_side,
        )

    relays = z_count >= 4

    def at_far_end(target):
        return jnp.logical_and(relays, jnp.abs(target - z) == z_count - 1)

    def passes_on(target):
        up = jnp.logical_and(target == z_count - 1, z == 1)
        down = jnp.logical_and(target == 0, z == z_count - 2)
        return jnp.logical_and(relays, jnp.logical_or(up, down))

    def to_z(index, target, span):
        far = at_far_end(target)
        there = jnp.where(far, jnp.where(z == 0, 1, z_count - 2), target)
        slot = jnp.where(far, there, z)
        return remote(
            grad_ref.at[index, local(span), target, y], z_buf.at[index, near(span), slot],
            z_ss.at[index, target], z_rs.at[index, slot], device(there, y, x, c),
        )

    def from_z(index, source, span):
        other = jnp.where(source == z, jnp.where(z == 1, 0, z_count - 1), source)
        await_arrival(z_buf.at[index, near(span), source], z_ss.at[index, source], z_rs.at[index, source], device(other, y, x, c))

    def both(shared, body):
        when(shared, lambda: body(None))
        when(otherwise(shared), lambda: body(1))

    def add(ref, at, extra):
        ref[at] = (ref[at].astype(single) + extra.astype(single)).astype(bfloat)

    def give_credit(index, kinds):
        for kind in kinds:
            side = (c_side, x_side, y_side)[kind]
            pl.semaphore_signal(credit.at[kind, index], inc=1, device_id=side, device_id_type=MESH)

    def start_matrix(index):
        give_credit(index, (0,))
        pl.semaphore_wait(credit.at[0, index], 1)
        loop(0, z_count, lambda target: to_c(index, target).start())

    def stage_c(unit):
        index, target = order(unit)
        from_c(index, target)
        for block in range(2):
            add(grad_ref, (index, 2 * c + block, target), w_ref[index, 2 * (1 - c) + block, target])
        shared = shared_reduce(index, target)

        @pl.when(target == 0)
        def _():
            pl.semaphore_wait(credit.at[1, index], 1)
            pl.semaphore_wait(credit.at[2, index], 1)

        when(shared, lambda: to_y(index, target, None).start())
        when(otherwise(shared), lambda: to_x(index, target).start())

    def stage_x(unit):
        index, target = order(unit)

        @pl.when(otherwise(shared_reduce(index, target)))
        def _():
            to_x(index, target).wait_recv()
            add(grad_ref, (index, 2 * c + x, target), w_ref[index, 2 * c, target])
            to_y(index, target, 1).start()

    def stage_y(unit):
        index, target = order(unit)

        def make(span):
            to_y(index, target, span).wait_recv()
            add(grad_ref, (index, local(span), target, y), w_ref[index, 2 * c + 1, target, near(span)])
            pl.when(jnp.logical_and(target != z, jnp.logical_not(passes_on(target))))(lambda: to_z(index, target, span).start())

        both(shared_reduce(index, target), make)

    def stage_r(unit):
        index, target = order(unit)

        def make(span):
            from_z(index, z, span)
            add(grad_ref, (index, local(span), target, y), z_buf[index, near(span), z])
            to_z(index, target, span).start()

        pl.when(passes_on(target))(lambda: both(shared_reduce(index, target), make))

    def final_shared(index):
        return remote(f_buf.at[index, 0], f_buf.at[index, 1], fx_ss.at[index], fx_rs.at[index], x_side)

    def final_split(index):
        mine = out_ref.at[index, 2 * c + x]
        return remote(mine, mine, fx_ss.at[index], fx_rs.at[index], x_side)

    def final_c(index):
        pair = out_ref.at[index, pl.ds(2 * c, 2)]
        return remote(pair, pair, fc_ss.at[index], fc_rs.at[index], c_side)

    def stage_z(step):
        index = mats - 1 - step

        def make(span):
            def sends(source):
                far = jnp.logical_and(relays, jnp.abs(source - z) == z_count - 1)
                return jnp.logical_and(source != z, jnp.logical_not(far))

            def one(source):
                pl.when(sends(source))(lambda: from_z(index, source, span))

            loop(0, z_count, one)
            part_ref[near(span)] = grad_ref[index, local(span), z, y].astype(single)

            def more(source):
                @pl.when(sends(source))
                def _():
                    part_ref[near(span)] = part_ref[near(span)] + z_buf[index, near(span), source].astype(single)

            loop(0, z_count, more)

        shared = shared_reduce(index, z)
        both(shared, make)

        @pl.when(shared)
        def _():
            f_buf[index, 0] = part_ref[...].astype(bfloat)
            final_shared(index).start()

        @pl.when(otherwise(shared))
        def _():
            out_ref[index, pl.ds(2 * c + x, 1)] = part_ref[pl.ds(x, 1)].astype(bfloat)
            final_split(index).start()

    def stage_f(step):
        index = mats - 1 - step
        shared = shared_reduce(index, z)

        @pl.when(shared)
        def _():
            final_shared(index).wait_recv()
            total = f_buf[index, 0].astype(single) + f_buf[index, 1].astype(single)
            out_ref[index, pl.ds(2 * c, 2)] = total.astype(bfloat)

        @pl.when(otherwise(shared))
        def _():
            final_split(index).wait_recv()

        final_c(index).start()
        values = out_ref[index, pl.ds(2 * c, 2)].astype(single)
        sum_ref[...] += jnp.sum((values * values).reshape(-1, 8, width), axis=0)

    def reduce_tick(step):
        for lag, stage in zip(REDUCE, (stage_c, stage_x, stage_y, stage_r)):
            unit = step - lag
            pl.when(jnp.logical_and(unit >= 0, unit < units))(functools.partial(stage, unit))
        for lag, stage in zip(REDUCE[4:], (stage_z, stage_f)):
            turn = step - lag
            whole = lax.div(turn, z_count)
            pl.when(jnp.logical_and(jnp.logical_and(turn >= 0, turn < units), turn == whole * z_count + z_count - 1))(
                functools.partial(stage, whole)
            )

    def spread_ticks(first, count, turn, turns):
        each = -(-count // turns)

        def one(step):
            mine = turn * each + step
            pl.when(mine < count)(lambda: reduce_tick(first + mine))

        loop(0, each, one)

    def small_step(stage):
        if stage == 0:
            remote(small_ref, s_c, s_ss.at[0], s_rs.at[0], c_side).start()
        elif stage == 1:
            remote(small_ref, s_c, s_ss.at[0], s_rs.at[0], c_side).wait_recv()
            s_cur[0] = small_ref[...] + s_c[...]
            remote(s_cur.at[0], s_x, s_ss.at[1], s_rs.at[1], x_side).start()
        elif stage == 2:
            remote(s_cur.at[0], s_x, s_ss.at[1], s_rs.at[1], x_side).wait_recv()
            s_cur[1] = s_cur[0] + s_x[...]
            remote(s_cur.at[1], s_y, s_ss.at[2], s_rs.at[2], y_side).start()
        elif stage == 3:
            remote(s_cur.at[1], s_y, s_ss.at[2], s_rs.at[2], y_side).wait_recv()
            s_z[z] = s_cur[1] + s_y[...]

            def send(step, carry):
                other = lax.rem(z + step, z_count)
                remote(s_z.at[z], s_z.at[z], s_ss.at[3 + other], s_rs.at[3 + z], device(other, y, x, c)).start()
                return carry

            lax.fori_loop(1, z_count, send, 0)
        else:

            def wait(step, carry):
                other = lax.rem(z + step, z_count)
                remote(s_z.at[other], s_z.at[other], s_ss.at[3 + other], s_rs.at[3 + other], device(other, y, x, c)).wait_recv()
                return carry

            lax.fori_loop(1, z_count, wait, 0)

            def gather(step, carry):
                return carry + s_z[step]

            total_ref[...] = lax.fori_loop(0, z_count, gather, jnp.zeros(total_ref.shape, single))


    for first in range(AHEAD):
        own(matrix_at(first))
    for copy in inputs:
        copy.wait()
    sum_ref[...] = jnp.zeros_like(sum_ref)

    def upright(row):
        down = lax.broadcasted_iota(jnp.int32, (entries, entries), 0)
        along = lax.broadcasted_iota(jnp.int32, (entries, entries), 1)
        return jnp.sum(jnp.where(down == along, row, 0.0), axis=1, keepdims=True)

    def half_of(values, part):
        return values[part * group : (part + 1) * group]

    def spread_slots(values):
        return jnp.concatenate([half_of(values, part) for part in range(2) for _ in range(SLOTS)], axis=0)

    def sum_slots(values):
        sums = []
        for part in range(2):
            total = values[part * half : part * half + group]
            for slot in range(1, SLOTS):
                at = part * half + slot * group
                total = total + values[at : at + group]
            sums.append(total)
        return jnp.concatenate(sums, axis=0)

    tags_row = tags_ref[...].astype(single)
    counts_col = upright(counts_ref[...].astype(single))
    group_col = lax.broadcasted_iota(jnp.int32, (entries, groups), 1).astype(single)
    onehot = (group_col == upright(tags_row)).astype(single)
    table_rows = lax.dot_general(
        onehot, table_ref[...], (((1,), (0,)), ((), ())), precision=highest, preferred_element_type=single
    )
    for part in range(2):
        mine = half_of(table_rows, part)
        for slot in range(SLOTS):
            at = part * half + slot * group
            if slot < PIECES:
                x_ref[at : at + group, :] = mine + pieces_ref[slot, part * group : (part + 1) * group, :].astype(single)
            else:
                x_ref[at : at + group, :] = mine

    row_at = lax.broadcasted_iota(jnp.int32, (half, 2 * half), 0)
    key_at = lax.rem(lax.broadcasted_iota(jnp.int32, (half, 2 * half), 1), half)
    same = lax.rem(row_at, group) == lax.rem(key_at, group)
    key_slot = lax.div(key_at, group).astype(single)
    low_lane = lax.broadcasted_iota(jnp.int32, (half, 128), 1) < HD

    def key_mask(part):
        counts_here = jnp.concatenate([half_of(counts_col, part)] * SLOTS, axis=0)
        return jnp.logical_and(same, key_slot < counts_here)

    def split_pair(values):
        zero = jnp.zeros_like(values)
        return jnp.concatenate([jnp.where(low_lane, values, zero), jnp.where(low_lane, zero, values)], axis=0)

    def gain_at(norm):
        return gain_ref[pl.ds(norm, 1), :]

    def bias_at(norm):
        return bias_ref[pl.ds(norm, 1), :]

    def front(layer):
        values = x_ref[...]
        unit, scale = normalize(values)
        unit_ref[2 * layer] = unit
        scale_ref[2 * layer] = scale
        a = (unit * gain_at(2 * layer) + bias_at(2 * layer)).astype(bfloat)
        a_ref[layer] = a
        for part in range(3):
            qkv_ref[layer, part] = dot_nn(a, block_of(3 * layer, part)).astype(bfloat)
        for part in range(2):
            mask = key_mask(part)
            here = slice(part * half, (part + 1) * half)
            for pair in range(pairs):
                lanes = slice(pair * 128, (pair + 1) * 128)
                q = qkv_ref[layer, 0, here, lanes]
                keys = split_pair(qkv_ref[layer, 1, here, lanes])
                vals = split_pair(qkv_ref[layer, 2, here, lanes])
                scores = dot_nt(q, keys) * HD ** (-0.5)
                scores = jnp.where(mask, scores, masked_score)
                probs = []
                for head in range(2):
                    mine = scores[:, head * half : (head + 1) * half]
                    top = jnp.max(mine, axis=-1, keepdims=True)
                    raised = jnp.exp(mine - top)
                    probs.append(raised / jnp.sum(raised, axis=-1, keepdims=True))
                prob = jnp.concatenate(probs, axis=1)
                prob_ref[layer, part * pairs + pair] = prob
                o_ref[layer, here, lanes] = dot_nn(prob.astype(bfloat), vals).astype(bfloat)
        middle = values + dot_nt(o_ref[layer], block_of(3 * layer, 3))
        unit, scale = normalize(middle)
        unit_ref[2 * layer + 1] = unit
        scale_ref[2 * layer + 1] = scale
        b_ref[layer] = (unit * gain_at(2 * layer + 1) + bias_at(2 * layer + 1)).astype(bfloat)
        x_ref[...] = middle

    def rise(layer):
        def hidden(block, carry):
            u = dot_nn(b_ref[layer], block_of(3 * layer + 1, block))
            gate = 0.5 * (1.0 + lax.erf(u * math.sqrt(0.5)))
            g_ref[layer, block] = (u * gate).astype(bfloat)
            slope_ref[layer, block] = gate + u * (jnp.exp(-0.5 * u * u) * (1.0 / math.sqrt(2.0 * math.pi)))
            return carry

        lax.fori_loop(0, BLOCKS, hidden, 0)

    def fall(layer):
        def hidden(block, carry):
            x_ref[...] += dot_nt(g_ref[layer, block], block_of(3 * layer + 2, block))
            return carry

        lax.fori_loop(0, BLOCKS, hidden, 0)

    def project():
        total = jnp.zeros((entries, width), single)
        for block in range(BLOCKS):
            total += dot_nt(cot_ref[:, block * width : (block + 1) * width], block_of(proj, block))
        dpool_ref[...] = total

    depth = LAGS[-1]

    def gather_tick(step, carry):
        @pl.when(step + AHEAD < mats)
        def _():
            own(matrix_at(step + AHEAD))

        for lag, stage in zip((0, *LAGS), (line, beside, opposite, finish)):
            turn = step - lag
            pl.when(jnp.logical_and(turn >= 0, turn < mats))(lambda: stage(matrix_at(turn)))
        index = matrix_at(step - depth)
        layer = lax.div(index, 3)
        ready = jnp.logical_and(step >= depth, index < proj)
        for kind, work in enumerate((front, rise, fall)):
            pl.when(jnp.logical_and(ready, lax.rem(index, 3) == kind))(lambda: work(layer))
        pl.when(jnp.logical_and(step >= depth, index == proj))(project)
        return carry

    lax.fori_loop(0, mats + depth, gather_tick, 0)


    unit, scale = normalize(x_ref[...])
    normed = unit * gain_at(final) + bias_at(final)
    slot_col = lax.div(lax.rem(lax.broadcasted_iota(jnp.int32, (rows, 1), 0), half), group).astype(single)
    used_col = (slot_col < spread_slots(counts_col)).astype(single)
    pooled_low = (sum_slots(normed * used_col) / counts_col).astype(bfloat)
    for block in range(BLOCKS):
        lanes = slice(block * width, (block + 1) * width)
        emb_ref[:, lanes] = dot_nn(pooled_low, block_of(proj, block))
        put_grad(proj, block, dot_tn(pooled_low, cot_ref[:, lanes]))
    lax.fori_loop(0, mats, lambda index, carry: (gather_sent(index), carry)[1], 0)
    start_matrix(proj)
    give_credit(proj, (1, 2))
    emb_out = pltpu.make_async_copy(emb_ref, emb_hbm, store_sem.at[0])
    emb_out.start()
    grad_normed = spread_slots(dpool_ref[...] / counts_col) * used_col
    small_ref[...] = jnp.zeros_like(small_ref)
    small_ref[pl.ds(final, 1), :] = jnp.sum(grad_normed * unit, axis=0, keepdims=True)
    small_ref[pl.ds(SLOTS + final, 1), :] = jnp.sum(grad_normed, axis=0, keepdims=True)
    acc_ref[...] = normalize_back(grad_normed, unit, scale, gain_at(final))

    def backward(step, carry):
        layer = layers - 1 - step
        tick = 3 * z_count * step
        grad_next = acc_ref[...]
        do_ref[...] = grad_next.astype(bfloat)
        turn_ref[0] = grad_next.T.astype(bfloat)
        turn_ref[1] = b_ref[layer].astype(single).T.astype(bfloat)
        x_ref[...] = jnp.zeros_like(x_ref)

        def hidden(turn, carry):
            block = lax.rem(turn + 2 * (1 - c), BLOCKS)
            put_grad(3 * layer + 2, block, dot_nn(turn_ref[0], g_ref[layer, block]))
            grad_act = dot_nn(do_ref[...], block_of(3 * layer + 2, block))
            du = (grad_act * slope_ref[layer, block]).astype(bfloat)
            put_grad(3 * layer + 1, block, dot_nn(turn_ref[1], du))
            x_ref[...] += dot_nt(du, block_of(3 * layer + 1, block))

            @pl.when(turn == 1)
            def _():
                start_matrix(3 * layer + 2)
                start_matrix(3 * layer + 1)

            spread_ticks(tick - SHIFT, z_count, turn, BLOCKS)
            return carry

        lax.fori_loop(0, BLOCKS, hidden, 0)
        give_credit(3 * layer + 2, (1, 2))
        give_credit(3 * layer + 1, (1, 2))
        grad_b = x_ref[...]
        unit = unit_ref[2 * layer + 1]
        small_ref[pl.ds(2 * layer + 1, 1), :] = jnp.sum(grad_b * unit, axis=0, keepdims=True)
        small_ref[pl.ds(SLOTS + 2 * layer + 1, 1), :] = jnp.sum(grad_b, axis=0, keepdims=True)
        grad_middle = grad_next + normalize_back(grad_b, unit, scale_ref[2 * layer + 1], gain_at(2 * layer + 1))
        acc_ref[...] = grad_middle
        dy = grad_middle.astype(bfloat)
        put_grad(3 * layer, 3, dot_nn(grad_middle.T.astype(bfloat), o_ref[layer]))
        do_ref[...] = dot_nn(dy, block_of(3 * layer, 3)).astype(bfloat)

        def attend(pair, carry):
            lanes = pl.ds(pl.multiple_of(pair * 128, 128), 128)
            for part in range(2):
                here = slice(part * half, (part + 1) * half)
                q = qkv_ref[layer, 0, here, lanes]
                keys = split_pair(qkv_ref[layer, 1, here, lanes])
                vals = split_pair(qkv_ref[layer, 2, here, lanes])
                do = do_ref[here, lanes]
                prob = prob_ref[layer, part * pairs + pair]
                grad_prob = dot_nt(do, vals)
                product = grad_prob * prob
                scored = []
                for head in range(2):
                    spans = slice(head * half, (head + 1) * half)
                    total = jnp.sum(product[:, spans], axis=-1, keepdims=True)
                    scored.append(product[:, spans] - prob[:, spans] * total)
                ds_low = jnp.concatenate(scored, axis=1).astype(bfloat)
                dv = dot_tn(prob.astype(bfloat), do)
                dk = dot_tn(ds_low, q)
                dq = dot_nn(ds_low, keys)
                dqkv_ref[0, here, lanes] = (dq * HD ** (-0.5)).astype(bfloat)
                dqkv_ref[1, here, lanes] = (jnp.where(low_lane, dk[:half], dk[half:]) * HD ** (-0.5)).astype(bfloat)
                dqkv_ref[2, here, lanes] = jnp.where(low_lane, dv[:half], dv[half:]).astype(bfloat)
            spread_ticks(tick + z_count - SHIFT, 2 * z_count, pair, pairs)
            return carry

        lax.fori_loop(0, pairs, attend, 0)
        turned = a_ref[layer].astype(single).T.astype(bfloat)
        grad_a = jnp.zeros((rows, width), single)
        for part in range(3):
            put_grad(3 * layer, part, dot_nn(turned, dqkv_ref[part]))
            grad_a += dot_nt(dqkv_ref[part], block_of(3 * layer, part))
        start_matrix(3 * layer)
        give_credit(3 * layer, (1, 2))
        unit = unit_ref[2 * layer]
        small_ref[pl.ds(2 * layer, 1), :] = jnp.sum(grad_a * unit, axis=0, keepdims=True)
        small_ref[pl.ds(SLOTS + 2 * layer, 1), :] = jnp.sum(grad_a, axis=0, keepdims=True)
        acc_ref[...] += normalize_back(grad_a, unit, scale_ref[2 * layer], gain_at(2 * layer))
        return carry

    lax.fori_loop(0, layers, backward, 0)
    group_row = lax.broadcasted_iota(jnp.int32, (groups, entries), 0).astype(single)
    spread = (group_row == tags_row).astype(single)
    small_ref[2 * SLOTS : 2 * SLOTS + groups, :] = lax.dot_general(
        spread, sum_slots(acc_ref[...]), (((1,), (0,)), ((), ())), precision=highest, preferred_element_type=single
    )
    small_step(0)
    for part in range(2):
        for slot in range(PIECES):
            at = part * half + slot * group
            dx_ref[slot, part * group : (part + 1) * group, :] = acc_ref[at : at + group, :]
    dx_out = pltpu.make_async_copy(dx_ref, dx_hbm, store_sem.at[1])
    dx_out.start()

    def tail_tick(step, carry):
        reduce_tick(step)
        return carry

    first, end = units - z_count - SHIFT, units + REDUCE[-1]
    marks = [first, *(min(first + mark, end) for mark in MARKS), end]
    for stage in range(4):
        lax.fori_loop(marks[stage], marks[stage + 1], tail_tick, 0)
        small_step(stage + 1)
    lax.fori_loop(marks[4], marks[5], tail_tick, 0)

    place_here = me * 2 + c
    n_buf[place_here] = functools.reduce(jnp.add, [sum_ref[:, at * 128 : (at + 1) * 128] for at in range(width // 128)])

    def send_norm(step):
        other = lax.rem(place_here + step, 2 * dp)
        return remote(
            n_buf.at[place_here], n_buf.at[place_here], n_ss.at[other], n_rs.at[place_here],
            (lax.div(other, 2), x * 2 + lax.rem(other, 2)),
        )

    def take_norm(step):
        other = lax.rem(place_here + step, 2 * dp)
        await_arrival(n_buf.at[other], n_ss.at[other], n_rs.at[other], (lax.div(other, 2), x * 2 + lax.rem(other, 2)))

    def arrive(index):
        pair = out_ref.at[index, pl.ds(2 * (1 - c), 2)]
        await_arrival(pair, fc_ss.at[index], fc_rs.at[index], c_side)

    def many(low, high, body):
        lax.fori_loop(low, high, lambda step, carry: (body(step), carry)[1], 0)

    many(1, 2 * dp, lambda step: send_norm(step).start())
    many(0, mats, arrive)
    many(1, 2 * dp, take_norm)

    def sum_norm(step, carry):
        return carry + n_buf[step]

    spread = lax.fori_loop(0, 2 * dp, sum_norm, jnp.zeros(n_buf.shape[1:], single))
    smalls = total_ref[...]
    norm_ref[...] = jnp.broadcast_to(
        jnp.sum(jnp.sum(spread, axis=0, keepdims=True), axis=1, keepdims=True)
        + jnp.sum(jnp.sum(smalls * smalls, axis=0, keepdims=True), axis=1, keepdims=True),
        norm_ref.shape,
    )

    def done_unit(unit, carry):
        index, target = order(unit)
        to_c(index, target).wait_send()
        shared = shared_reduce(index, target)
        when(otherwise(shared), lambda: to_x(index, target).wait_send())

        def make(span):
            to_y(index, target, span).wait_send()
            pl.when(target != z)(lambda: to_z(index, target, span).wait_send())

        both(shared, make)
        return carry

    lax.fori_loop(0, units, done_unit, 0)

    def done_mat(index, carry):
        shared = shared_reduce(index, z)
        when(shared, lambda: final_shared(index).wait_send())
        when(otherwise(shared), lambda: final_split(index).wait_send())
        final_c(index).wait_send()
        return carry

    lax.fori_loop(0, mats, done_mat, 0)
    remote(small_ref, s_c, s_ss.at[0], s_rs.at[0], c_side).wait_send()
    remote(s_cur.at[0], s_x, s_ss.at[1], s_rs.at[1], x_side).wait_send()
    remote(s_cur.at[1], s_y, s_ss.at[2], s_rs.at[2], y_side).wait_send()

    def done_z(step, carry):
        other = lax.rem(z + step, z_count)
        remote(s_z.at[z], s_z.at[z], s_ss.at[3 + other], s_rs.at[3 + z], device(other, y, x, c)).wait_send()
        return carry

    lax.fori_loop(1, z_count, done_z, 0)

    many(1, 2 * dp, lambda step: send_norm(step).wait_send())
    emb_out.wait()
    dx_out.wait()


def train_step(pieces, tags, counts, cotangent, weights, gain, bias, table, layers, dp):
    _, entries, width = pieces.shape
    shard_rows = weights[0].shape[2]
    mats = 3 * layers + 1
    rows = entries * SLOTS
    pairs = width // 128
    z_count = dp // 2
    small = (SMALL_ROWS, width)
    vmem = pl.BlockSpec(memory_space=VMEM)
    where_it_is = pl.BlockSpec(memory_space=pltpu.HBM)
    dma = pltpu.SemaphoreType.DMA
    whole = (mats, BLOCKS, z_count, 2, shard_rows, width)
    return pl.pallas_call(
        functools.partial(step_kernel, layers, z_count),
        out_shape=(
            jax.ShapeDtypeStruct(cotangent.shape, single),
            jax.ShapeDtypeStruct(pieces.shape, single),
            jax.ShapeDtypeStruct((mats, BLOCKS, shard_rows, width), bfloat),
            jax.ShapeDtypeStruct(small, single),
            jax.ShapeDtypeStruct((8, 128), single),
        ),
        in_specs=[where_it_is] * 12,
        out_specs=(where_it_is, where_it_is, vmem, vmem, vmem),
        scratch_shapes=[
            VMEM(pieces.shape, bfloat),
            VMEM(tags.shape, jnp.int32),
            VMEM(counts.shape, jnp.int32),
            VMEM(cotangent.shape, bfloat),
            VMEM(gain.shape, single),
            VMEM(bias.shape, single),
            VMEM(table.shape, single),
            VMEM(cotangent.shape, single),
            VMEM(pieces.shape, single),
            VMEM((8, width), single),
            VMEM(whole, bfloat),
            VMEM(whole, bfloat),
            VMEM((mats, 2, z_count, shard_rows, width), bfloat),
            VMEM((mats, 2, 2, shard_rows, width), bfloat),
            VMEM((2, shard_rows, width), single),
            VMEM((rows, width), single),
            VMEM((2 * layers, rows, width), single),
            VMEM((2 * layers, rows, 1), single),
            VMEM((layers, rows, width), bfloat),
            VMEM((layers, rows, width), bfloat),
            VMEM((layers, 3, rows, width), bfloat),
            VMEM((layers, 2 * pairs, rows // 2, rows), single),
            VMEM((layers, rows, width), bfloat),
            VMEM((layers, BLOCKS, rows, width), bfloat),
            VMEM((layers, BLOCKS, rows, width), single),
            VMEM((3, rows, width), bfloat),
            VMEM((rows, width), bfloat),
            VMEM((rows, width), single),
            VMEM((2, width, rows), bfloat),
            VMEM((entries, width), single),
            VMEM(small, single),
            VMEM(small, single),
            VMEM(small, single),
            VMEM(small, single),
            VMEM((z_count, *small), single),
            VMEM((2, *small), single),
            VMEM((2 * dp, 8, 128), single),
            dma((mats, z_count, 2)),
            dma((mats,)),
            dma((mats, 2, z_count, 2)),
            dma((mats,)),
            *[dma((mats, z_count))] * 8,
            *[dma((mats,))] * 4,
            dma((3 + z_count,)),
            dma((3 + z_count,)),
            dma((2 * dp,)),
            dma((2 * dp,)),
            pltpu.SemaphoreType.REGULAR((3, mats)),
            dma((7,)),
            dma((mats, 2)),
            dma((2,)),
        ],
        compiler_params=pltpu.CompilerParams(collective_id=1, has_side_effects=True, vmem_limit_bytes=60 * 2**20),
        name="train_step",
    )(pieces, tags, counts, cotangent, *weights, gain, bias, table)


def update_kernel(layers, norms, *refs):
    norm_ref, grad_ref, small_ref, emb_in, dx_in = refs[:5]
    state_in, (emb_out, dx_out, root_ref), state_out = refs[5:29], refs[29:32], refs[32:56]
    held, (emb_ref, dx_ref, load_sem, store_sem, pass_sem) = refs[56:80], refs[80:]
    passing = [pltpu.make_async_copy(emb_in, emb_ref, pass_sem.at[0]), pltpu.make_async_copy(dx_in, dx_ref, pass_sem.at[1])]
    passed = [pltpu.make_async_copy(emb_ref, emb_out, pass_sem.at[2]), pltpu.make_async_copy(dx_ref, dx_out, pass_sem.at[3])]
    loads = [pltpu.make_async_copy(state_in[at], held[at], load_sem.at[at]) for at in range(24)]
    stores = [pltpu.make_async_copy(held[at], state_out[at], store_sem.at[at]) for at in range(24)]
    for copy in loads + passing:
        copy.start()
    root = jnp.sqrt(norm_ref[0:1, 0:1])
    root_ref[...] = root
    clip_scale = jnp.minimum(1.0, clip_level / (root + 1e-06))
    width = grad_ref.shape[3]
    proj = 3 * layers

    def piece(base, at, gradient, decay, rate):
        weight, first, second = (held[3 * base + kind] for kind in range(3))
        new = adam_update(weight[at], first[at], second[at], gradient.astype(single), clip_scale, decay, rate)
        weight[at], first[at], second[at] = new

    def group(base, work):
        for copy in loads[3 * base : 3 * base + 3]:
            copy.wait()
        work()
        for copy in stores[3 * base : 3 * base + 3]:
            copy.start()

    def each_layer(body):
        def wrapped(layer, carry):
            body(layer)
            return carry

        return lambda: lax.fori_loop(0, layers, wrapped, 0)

    def lanes(block):
        return slice(block * width, (block + 1) * width)

    def front(layer):
        for part in range(3):
            piece(0, (layer, part), grad_ref[3 * layer, part], decay_rate, learn_rate)

    def outward(layer):
        piece(1, (layer,), grad_ref[3 * layer, 3], decay_rate, learn_rate)

    def rise(layer):
        for block in range(BLOCKS):
            piece(2, (layer, slice(None), lanes(block)), grad_ref[3 * layer + 1, block], decay_rate, learn_rate)

    def fall(layer):
        for block in range(BLOCKS):
            piece(3, (layer, slice(None), lanes(block)), grad_ref[3 * layer + 2, block], decay_rate, learn_rate)

    def project():
        for block in range(BLOCKS):
            piece(4, (slice(None), lanes(block)), grad_ref[proj, block], decay_rate, learn_rate)

    group(0, each_layer(front))
    group(1, each_layer(outward))
    for arrived, copy in zip(passing, passed):
        arrived.wait()
        copy.start()
    group(2, each_layer(rise))
    group(3, each_layer(fall))
    group(4, project)
    whole = (slice(None), slice(None))
    group(5, lambda: piece(5, whole, small_ref[:norms], 0.0, small_rate))
    group(6, lambda: piece(6, whole, small_ref[SLOTS : SLOTS + norms], 0.0, small_rate))
    group(7, lambda: piece(7, whole, small_ref[2 * SLOTS : 2 * SLOTS + held[21].shape[0]], 0.0, small_rate))
    for copy in stores + passed:
        copy.wait()


def update(square_total, reduced, small_total, embeddings, input_grad, state, layers, norms):
    vmem = pl.BlockSpec(memory_space=VMEM)
    where_it_is = pl.BlockSpec(memory_space=pltpu.HBM)
    dma = pltpu.SemaphoreType.DMA
    like = lambda array: jax.ShapeDtypeStruct(array.shape, single)
    return pl.pallas_call(
        functools.partial(update_kernel, layers, norms),
        out_shape=(like(embeddings), like(input_grad), jax.ShapeDtypeStruct((1, 1), single), *map(like, state)),
        in_specs=[vmem] * 3 + [where_it_is] * 26,
        out_specs=(where_it_is, where_it_is, vmem) + (where_it_is,) * 24,
        scratch_shapes=[*[VMEM(array.shape, single) for array in (*state, embeddings, input_grad)], dma((24,)), dma((24,)), dma((4,))],
        compiler_params=pltpu.CompilerParams(vmem_limit_bytes=60 * 2**20),
        name="update",
    )(square_total, reduced, small_total, embeddings, input_grad, *state)


def adam_update(weight, first, second, gradient, clip_scale, decay, step_rate):
    clipped = gradient * clip_scale
    first_new = beta_first * first + (1.0 - beta_first) * clipped
    second_new = beta_second * second + (1.0 - beta_second) * clipped * clipped
    first_hat = first_new / (1.0 - beta_first**STEP)
    second_hat = second_new / (1.0 - beta_second**STEP)
    weight_new = weight - step_rate * (first_hat / (jnp.sqrt(second_hat) + adam_eps) + decay * weight)
    return (weight_new, first_new, second_new)


def per_device(
    pieces, script_tags, counts, cotangent,
    qkv_weight, qkv_first, qkv_second,
    out_weight, out_first, out_second,
    up_weight, up_first, up_second,
    down_weight, down_first, down_second,
    proj_weight, proj_first, proj_second,
    norm_gain, gain_first, gain_second,
    norm_bias, bias_first, bias_second,
    group_table, table_first, table_second,
):
    layers = qkv_weight.shape[0]
    dp = lax.axis_size("dp")
    norms = norm_gain.shape[0]

    def turn(array):
        return jnp.swapaxes(array, 1, 2)

    state = (
        qkv_weight, qkv_first, qkv_second,
        turn(out_weight), turn(out_first), turn(out_second),
        up_weight, up_first, up_second,
        turn(down_weight), turn(down_first), turn(down_second),
        proj_weight, proj_first, proj_second,
        norm_gain, gain_first, gain_second,
        norm_bias, bias_first, bias_second,
        group_table, table_first, table_second,
    )
    embeddings, input_grad, reduced, small_total, square_total = train_step(
        jnp.swapaxes(pieces, 0, 1), script_tags.reshape(1, -1), counts.reshape(1, -1), cotangent, state[0:15:3],
        norm_gain, norm_bias, group_table, layers, dp,
    )
    embeddings, input_grad, grad_norm, *state = update(
        square_total, reduced, small_total, embeddings, input_grad, state, layers, norms
    )
    state[3:6] = map(turn, state[3:6])
    state[9:12] = map(turn, state[9:12])
    return (embeddings, jnp.swapaxes(input_grad, 0, 1), grad_norm.reshape(()), *state)


def solution(mesh):
    entry_split = ("dp", "mp")
    weight_specs = (P(None, None, "dp", None), P(None, None, "dp"), P(None, "dp", None), P(None, None, "dp"), P("dp", None))
    state = tuple(spec for spec in weight_specs for _ in range(3)) + (P(),) * 9
    return jax.shard_map(
        per_device,
        mesh=mesh,
        in_specs=(P(entry_split, None, None), P(entry_split), P(entry_split), P(entry_split, None)) + state,
        out_specs=(P(entry_split, None), P(entry_split, None, None), P()) + state,
        check_vma=False,
    )
```

```python
import functools
import math

import jax
import jax.numpy as jnp
from jax import lax
from jax.experimental import pallas as pl
from jax.experimental.pallas import tpu as pltpu
from jax.sharding import PartitionSpec as P

HD = 64
PIECES = 7
SLOTS = 8
STEP = 10
BLOCKS = 4
SMALL_ROWS = 32

norm_eps = 1e-05
beta_first = 0.9
beta_second = 0.999
adam_eps = 1e-08
learn_rate = 0.03
small_rate = 0.5
decay_rate = 0.01
clip_level = 1.0
masked_score = -1000000000.0
bfloat = jnp.bfloat16
single = jnp.float32
highest = lax.Precision.HIGHEST
MESH = pl.DeviceIdType.MESH
VMEM = pltpu.VMEM


def place():
    along, across = lax.axis_index("dp"), lax.axis_index("mp")
    return lax.div(along, 2), lax.rem(along, 2), lax.div(across, 2), lax.rem(across, 2)


def device(z, y, x, c):
    return (z * 2 + y, x * 2 + c)


def remote(src, dst, send_sem, recv_sem, target):
    return pltpu.make_async_remote_copy(
        src_ref=src, dst_ref=dst, send_sem=send_sem, recv_sem=recv_sem, device_id=target, device_id_type=MESH
    )


def await_arrival(dst, send_sem, recv_sem, target):
    remote(dst, dst, send_sem, recv_sem, target).wait_recv()


def greet(z_count):
    z, y, x, c = place()
    barrier = pltpu.get_barrier_semaphore()

    def signal(target):
        pl.semaphore_signal(barrier, inc=1, device_id=target, device_id_type=MESH)

    signal(device(z, y, 1 - x, c))
    signal(device(z, y, x, 1 - c))
    dp = 2 * z_count

    def one(step):
        other = lax.rem(z * 2 + y + step, dp)
        signal((other, x * 2 + c))
        signal((other, x * 2 + 1 - c))

    loop(1, dp, one)
    return lambda: pl.semaphore_wait(barrier, 2 * dp)


def when(condition, body):
    if isinstance(condition, bool):
        if condition:
            body()
    else:
        pl.when(condition)(body)


def otherwise(condition):
    return not condition if isinstance(condition, bool) else jnp.logical_not(condition)


def loop(low, high, body):
    if high - low <= 8:
        for step in range(low, high):
            body(step)
    else:

        def wrapped(step, carry):
            body(step)
            return carry

        lax.fori_loop(low, high, wrapped, 0)


def dot_nn(left_side, right_side):
    return lax.dot_general(left_side, right_side, (((1,), (0,)), ((), ())), preferred_element_type=single)


def dot_nt(left_side, right_side):
    return lax.dot_general(left_side, right_side, (((1,), (1,)), ((), ())), preferred_element_type=single)


def dot_tn(left_side, right_side):
    return lax.dot_general(left_side, right_side, (((0,), (0,)), ((), ())), preferred_element_type=single)


def normalize(values):
    centre = jnp.mean(values, axis=-1, keepdims=True)
    offset = values - centre
    spread = jnp.mean(offset * offset, axis=-1, keepdims=True)
    scale = lax.rsqrt(spread + norm_eps)
    return offset * scale, scale


def normalize_back(grad, unit, scale, gain_row):
    grad_unit = grad * gain_row
    first = jnp.mean(grad_unit, axis=-1, keepdims=True)
    second = jnp.mean(grad_unit * unit, axis=-1, keepdims=True)
    return scale * (grad_unit - first - unit * second)


def shared_gather(layers, index, zz):
    return jnp.logical_or(index == 3 * layers - 1, lax.rem(index * 4 + zz, 8) == 0)


def shared_reduce(index, target):
    return lax.rem(index + target, 2) == 1


AHEAD = 1
LAGS = (1, 2, 3)
REDUCE = (0, 3, 6, 8, 9, 11)
SHIFT = 0
MARKS = (3, 7, 10, 13)


def step_kernel(
    layers, z_count,
    pieces_hbm, tags_hbm, counts_hbm, cot_hbm, qkv_hbm, outward_hbm, rise_hbm, fall_hbm, proj_hbm, gain_hbm, bias_hbm, table_hbm,
    emb_hbm, dx_hbm, out_hbm, total_ref, norm_ref,
    out_ref,
    pieces_ref, tags_ref, counts_ref, cot_ref, gain_ref, bias_ref, table_ref, emb_ref, dx_ref, sum_ref,
    w_ref, grad_ref, z_buf, f_buf, part_ref,
    x_ref, unit_ref, scale_ref, a_ref, b_ref, qkv_ref, prob_ref, o_ref, g_ref, slope_ref, dqkv_ref, do_ref, acc_ref, turn_ref, dpool_ref,
    small_ref, s_c, s_x, s_y, s_z, s_cur, n_buf,
    gx_ss, gc_ss, g_rs, gc_rs,
    c_ss, c_rs, x_ss, x_rs, y_ss, y_rs, z_ss, z_rs, fx_ss, fx_rs, fc_ss, fc_rs, s_ss, s_rs, n_ss, n_rs, credit,
    in_sem, load_sem, store_sem, out_sem,
):
    mats = 3 * layers + 1
    proj = 3 * layers
    final = 2 * layers
    _, entries, width = pieces_ref.shape
    rows = entries * SLOTS
    half = rows // 2
    group = entries // 2
    groups = table_ref.shape[0]
    pairs = width // 128
    dp = 2 * z_count
    shard_rows = out_ref.shape[2]
    z, y, x, c = place()
    me = z * 2 + y
    y_side, x_side, c_side = device(z, 1 - y, x, c), device(z, y, 1 - x, c), device(z, y, x, 1 - c)
    all_here = greet(z_count)


    inputs = [
        pltpu.make_async_copy(src, dst, in_sem.at[at])
        for at, (src, dst) in enumerate(
            (
                (tags_hbm, tags_ref), (counts_hbm, counts_ref), (pieces_hbm, pieces_ref), (table_hbm, table_ref),
                (gain_hbm, gain_ref), (bias_hbm, bias_ref), (cot_hbm, cot_ref),
            )
        )
    ]

    def shard_slot(index, block):
        at = 2 * index + block
        return slope_ref.at[at % layers, at // layers % BLOCKS, pl.ds(at // (layers * BLOCKS) * shard_rows, shard_rows)]

    def load(index, block, src):
        return pltpu.make_async_copy(src, shard_slot(index, block), load_sem.at[index, block])

    def each_load(act):
        for first in range(mats):
            index = gather_order[first]
            layer, kind = divmod(index, 3)
            for block in range(2):
                if index == proj or kind:
                    source = proj_hbm if index == proj else (rise_hbm, fall_hbm)[kind - 1].at[layer]
                    act(index, block, load(index, block, source.at[:, pl.ds(pl.multiple_of((2 * c + block) * width, width), width)]))
                else:
                    choice = (qkv_hbm.at[layer, block], qkv_hbm.at[layer, 2] if block == 0 else outward_hbm.at[layer])
                    for core in range(2):
                        pl.when(c == core)(functools.partial(act, index, block, load(index, block, choice[core])))

    gather_order = [*range(3 * (layers - 1)), proj, *range(3 * (layers - 1), proj)]

    def place_block(index, block, copy):
        copy.wait()
        w_ref[index, 2 * c + block, z, y] = shard_slot(index, block)[...].astype(bfloat)

    each_load(lambda index, block, copy: copy.start())
    for copy in inputs:
        copy.start()
    each_load(place_block)
    all_here()


    def matrix_at(turn):
        early = 3 * (layers - 1)
        return jnp.where(turn < early, turn, jnp.where(turn == early, proj, turn - 1))

    def by_type(index, zz, body):
        shared = shared_gather(layers, index, zz)
        when(shared, lambda: body(pl.ds(2 * c, 2), False))
        when(otherwise(shared), lambda: body(pl.ds(2 * c + x, 1), True))

    def gather_z(index, other, span):
        return remote(
            w_ref.at[index, span, z, y], w_ref.at[index, span, z, y], z_ss.at[index, other], g_rs.at[index, 0, z, y], device(other, y, x, c)
        )

    def gather_y(index, zz, span):
        spot = w_ref.at[index, span, zz, y]
        return remote(spot, spot, y_ss.at[index, zz], g_rs.at[index, 0, zz, y], y_side)

    def gather_x(index, zz, yy, span):
        spot = w_ref.at[index, span, zz, yy]
        return remote(spot, spot, gx_ss.at[index, zz, yy], g_rs.at[index, 1, zz, yy], x_side)

    def gather_c(index):
        pair = w_ref.at[index, pl.ds(2 * c, 2)]
        return remote(pair, pair, gc_ss.at[index], gc_rs.at[index], c_side)

    def arrived(index, zz, yy, span):
        await_arrival(w_ref.at[index, span, zz, yy], y_ss.at[index, zz], g_rs.at[index, 0, zz, yy], y_side)

    def own(index):
        def send(span, cross):
            gather_y(index, z, span).start()

            def one(other):
                pl.when(other != z)(lambda: gather_z(index, other, span).start())

            loop(0, z_count, one)

        by_type(index, z, send)

    def line(index):
        def one(zz):
            def pass_on(span, cross):
                arrived(index, zz, y, span)
                if cross:
                    gather_x(index, zz, y, span).start()
                gather_y(index, zz, span).start()

            pl.when(z != zz)(lambda: by_type(index, zz, pass_on))

        loop(0, z_count, one)

    def beside(index):
        def one(zz):
            def pass_on(span, cross):
                arrived(index, zz, 1 - y, span)
                if cross:
                    gather_x(index, zz, 1 - y, span).start()

            by_type(index, zz, pass_on)

        loop(0, z_count, one)

    def opposite(index):
        def each(zz):
            def one(yy):
                block = w_ref.at[index, pl.ds(2 * c + 1 - x, 1), zz, yy]
                await_arrival(block, gx_ss.at[index, zz, yy], g_rs.at[index, 1, zz, yy], x_side)

            def two():
                pl.when(zz != z)(lambda: one(y))
                one(1 - y)

            when(otherwise(shared_gather(layers, index, zz)), two)

        loop(0, z_count, each)
        gather_c(index).start()

    def finish(index):
        pair = w_ref.at[index, pl.ds(2 * (1 - c), 2)]
        await_arrival(pair, gc_ss.at[index], gc_rs.at[index], c_side)

    def gather_sent(index):
        def each(zz):
            def done(span, cross):
                gather_y(index, zz, span).wait_send()
                if cross:
                    pl.when(zz != z)(lambda: gather_x(index, zz, y, span).wait_send())
                    gather_x(index, zz, 1 - y, span).wait_send()

                def one(other):
                    pl.when(other != z)(lambda: gather_z(index, other, span).wait_send())

                pl.when(zz == z)(lambda: loop(0, z_count, one))

            by_type(index, zz, done)

        loop(0, z_count, each)
        gather_c(index).wait_send()

    def block_of(index, block):
        return w_ref[index, block].reshape(width, width)

    def put_grad(index, block, values):
        grad_ref[index, block] = values.astype(bfloat).reshape(grad_ref.shape[2:])


    units = mats * z_count
    pair_c = pl.ds(2 * c, 2)

    def order(unit):
        return mats - 1 - lax.div(unit, z_count), lax.rem(unit, z_count)

    def local(span):
        return pl.ds(2 * c, 2) if span is None else pl.ds(2 * c + x, 1)

    def near(span):
        return pl.ds(0, 2) if span is None else pl.ds(x, 1)

    def to_c(index, target):
        return remote(
            grad_ref.at[index, pl.ds(2 * (1 - c), 2), target], w_ref.at[index, pl.ds(2 * c, 2), target],
            c_ss.at[index, target], c_rs.at[index, target], c_side,
        )

    def from_c(index, target):
        await_arrival(w_ref.at[index, pl.ds(2 * (1 - c), 2), target], c_ss.at[index, target], c_rs.at[index, target], c_side)

    def to_x(index, target):
        return remote(
            grad_ref.at[index, 2 * c + 1 - x, target], w_ref.at[index, 2 * c, target], x_ss.at[index, target], x_rs.at[index, target], x_side
        )

    def to_y(index, target, span):
        return remote(
            grad_ref.at[index, local(span), target, 1 - y], w_ref.at[index, 2 * c + 1, target, near(span)],
            y_ss.at[index, target], y_rs.at[index, target], y_side,
        )

    relays = z_count >= 4

    def at_far_end(target):
        return jnp.logical_and(relays, jnp.abs(target - z) == z_count - 1)

    def passes_on(target):
        up = jnp.logical_and(target == z_count - 1, z == 1)
        down = jnp.logical_and(target == 0, z == z_count - 2)
        return jnp.logical_and(relays, jnp.logical_or(up, down))

    def to_z(index, target, span):
        far = at_far_end(target)
        there = jnp.where(far, jnp.where(z == 0, 1, z_count - 2), target)
        slot = jnp.where(far, there, z)
        return remote(
            grad_ref.at[index, local(span), target, y], z_buf.at[index, near(span), slot],
            z_ss.at[index, target], z_rs.at[index, slot], device(there, y, x, c),
        )

    def from_z(index, source, span):
        other = jnp.where(source == z, jnp.where(z == 1, 0, z_count - 1), source)
        await_arrival(z_buf.at[index, near(span), source], z_ss.at[index, source], z_rs.at[index, source], device(other, y, x, c))

    def both(shared, body):
        when(shared, lambda: body(None))
        when(otherwise(shared), lambda: body(1))

    def add(ref, at, extra):
        ref[at] = (ref[at].astype(single) + extra.astype(single)).astype(bfloat)

    def give_credit(index, kinds):
        for kind in kinds:
            side = (c_side, x_side, y_side)[kind]
            pl.semaphore_signal(credit.at[kind, index], inc=1, device_id=side, device_id_type=MESH)

    def start_matrix(index):
        give_credit(index, (0,))
        pl.semaphore_wait(credit.at[0, index], 1)
        loop(0, z_count, lambda target: to_c(index, target).start())

    def stage_c(unit):
        index, target = order(unit)
        from_c(index, target)
        for block in range(2):
            add(grad_ref, (index, 2 * c + block, target), w_ref[index, 2 * (1 - c) + block, target])
        shared = shared_reduce(index, target)

        @pl.when(target == 0)
        def _():
            pl.semaphore_wait(credit.at[1, index], 1)
            pl.semaphore_wait(credit.at[2, index], 1)

        when(shared, lambda: to_y(index, target, None).start())
        when(otherwise(shared), lambda: to_x(index, target).start())

    def stage_x(unit):
        index, target = order(unit)

        @pl.when(otherwise(shared_reduce(index, target)))
        def _():
            to_x(index, target).wait_recv()
            add(grad_ref, (index, 2 * c + x, target), w_ref[index, 2 * c, target])
            to_y(index, target, 1).start()

    def stage_y(unit):
        index, target = order(unit)

        def make(span):
            to_y(index, target, span).wait_recv()
            add(grad_ref, (index, local(span), target, y), w_ref[index, 2 * c + 1, target, near(span)])
            pl.when(jnp.logical_and(target != z, jnp.logical_not(passes_on(target))))(lambda: to_z(index, target, span).start())

        both(shared_reduce(index, target), make)

    def stage_r(unit):
        index, target = order(unit)

        def make(span):
            from_z(index, z, span)
            add(grad_ref, (index, local(span), target, y), z_buf[index, near(span), z])
            to_z(index, target, span).start()

        pl.when(passes_on(target))(lambda: both(shared_reduce(index, target), make))

    def final_shared(index):
        return remote(f_buf.at[index, 0], f_buf.at[index, 1], fx_ss.at[index], fx_rs.at[index], x_side)

    def final_split(index):
        mine = out_ref.at[index, 2 * c + x]
        return remote(mine, mine, fx_ss.at[index], fx_rs.at[index], x_side)

    def final_c(index):
        pair = out_ref.at[index, pl.ds(2 * c, 2)]
        return remote(pair, pair, fc_ss.at[index], fc_rs.at[index], c_side)

    def stage_z(step):
        index = mats - 1 - step

        def make(span):
            def sends(source):
                far = jnp.logical_and(relays, jnp.abs(source - z) == z_count - 1)
                return jnp.logical_and(source != z, jnp.logical_not(far))

            def one(source):
                pl.when(sends(source))(lambda: from_z(index, source, span))

            loop(0, z_count, one)
            part_ref[near(span)] = grad_ref[index, local(span), z, y].astype(single)

            def more(source):
                @pl.when(sends(source))
                def _():
                    part_ref[near(span)] = part_ref[near(span)] + z_buf[index, near(span), source].astype(single)

            loop(0, z_count, more)

        shared = shared_reduce(index, z)
        both(shared, make)

        @pl.when(shared)
        def _():
            f_buf[index, 0] = part_ref[...].astype(bfloat)
            final_shared(index).start()

        @pl.when(otherwise(shared))
        def _():
            out_ref[index, pl.ds(2 * c + x, 1)] = part_ref[pl.ds(x, 1)].astype(bfloat)
            final_split(index).start()

    def stage_f(step):
        index = mats - 1 - step
        shared = shared_reduce(index, z)

        @pl.when(shared)
        def _():
            final_shared(index).wait_recv()
            total = f_buf[index, 0].astype(single) + f_buf[index, 1].astype(single)
            out_ref[index, pl.ds(2 * c, 2)] = total.astype(bfloat)

        @pl.when(otherwise(shared))
        def _():
            final_split(index).wait_recv()

        final_c(index).start()
        values = out_ref[index, pl.ds(2 * c, 2)].astype(single)
        sum_ref[...] += jnp.sum((values * values).reshape(-1, 8, width), axis=0)

    def reduce_tick(step):
        for lag, stage in zip(REDUCE, (stage_c, stage_x, stage_y, stage_r)):
            unit = step - lag
            pl.when(jnp.logical_and(unit >= 0, unit < units))(functools.partial(stage, unit))
        for lag, stage in zip(REDUCE[4:], (stage_z, stage_f)):
            turn = step - lag
            whole = lax.div(turn, z_count)
            pl.when(jnp.logical_and(jnp.logical_and(turn >= 0, turn < units), turn == whole * z_count + z_count - 1))(
                functools.partial(stage, whole)
            )

    def spread_ticks(first, count, turn, turns):
        each = -(-count // turns)

        def one(step):
            mine = turn * each + step
            pl.when(mine < count)(lambda: reduce_tick(first + mine))

        loop(0, each, one)

    def small_step(stage):
        if stage == 0:
            remote(small_ref, s_c, s_ss.at[0], s_rs.at[0], c_side).start()
        elif stage == 1:
            remote(small_ref, s_c, s_ss.at[0], s_rs.at[0], c_side).wait_recv()
            s_cur[0] = small_ref[...] + s_c[...]
            remote(s_cur.at[0], s_x, s_ss.at[1], s_rs.at[1], x_side).start()
        elif stage == 2:
            remote(s_cur.at[0], s_x, s_ss.at[1], s_rs.at[1], x_side).wait_recv()
            s_cur[1] = s_cur[0] + s_x[...]
            remote(s_cur.at[1], s_y, s_ss.at[2], s_rs.at[2], y_side).start()
        elif stage == 3:
            remote(s_cur.at[1], s_y, s_ss.at[2], s_rs.at[2], y_side).wait_recv()
            s_z[z] = s_cur[1] + s_y[...]

            def send(step, carry):
                other = lax.rem(z + step, z_count)
                remote(s_z.at[z], s_z.at[z], s_ss.at[3 + other], s_rs.at[3 + z], device(other, y, x, c)).start()
                return carry

            lax.fori_loop(1, z_count, send, 0)
        else:

            def wait(step, carry):
                other = lax.rem(z + step, z_count)
                remote(s_z.at[other], s_z.at[other], s_ss.at[3 + other], s_rs.at[3 + other], device(other, y, x, c)).wait_recv()
                return carry

            lax.fori_loop(1, z_count, wait, 0)

            def gather(step, carry):
                return carry + s_z[step]

            total_ref[...] = lax.fori_loop(0, z_count, gather, jnp.zeros(total_ref.shape, single))


    for first in range(AHEAD):
        own(matrix_at(first))
    for copy in inputs:
        copy.wait()
    sum_ref[...] = jnp.zeros_like(sum_ref)

    def upright(row):
        down = lax.broadcasted_iota(jnp.int32, (entries, entries), 0)
        along = lax.broadcasted_iota(jnp.int32, (entries, entries), 1)
        return jnp.sum(jnp.where(down == along, row, 0.0), axis=1, keepdims=True)

    def half_of(values, part):
        return values[part * group : (part + 1) * group]

    def spread_slots(values):
        return jnp.concatenate([half_of(values, part) for part in range(2) for _ in range(SLOTS)], axis=0)

    def sum_slots(values):
        sums = []
        for part in range(2):
            total = values[part * half : part * half + group]
            for slot in range(1, SLOTS):
                at = part * half + slot * group
                total = total + values[at : at + group]
            sums.append(total)
        return jnp.concatenate(sums, axis=0)

    tags_row = tags_ref[...].astype(single)
    counts_col = upright(counts_ref[...].astype(single))
    group_col = lax.broadcasted_iota(jnp.int32, (entries, groups), 1).astype(single)
    onehot = (group_col == upright(tags_row)).astype(single)
    table_rows = lax.dot_general(
        onehot, table_ref[...], (((1,), (0,)), ((), ())), precision=highest, preferred_element_type=single
    )
    for part in range(2):
        mine = half_of(table_rows, part)
        for slot in range(SLOTS):
            at = part * half + slot * group
            if slot < PIECES:
                x_ref[at : at + group, :] = mine + pieces_ref[slot, part * group : (part + 1) * group, :].astype(single)
            else:
                x_ref[at : at + group, :] = mine

    row_at = lax.broadcasted_iota(jnp.int32, (half, 2 * half), 0)
    key_at = lax.rem(lax.broadcasted_iota(jnp.int32, (half, 2 * half), 1), half)
    same = lax.rem(row_at, group) == lax.rem(key_at, group)
    key_slot = lax.div(key_at, group).astype(single)
    low_lane = lax.broadcasted_iota(jnp.int32, (half, 128), 1) < HD

    def key_mask(part):
        counts_here = jnp.concatenate([half_of(counts_col, part)] * SLOTS, axis=0)
        return jnp.logical_and(same, key_slot < counts_here)

    def split_pair(values):
        zero = jnp.zeros_like(values)
        return jnp.concatenate([jnp.where(low_lane, values, zero), jnp.where(low_lane, zero, values)], axis=0)

    def gain_at(norm):
        return gain_ref[pl.ds(norm, 1), :]

    def bias_at(norm):
        return bias_ref[pl.ds(norm, 1), :]

    def front(layer):
        values = x_ref[...]
        unit, scale = normalize(values)
        unit_ref[2 * layer] = unit
        scale_ref[2 * layer] = scale
        a = (unit * gain_at(2 * layer) + bias_at(2 * layer)).astype(bfloat)
        a_ref[layer] = a
        for part in range(3):
            qkv_ref[layer, part] = dot_nn(a, block_of(3 * layer, part)).astype(bfloat)
        for part in range(2):
            mask = key_mask(part)
            here = slice(part * half, (part + 1) * half)
            for pair in range(pairs):
                lanes = slice(pair * 128, (pair + 1) * 128)
                q = qkv_ref[layer, 0, here, lanes]
                keys = split_pair(qkv_ref[layer, 1, here, lanes])
                vals = split_pair(qkv_ref[layer, 2, here, lanes])
                scores = dot_nt(q, keys) * HD ** (-0.5)
                scores = jnp.where(mask, scores, masked_score)
                probs = []
                for head in range(2):
                    mine = scores[:, head * half : (head + 1) * half]
                    top = jnp.max(mine, axis=-1, keepdims=True)
                    raised = jnp.exp(mine - top)
                    probs.append(raised / jnp.sum(raised, axis=-1, keepdims=True))
                prob = jnp.concatenate(probs, axis=1)
                prob_ref[layer, part * pairs + pair] = prob
                o_ref[layer, here, lanes] = dot_nn(prob.astype(bfloat), vals).astype(bfloat)
        middle = values + dot_nt(o_ref[layer], block_of(3 * layer, 3))
        unit, scale = normalize(middle)
        unit_ref[2 * layer + 1] = unit
        scale_ref[2 * layer + 1] = scale
        b_ref[layer] = (unit * gain_at(2 * layer + 1) + bias_at(2 * layer + 1)).astype(bfloat)
        x_ref[...] = middle

    def rise(layer):
        def hidden(block, carry):
            u = dot_nn(b_ref[layer], block_of(3 * layer + 1, block))
            gate = 0.5 * (1.0 + lax.erf(u * math.sqrt(0.5)))
            g_ref[layer, block] = (u * gate).astype(bfloat)
            slope_ref[layer, block] = gate + u * (jnp.exp(-0.5 * u * u) * (1.0 / math.sqrt(2.0 * math.pi)))
            return carry

        lax.fori_loop(0, BLOCKS, hidden, 0)

    def fall(layer):
        def hidden(block, carry):
            x_ref[...] += dot_nt(g_ref[layer, block], block_of(3 * layer + 2, block))
            return carry

        lax.fori_loop(0, BLOCKS, hidden, 0)

    def project():
        total = jnp.zeros((entries, width), single)
        for block in range(BLOCKS):
            total += dot_nt(cot_ref[:, block * width : (block + 1) * width], block_of(proj, block))
        dpool_ref[...] = total

    depth = LAGS[-1]

    def gather_tick(step, carry):
        @pl.when(step + AHEAD < mats)
        def _():
            own(matrix_at(step + AHEAD))

        for lag, stage in zip((0, *LAGS), (line, beside, opposite, finish)):
            turn = step - lag
            pl.when(jnp.logical_and(turn >= 0, turn < mats))(lambda: stage(matrix_at(turn)))
        index = matrix_at(step - depth)
        layer = lax.div(index, 3)
        ready = jnp.logical_and(step >= depth, index < proj)
        for kind, work in enumerate((front, rise, fall)):
            pl.when(jnp.logical_and(ready, lax.rem(index, 3) == kind))(lambda: work(layer))
        pl.when(jnp.logical_and(step >= depth, index == proj))(project)
        return carry

    lax.fori_loop(0, mats + depth, gather_tick, 0)


    unit, scale = normalize(x_ref[...])
    normed = unit * gain_at(final) + bias_at(final)
    slot_col = lax.div(lax.rem(lax.broadcasted_iota(jnp.int32, (rows, 1), 0), half), group).astype(single)
    used_col = (slot_col < spread_slots(counts_col)).astype(single)
    pooled_low = (sum_slots(normed * used_col) / counts_col).astype(bfloat)
    for block in range(BLOCKS):
        lanes = slice(block * width, (block + 1) * width)
        emb_ref[:, lanes] = dot_nn(pooled_low, block_of(proj, block))
        put_grad(proj, block, dot_tn(pooled_low, cot_ref[:, lanes]))
    lax.fori_loop(0, mats, lambda index, carry: (gather_sent(index), carry)[1], 0)
    start_matrix(proj)
    give_credit(proj, (1, 2))
    emb_out = pltpu.make_async_copy(emb_ref, emb_hbm, store_sem.at[0])
    emb_out.start()
    grad_normed = spread_slots(dpool_ref[...] / counts_col) * used_col
    small_ref[...] = jnp.zeros_like(small_ref)
    small_ref[pl.ds(final, 1), :] = jnp.sum(grad_normed * unit, axis=0, keepdims=True)
    small_ref[pl.ds(SLOTS + final, 1), :] = jnp.sum(grad_normed, axis=0, keepdims=True)
    acc_ref[...] = normalize_back(grad_normed, unit, scale, gain_at(final))

    def backward(step, carry):
        layer = layers - 1 - step
        tick = 3 * z_count * step
        grad_next = acc_ref[...]
        do_ref[...] = grad_next.astype(bfloat)
        turn_ref[0] = grad_next.T.astype(bfloat)
        turn_ref[1] = b_ref[layer].astype(single).T.astype(bfloat)
        x_ref[...] = jnp.zeros_like(x_ref)

        def hidden(turn, carry):
            block = lax.rem(turn + 2 * (1 - c), BLOCKS)
            spread_ticks(tick - SHIFT, z_count, turn, BLOCKS)
            put_grad(3 * layer + 2, block, dot_nn(turn_ref[0], g_ref[layer, block]))
            grad_act = dot_nn(do_ref[...], block_of(3 * layer + 2, block))
            du = (grad_act * slope_ref[layer, block]).astype(bfloat)
            put_grad(3 * layer + 1, block, dot_nn(turn_ref[1], du))
            x_ref[...] += dot_nt(du, block_of(3 * layer + 1, block))

            @pl.when(turn == 1)
            def _():
                start_matrix(3 * layer + 2)
                start_matrix(3 * layer + 1)

            return carry

        lax.fori_loop(0, BLOCKS, hidden, 0)
        give_credit(3 * layer + 2, (1, 2))
        give_credit(3 * layer + 1, (1, 2))
        grad_b = x_ref[...]
        unit = unit_ref[2 * layer + 1]
        small_ref[pl.ds(2 * layer + 1, 1), :] = jnp.sum(grad_b * unit, axis=0, keepdims=True)
        small_ref[pl.ds(SLOTS + 2 * layer + 1, 1), :] = jnp.sum(grad_b, axis=0, keepdims=True)
        grad_middle = grad_next + normalize_back(grad_b, unit, scale_ref[2 * layer + 1], gain_at(2 * layer + 1))
        acc_ref[...] = grad_middle
        dy = grad_middle.astype(bfloat)
        put_grad(3 * layer, 3, dot_nn(grad_middle.T.astype(bfloat), o_ref[layer]))
        do_ref[...] = dot_nn(dy, block_of(3 * layer, 3)).astype(bfloat)

        def attend(pair, carry):
            lanes = pl.ds(pl.multiple_of(pair * 128, 128), 128)
            spread_ticks(tick + z_count - SHIFT, 2 * z_count, pair, pairs)
            for part in range(2):
                here = slice(part * half, (part + 1) * half)
                q = qkv_ref[layer, 0, here, lanes]
                keys = split_pair(qkv_ref[layer, 1, here, lanes])
                vals = split_pair(qkv_ref[layer, 2, here, lanes])
                do = do_ref[here, lanes]
                prob = prob_ref[layer, part * pairs + pair]
                grad_prob = dot_nt(do, vals)
                product = grad_prob * prob
                scored = []
                for head in range(2):
                    spans = slice(head * half, (head + 1) * half)
                    total = jnp.sum(product[:, spans], axis=-1, keepdims=True)
                    scored.append(product[:, spans] - prob[:, spans] * total)
                ds_low = jnp.concatenate(scored, axis=1).astype(bfloat)
                dv = dot_tn(prob.astype(bfloat), do)
                dk = dot_tn(ds_low, q)
                dq = dot_nn(ds_low, keys)
                dqkv_ref[0, here, lanes] = (dq * HD ** (-0.5)).astype(bfloat)
                dqkv_ref[1, here, lanes] = (jnp.where(low_lane, dk[:half], dk[half:]) * HD ** (-0.5)).astype(bfloat)
                dqkv_ref[2, here, lanes] = jnp.where(low_lane, dv[:half], dv[half:]).astype(bfloat)
            return carry

        lax.fori_loop(0, pairs, attend, 0)
        turned = a_ref[layer].astype(single).T.astype(bfloat)
        grad_a = jnp.zeros((rows, width), single)
        for part in range(3):
            put_grad(3 * layer, part, dot_nn(turned, dqkv_ref[part]))
            grad_a += dot_nt(dqkv_ref[part], block_of(3 * layer, part))
        start_matrix(3 * layer)
        give_credit(3 * layer, (1, 2))
        unit = unit_ref[2 * layer]
        small_ref[pl.ds(2 * layer, 1), :] = jnp.sum(grad_a * unit, axis=0, keepdims=True)
        small_ref[pl.ds(SLOTS + 2 * layer, 1), :] = jnp.sum(grad_a, axis=0, keepdims=True)
        acc_ref[...] += normalize_back(grad_a, unit, scale_ref[2 * layer], gain_at(2 * layer))
        return carry

    lax.fori_loop(0, layers, backward, 0)
    group_row = lax.broadcasted_iota(jnp.int32, (groups, entries), 0).astype(single)
    spread = (group_row == tags_row).astype(single)
    small_ref[2 * SLOTS : 2 * SLOTS + groups, :] = lax.dot_general(
        spread, sum_slots(acc_ref[...]), (((1,), (0,)), ((), ())), precision=highest, preferred_element_type=single
    )
    small_step(0)
    for part in range(2):
        for slot in range(PIECES):
            at = part * half + slot * group
            dx_ref[slot, part * group : (part + 1) * group, :] = acc_ref[at : at + group, :]
    dx_out = pltpu.make_async_copy(dx_ref, dx_hbm, store_sem.at[1])
    dx_out.start()

    def tail_tick(step, carry):
        reduce_tick(step)
        return carry

    first, end = units - z_count - SHIFT, units + REDUCE[-1]
    marks = [first, *(min(first + mark, end) for mark in MARKS), end]
    for stage in range(4):
        lax.fori_loop(marks[stage], marks[stage + 1], tail_tick, 0)
        small_step(stage + 1)
    lax.fori_loop(marks[4], marks[5], tail_tick, 0)

    place_here = me * 2 + c
    n_buf[place_here] = functools.reduce(jnp.add, [sum_ref[:, at * 128 : (at + 1) * 128] for at in range(width // 128)])

    def send_norm(step):
        other = lax.rem(place_here + step, 2 * dp)
        return remote(
            n_buf.at[place_here], n_buf.at[place_here], n_ss.at[other], n_rs.at[place_here],
            (lax.div(other, 2), x * 2 + lax.rem(other, 2)),
        )

    def take_norm(step):
        other = lax.rem(place_here + step, 2 * dp)
        await_arrival(n_buf.at[other], n_ss.at[other], n_rs.at[other], (lax.div(other, 2), x * 2 + lax.rem(other, 2)))

    def out_copy(index):
        return pltpu.make_async_copy(out_ref.at[index], out_hbm.at[index], out_sem.at[index])

    def arrive(index):
        pair = out_ref.at[index, pl.ds(2 * (1 - c), 2)]
        await_arrival(pair, fc_ss.at[index], fc_rs.at[index], c_side)
        out_copy(index).start()

    def many(low, high, body):
        lax.fori_loop(low, high, lambda step, carry: (body(step), carry)[1], 0)

    many(1, 2 * dp, lambda step: send_norm(step).start())
    many(0, mats, arrive)
    many(1, 2 * dp, take_norm)

    def sum_norm(step, carry):
        return carry + n_buf[step]

    spread = lax.fori_loop(0, 2 * dp, sum_norm, jnp.zeros(n_buf.shape[1:], single))
    smalls = total_ref[...]
    norm_ref[...] = jnp.broadcast_to(
        jnp.sum(jnp.sum(spread, axis=0, keepdims=True), axis=1, keepdims=True)
        + jnp.sum(jnp.sum(smalls * smalls, axis=0, keepdims=True), axis=1, keepdims=True),
        norm_ref.shape,
    )

    def done_unit(unit, carry):
        index, target = order(unit)
        to_c(index, target).wait_send()
        shared = shared_reduce(index, target)
        when(otherwise(shared), lambda: to_x(index, target).wait_send())

        def make(span):
            to_y(index, target, span).wait_send()
            pl.when(target != z)(lambda: to_z(index, target, span).wait_send())

        both(shared, make)
        return carry

    lax.fori_loop(0, units, done_unit, 0)

    def done_mat(index, carry):
        shared = shared_reduce(index, z)
        when(shared, lambda: final_shared(index).wait_send())
        when(otherwise(shared), lambda: final_split(index).wait_send())
        final_c(index).wait_send()
        return carry

    lax.fori_loop(0, mats, done_mat, 0)
    remote(small_ref, s_c, s_ss.at[0], s_rs.at[0], c_side).wait_send()
    remote(s_cur.at[0], s_x, s_ss.at[1], s_rs.at[1], x_side).wait_send()
    remote(s_cur.at[1], s_y, s_ss.at[2], s_rs.at[2], y_side).wait_send()

    def done_z(step, carry):
        other = lax.rem(z + step, z_count)
        remote(s_z.at[z], s_z.at[z], s_ss.at[3 + other], s_rs.at[3 + z], device(other, y, x, c)).wait_send()
        return carry

    lax.fori_loop(1, z_count, done_z, 0)

    many(1, 2 * dp, lambda step: send_norm(step).wait_send())
    emb_out.wait()
    dx_out.wait()
    many(0, mats, lambda index: out_copy(index).wait())


def train_step(pieces, tags, counts, cotangent, weights, gain, bias, table, layers, dp):
    _, entries, width = pieces.shape
    shard_rows = weights[0].shape[2]
    mats = 3 * layers + 1
    rows = entries * SLOTS
    pairs = width // 128
    z_count = dp // 2
    small = (SMALL_ROWS, width)
    vmem = pl.BlockSpec(memory_space=VMEM)
    where_it_is = pl.BlockSpec(memory_space=pltpu.HBM)
    dma = pltpu.SemaphoreType.DMA
    whole = (mats, BLOCKS, z_count, 2, shard_rows, width)
    return pl.pallas_call(
        functools.partial(step_kernel, layers, z_count),
        out_shape=(
            jax.ShapeDtypeStruct(cotangent.shape, single),
            jax.ShapeDtypeStruct(pieces.shape, single),
            jax.ShapeDtypeStruct((mats, BLOCKS, shard_rows, width), bfloat),
            jax.ShapeDtypeStruct(small, single),
            jax.ShapeDtypeStruct((8, 128), single),
        ),
        in_specs=[where_it_is] * 12,
        out_specs=(where_it_is, where_it_is, where_it_is, vmem, vmem),
        scratch_shapes=[
            VMEM((mats, BLOCKS, shard_rows, width), bfloat),
            VMEM(pieces.shape, bfloat),
            VMEM(tags.shape, jnp.int32),
            VMEM(counts.shape, jnp.int32),
            VMEM(cotangent.shape, bfloat),
            VMEM(gain.shape, single),
            VMEM(bias.shape, single),
            VMEM(table.shape, single),
            VMEM(cotangent.shape, single),
            VMEM(pieces.shape, single),
            VMEM((8, width), single),
            VMEM(whole, bfloat),
            VMEM(whole, bfloat),
            VMEM((mats, 2, z_count, shard_rows, width), bfloat),
            VMEM((mats, 2, 2, shard_rows, width), bfloat),
            VMEM((2, shard_rows, width), single),
            VMEM((rows, width), single),
            VMEM((2 * layers, rows, width), single),
            VMEM((2 * layers, rows, 1), single),
            VMEM((layers, rows, width), bfloat),
            VMEM((layers, rows, width), bfloat),
            VMEM((layers, 3, rows, width), bfloat),
            VMEM((layers, 2 * pairs, rows // 2, rows), single),
            VMEM((layers, rows, width), bfloat),
            VMEM((layers, BLOCKS, rows, width), bfloat),
            VMEM((layers, BLOCKS, rows, width), single),
            VMEM((3, rows, width), bfloat),
            VMEM((rows, width), bfloat),
            VMEM((rows, width), single),
            VMEM((2, width, rows), bfloat),
            VMEM((entries, width), single),
            VMEM(small, single),
            VMEM(small, single),
            VMEM(small, single),
            VMEM(small, single),
            VMEM((z_count, *small), single),
            VMEM((2, *small), single),
            VMEM((2 * dp, 8, 128), single),
            dma((mats, z_count, 2)),
            dma((mats,)),
            dma((mats, 2, z_count, 2)),
            dma((mats,)),
            *[dma((mats, z_count))] * 8,
            *[dma((mats,))] * 4,
            dma((3 + z_count,)),
            dma((3 + z_count,)),
            dma((2 * dp,)),
            dma((2 * dp,)),
            pltpu.SemaphoreType.REGULAR((3, mats)),
            dma((7,)),
            dma((mats, 2)),
            dma((2,)),
            dma((mats,)),
        ],
        compiler_params=pltpu.CompilerParams(collective_id=1, has_side_effects=True, vmem_limit_bytes=60 * 2**20),
        name="train_step",
    )(pieces, tags, counts, cotangent, *weights, gain, bias, table)


def update_kernel(layers, norms, *refs):
    norm_ref, grad_in, small_ref, emb_in, dx_in = refs[:5]
    state_in, (emb_out, dx_out, root_ref), state_out = refs[5:29], refs[29:32], refs[32:56]
    held, (emb_ref, dx_ref, grad_ref, load_sem, store_sem, pass_sem) = refs[56:80], refs[80:]
    passing = [pltpu.make_async_copy(emb_in, emb_ref, pass_sem.at[0]), pltpu.make_async_copy(dx_in, dx_ref, pass_sem.at[1])]
    passed = [pltpu.make_async_copy(emb_ref, emb_out, pass_sem.at[2]), pltpu.make_async_copy(dx_ref, dx_out, pass_sem.at[3])]
    loads = [pltpu.make_async_copy(state_in[at], held[at], load_sem.at[at]) for at in range(24)]
    stores = [pltpu.make_async_copy(held[at], state_out[at], store_sem.at[at]) for at in range(24)]
    grads = pltpu.make_async_copy(grad_in, grad_ref, pass_sem.at[4])
    grads.start()
    for copy in loads[:9]:
        copy.start()
    root = jnp.sqrt(norm_ref[0:1, 0:1])
    root_ref[...] = root
    clip_scale = jnp.minimum(1.0, clip_level / (root + 1e-06))
    width = grad_ref.shape[3]
    proj = 3 * layers

    def piece(base, at, gradient, decay, rate):
        weight, first, second = (held[3 * base + kind] for kind in range(3))
        new = adam_update(weight[at], first[at], second[at], gradient.astype(single), clip_scale, decay, rate)
        weight[at], first[at], second[at] = new

    def group(base, work, ahead=()):
        for copy in loads[3 * base : 3 * base + 3]:
            copy.wait()
        for copy in ahead:
            copy.start()
        work()
        for copy in stores[3 * base : 3 * base + 3]:
            copy.start()

    def each_layer(body):
        def wrapped(layer, carry):
            body(layer)
            return carry

        return lambda: lax.fori_loop(0, layers, wrapped, 0)

    def lanes(block):
        return slice(block * width, (block + 1) * width)

    def front(layer):
        for part in range(3):
            piece(0, (layer, part), grad_ref[3 * layer, part], decay_rate, learn_rate)

    def outward(layer):
        piece(1, (layer,), grad_ref[3 * layer, 3], decay_rate, learn_rate)

    def rise(layer):
        for block in range(BLOCKS):
            piece(2, (layer, slice(None), lanes(block)), grad_ref[3 * layer + 1, block], decay_rate, learn_rate)

    def fall(layer):
        for block in range(BLOCKS):
            piece(3, (layer, slice(None), lanes(block)), grad_ref[3 * layer + 2, block], decay_rate, learn_rate)

    def project():
        for block in range(BLOCKS):
            piece(4, (slice(None), lanes(block)), grad_ref[proj, block], decay_rate, learn_rate)

    grads.wait()
    group(0, each_layer(front), loads[9:12])
    group(1, each_layer(outward), loads[12:15])
    group(2, each_layer(rise), passing + loads[15:])
    group(3, each_layer(fall))
    for arrived, copy in zip(passing, passed):
        arrived.wait()
        copy.start()
    group(4, project)
    whole = (slice(None), slice(None))
    group(5, lambda: piece(5, whole, small_ref[:norms], 0.0, small_rate))
    group(6, lambda: piece(6, whole, small_ref[SLOTS : SLOTS + norms], 0.0, small_rate))
    group(7, lambda: piece(7, whole, small_ref[2 * SLOTS : 2 * SLOTS + held[21].shape[0]], 0.0, small_rate))
    for copy in stores + passed:
        copy.wait()


def update(square_total, reduced, small_total, embeddings, input_grad, state, layers, norms):
    vmem = pl.BlockSpec(memory_space=VMEM)
    where_it_is = pl.BlockSpec(memory_space=pltpu.HBM)
    dma = pltpu.SemaphoreType.DMA
    like = lambda array: jax.ShapeDtypeStruct(array.shape, single)
    return pl.pallas_call(
        functools.partial(update_kernel, layers, norms),
        out_shape=(like(embeddings), like(input_grad), jax.ShapeDtypeStruct((1, 1), single), *map(like, state)),
        in_specs=[vmem, where_it_is, vmem] + [where_it_is] * 26,
        out_specs=(where_it_is, where_it_is, vmem) + (where_it_is,) * 24,
        scratch_shapes=[*[VMEM(array.shape, single) for array in (*state, embeddings, input_grad)], VMEM(reduced.shape, bfloat), dma((24,)), dma((24,)), dma((5,))],
        compiler_params=pltpu.CompilerParams(vmem_limit_bytes=60 * 2**20),
        name="update",
    )(square_total, reduced, small_total, embeddings, input_grad, *state)


def adam_update(weight, first, second, gradient, clip_scale, decay, step_rate):
    clipped = gradient * clip_scale
    first_new = beta_first * first + (1.0 - beta_first) * clipped
    second_new = beta_second * second + (1.0 - beta_second) * clipped * clipped
    first_hat = first_new / (1.0 - beta_first**STEP)
    second_hat = second_new / (1.0 - beta_second**STEP)
    weight_new = weight - step_rate * (first_hat / (jnp.sqrt(second_hat) + adam_eps) + decay * weight)
    return (weight_new, first_new, second_new)


def per_device(
    pieces, script_tags, counts, cotangent,
    qkv_weight, qkv_first, qkv_second,
    out_weight, out_first, out_second,
    up_weight, up_first, up_second,
    down_weight, down_first, down_second,
    proj_weight, proj_first, proj_second,
    norm_gain, gain_first, gain_second,
    norm_bias, bias_first, bias_second,
    group_table, table_first, table_second,
):
    layers = qkv_weight.shape[0]
    dp = lax.axis_size("dp")
    norms = norm_gain.shape[0]

    def turn(array):
        return jnp.swapaxes(array, 1, 2)

    state = (
        qkv_weight, qkv_first, qkv_second,
        turn(out_weight), turn(out_first), turn(out_second),
        up_weight, up_first, up_second,
        turn(down_weight), turn(down_first), turn(down_second),
        proj_weight, proj_first, proj_second,
        norm_gain, gain_first, gain_second,
        norm_bias, bias_first, bias_second,
        group_table, table_first, table_second,
    )
    embeddings, input_grad, reduced, small_total, square_total = train_step(
        jnp.swapaxes(pieces, 0, 1), script_tags.reshape(1, -1), counts.reshape(1, -1), cotangent, state[0:15:3],
        norm_gain, norm_bias, group_table, layers, dp,
    )
    embeddings, input_grad, grad_norm, *state = update(
        square_total, reduced, small_total, embeddings, input_grad, state, layers, norms
    )
    state[3:6] = map(turn, state[3:6])
    state[9:12] = map(turn, state[9:12])
    return (embeddings, jnp.swapaxes(input_grad, 0, 1), grad_norm.reshape(()), *state)


def solution(mesh):
    entry_split = ("dp", "mp")
    weight_specs = (P(None, None, "dp", None), P(None, None, "dp"), P(None, "dp", None), P(None, None, "dp"), P("dp", None))
    state = tuple(spec for spec in weight_specs for _ in range(3)) + (P(),) * 9
    return jax.shard_map(
        per_device,
        mesh=mesh,
        in_specs=(P(entry_split, None, None), P(entry_split), P(entry_split), P(entry_split, None)) + state,
        out_specs=(P(entry_split, None), P(entry_split, None, None), P()) + state,
        check_vma=False,
    )
```

```python
import functools
import math

import jax
import jax.numpy as jnp
from jax import lax
from jax.experimental import pallas as pl
from jax.experimental.pallas import tpu as pltpu
from jax.sharding import PartitionSpec as P

HD = 64
PIECES = 7
SLOTS = 8
STEP = 10
BLOCKS = 4
SMALL_ROWS = 32

norm_eps = 1e-05
beta_first = 0.9
beta_second = 0.999
adam_eps = 1e-08
learn_rate = 0.03
small_rate = 0.5
decay_rate = 0.01
clip_level = 1.0
masked_score = -1000000000.0
bfloat = jnp.bfloat16
single = jnp.float32
highest = lax.Precision.HIGHEST
MESH = pl.DeviceIdType.MESH
VMEM = pltpu.VMEM


def place():
    along, across = lax.axis_index("dp"), lax.axis_index("mp")
    return lax.div(along, 2), lax.rem(along, 2), lax.div(across, 2), lax.rem(across, 2)


def device(z, y, x, c):
    return (z * 2 + y, x * 2 + c)


def remote(src, dst, send_sem, recv_sem, target):
    return pltpu.make_async_remote_copy(
        src_ref=src, dst_ref=dst, send_sem=send_sem, recv_sem=recv_sem, device_id=target, device_id_type=MESH
    )


def await_arrival(dst, send_sem, recv_sem, target):
    remote(dst, dst, send_sem, recv_sem, target).wait_recv()


def greet(z_count):
    z, y, x, c = place()
    barrier = pltpu.get_barrier_semaphore()

    def signal(target):
        pl.semaphore_signal(barrier, inc=1, device_id=target, device_id_type=MESH)

    signal(device(z, y, 1 - x, c))
    signal(device(z, y, x, 1 - c))
    dp = 2 * z_count

    def one(step):
        other = lax.rem(z * 2 + y + step, dp)
        signal((other, x * 2 + c))
        signal((other, x * 2 + 1 - c))

    loop(1, dp, one)
    return lambda: pl.semaphore_wait(barrier, 2 * dp)


def when(condition, body):
    if isinstance(condition, bool):
        if condition:
            body()
    else:
        pl.when(condition)(body)


def otherwise(condition):
    return not condition if isinstance(condition, bool) else jnp.logical_not(condition)


def loop(low, high, body):
    if high - low <= 8:
        for step in range(low, high):
            body(step)
    else:

        def wrapped(step, carry):
            body(step)
            return carry

        lax.fori_loop(low, high, wrapped, 0)


def dot_nn(left_side, right_side):
    return lax.dot_general(left_side, right_side, (((1,), (0,)), ((), ())), preferred_element_type=single)


def dot_nt(left_side, right_side):
    return lax.dot_general(left_side, right_side, (((1,), (1,)), ((), ())), preferred_element_type=single)


def dot_tn(left_side, right_side):
    return lax.dot_general(left_side, right_side, (((0,), (0,)), ((), ())), preferred_element_type=single)


def normalize(values):
    centre = jnp.mean(values, axis=-1, keepdims=True)
    offset = values - centre
    spread = jnp.mean(offset * offset, axis=-1, keepdims=True)
    scale = lax.rsqrt(spread + norm_eps)
    return offset * scale, scale


def normalize_back(grad, unit, scale, gain_row):
    grad_unit = grad * gain_row
    first = jnp.mean(grad_unit, axis=-1, keepdims=True)
    second = jnp.mean(grad_unit * unit, axis=-1, keepdims=True)
    return scale * (grad_unit - first - unit * second)


def shared_gather(layers, index, zz):
    return jnp.logical_or(index == 3 * layers - 1, lax.rem(index * 4 + zz, 8) == 0)


def shared_reduce(index, target):
    return lax.rem(index + target, 2) == 1


AHEAD = 1
LAGS = (1, 2, 3)
REDUCE = (0, 3, 6, 8, 11, 15)
SHIFT = 0
MARKS = (4, 8, 12, 16)


def step_kernel(
    layers, z_count,
    pieces_hbm, tags_hbm, counts_hbm, cot_hbm, qkv_hbm, outward_hbm, rise_hbm, fall_hbm, proj_hbm, gain_hbm, bias_hbm, table_hbm,
    emb_hbm, dx_hbm, out_hbm, total_ref, norm_ref,
    out_ref,
    pieces_ref, tags_ref, counts_ref, cot_ref, gain_ref, bias_ref, table_ref, emb_ref, dx_ref, sum_ref,
    w_ref, grad_ref, z_buf, f_buf, part_ref,
    x_ref, unit_ref, scale_ref, a_ref, b_ref, qkv_ref, prob_ref, o_ref, g_ref, slope_ref, dqkv_ref, do_ref, acc_ref, turn_ref, dpool_ref,
    small_ref, s_c, s_x, s_y, s_z, s_cur, n_buf,
    gx_ss, gc_ss, g_rs, gc_rs,
    c_ss, c_rs, x_ss, x_rs, y_ss, y_rs, z_ss, z_rs, fx_ss, fx_rs, fc_ss, fc_rs, s_ss, s_rs, n_ss, n_rs, credit,
    in_sem, load_sem, store_sem, out_sem,
):
    mats = 3 * layers + 1
    proj = 3 * layers
    final = 2 * layers
    _, entries, width = pieces_ref.shape
    rows = entries * SLOTS
    half = rows // 2
    group = entries // 2
    groups = table_ref.shape[0]
    pairs = width // 128
    dp = 2 * z_count
    shard_rows = out_ref.shape[2]
    z, y, x, c = place()
    me = z * 2 + y
    y_side, x_side, c_side = device(z, 1 - y, x, c), device(z, y, 1 - x, c), device(z, y, x, 1 - c)
    all_here = greet(z_count)


    inputs = [
        pltpu.make_async_copy(src, dst, in_sem.at[at])
        for at, (src, dst) in enumerate(
            (
                (tags_hbm, tags_ref), (counts_hbm, counts_ref), (pieces_hbm, pieces_ref), (table_hbm, table_ref),
                (gain_hbm, gain_ref), (bias_hbm, bias_ref), (cot_hbm, cot_ref),
            )
        )
    ]

    def shard_slot(index, block):
        at = 2 * index + block
        return slope_ref.at[at % layers, at // layers % BLOCKS, pl.ds(at // (layers * BLOCKS) * shard_rows, shard_rows)]

    def load(index, block, src):
        return pltpu.make_async_copy(src, shard_slot(index, block), load_sem.at[index, block])

    def each_load(act):
        for first in range(mats):
            index = gather_order[first]
            layer, kind = divmod(index, 3)
            for block in range(2):
                if index == proj or kind:
                    source = proj_hbm if index == proj else (rise_hbm, fall_hbm)[kind - 1].at[layer]
                    act(index, block, load(index, block, source.at[:, pl.ds(pl.multiple_of((2 * c + block) * width, width), width)]))
                else:
                    choice = (qkv_hbm.at[layer, block], qkv_hbm.at[layer, 2] if block == 0 else outward_hbm.at[layer])
                    for core in range(2):
                        pl.when(c == core)(functools.partial(act, index, block, load(index, block, choice[core])))

    gather_order = [*range(3 * (layers - 1)), proj, *range(3 * (layers - 1), proj)]

    def place_block(index, block, copy):
        copy.wait()
        w_ref[index, 2 * c + block, z, y] = shard_slot(index, block)[...].astype(bfloat)

    each_load(lambda index, block, copy: copy.start())
    for copy in inputs:
        copy.start()
    each_load(place_block)
    all_here()


    def matrix_at(turn):
        early = 3 * (layers - 1)
        return jnp.where(turn < early, turn, jnp.where(turn == early, proj, turn - 1))

    def by_type(index, zz, body):
        shared = shared_gather(layers, index, zz)
        when(shared, lambda: body(pl.ds(2 * c, 2), False))
        when(otherwise(shared), lambda: body(pl.ds(2 * c + x, 1), True))

    def gather_z(index, other, span):
        return remote(
            w_ref.at[index, span, z, y], w_ref.at[index, span, z, y], z_ss.at[index, other], g_rs.at[index, 0, z, y], device(other, y, x, c)
        )

    def gather_y(index, zz, span):
        spot = w_ref.at[index, span, zz, y]
        return remote(spot, spot, y_ss.at[index, zz], g_rs.at[index, 0, zz, y], y_side)

    def gather_x(index, zz, yy, span):
        spot = w_ref.at[index, span, zz, yy]
        return remote(spot, spot, gx_ss.at[index, zz, yy], g_rs.at[index, 1, zz, yy], x_side)

    def gather_c(index):
        pair = w_ref.at[index, pl.ds(2 * c, 2)]
        return remote(pair, pair, gc_ss.at[index], gc_rs.at[index], c_side)

    def arrived(index, zz, yy, span):
        await_arrival(w_ref.at[index, span, zz, yy], y_ss.at[index, zz], g_rs.at[index, 0, zz, yy], y_side)

    def own(index):
        def send(span, cross):
            gather_y(index, z, span).start()

            def one(other):
                pl.when(other != z)(lambda: gather_z(index, other, span).start())

            loop(0, z_count, one)

        by_type(index, z, send)

    def line(index):
        def one(zz):
            def pass_on(span, cross):
                arrived(index, zz, y, span)
                if cross:
                    gather_x(index, zz, y, span).start()
                gather_y(index, zz, span).start()

            pl.when(z != zz)(lambda: by_type(index, zz, pass_on))

        loop(0, z_count, one)

    def beside(index):
        def one(zz):
            def pass_on(span, cross):
                arrived(index, zz, 1 - y, span)
                if cross:
                    gather_x(index, zz, 1 - y, span).start()

            by_type(index, zz, pass_on)

        loop(0, z_count, one)

    def opposite(index):
        def each(zz):
            def one(yy):
                block = w_ref.at[index, pl.ds(2 * c + 1 - x, 1), zz, yy]
                await_arrival(block, gx_ss.at[index, zz, yy], g_rs.at[index, 1, zz, yy], x_side)

            def two():
                pl.when(zz != z)(lambda: one(y))
                one(1 - y)

            when(otherwise(shared_gather(layers, index, zz)), two)

        loop(0, z_count, each)
        gather_c(index).start()

    def finish(index):
        pair = w_ref.at[index, pl.ds(2 * (1 - c), 2)]
        await_arrival(pair, gc_ss.at[index], gc_rs.at[index], c_side)

    def gather_sent(index):
        def each(zz):
            def done(span, cross):
                gather_y(index, zz, span).wait_send()
                if cross:
                    pl.when(zz != z)(lambda: gather_x(index, zz, y, span).wait_send())
                    gather_x(index, zz, 1 - y, span).wait_send()

                def one(other):
                    pl.when(other != z)(lambda: gather_z(index, other, span).wait_send())

                pl.when(zz == z)(lambda: loop(0, z_count, one))

            by_type(index, zz, done)

        loop(0, z_count, each)
        gather_c(index).wait_send()

    def block_of(index, block):
        return w_ref[index, block].reshape(width, width)

    def put_grad(index, block, values):
        grad_ref[index, block] = values.astype(bfloat).reshape(grad_ref.shape[2:])


    units = mats * z_count
    pair_c = pl.ds(2 * c, 2)

    def order(unit):
        return mats - 1 - lax.div(unit, z_count), lax.rem(unit, z_count)

    def local(span):
        return pl.ds(2 * c, 2) if span is None else pl.ds(2 * c + x, 1)

    def near(span):
        return pl.ds(0, 2) if span is None else pl.ds(x, 1)

    def to_c(index, target):
        return remote(
            grad_ref.at[index, pl.ds(2 * (1 - c), 2), target], w_ref.at[index, pl.ds(2 * c, 2), target],
            c_ss.at[index, target], c_rs.at[index, target], c_side,
        )

    def from_c(index, target):
        await_arrival(w_ref.at[index, pl.ds(2 * (1 - c), 2), target], c_ss.at[index, target], c_rs.at[index, target], c_side)

    def to_x(index, target):
        return remote(
            grad_ref.at[index, 2 * c + 1 - x, target], w_ref.at[index, 2 * c, target], x_ss.at[index, target], x_rs.at[index, target], x_side
        )

    def to_y(index, target, span):
        return remote(
            grad_ref.at[index, local(span), target, 1 - y], w_ref.at[index, 2 * c + 1, target, near(span)],
            y_ss.at[index, target], y_rs.at[index, target], y_side,
        )

    relays = z_count >= 4

    def at_far_end(target):
        return jnp.logical_and(relays, jnp.abs(target - z) == z_count - 1)

    def passes_on(target):
        up = jnp.logical_and(target == z_count - 1, z == 1)
        down = jnp.logical_and(target == 0, z == z_count - 2)
        return jnp.logical_and(relays, jnp.logical_or(up, down))

    def to_z(index, target, span):
        far = at_far_end(target)
        there = jnp.where(far, jnp.where(z == 0, 1, z_count - 2), target)
        slot = jnp.where(far, there, z)
        return remote(
            grad_ref.at[index, local(span), target, y], z_buf.at[index, near(span), slot],
            z_ss.at[index, target], z_rs.at[index, slot], device(there, y, x, c),
        )

    def from_z(index, source, span):
        other = jnp.where(source == z, jnp.where(z == 1, 0, z_count - 1), source)
        await_arrival(z_buf.at[index, near(span), source], z_ss.at[index, source], z_rs.at[index, source], device(other, y, x, c))

    def both(shared, body):
        when(shared, lambda: body(None))
        when(otherwise(shared), lambda: body(1))

    def add(ref, at, extra):
        ref[at] = (ref[at].astype(single) + extra.astype(single)).astype(bfloat)

    def give_credit(index, kinds):
        for kind in kinds:
            side = (c_side, x_side, y_side)[kind]
            pl.semaphore_signal(credit.at[kind, index], inc=1, device_id=side, device_id_type=MESH)

    def start_matrix(index):
        give_credit(index, (0,))
        pl.semaphore_wait(credit.at[0, index], 1)
        loop(0, z_count, lambda target: to_c(index, target).start())

    def stage_c(unit):
        index, target = order(unit)
        from_c(index, target)
        for block in range(2):
            add(grad_ref, (index, 2 * c + block, target), w_ref[index, 2 * (1 - c) + block, target])
        shared = shared_reduce(index, target)

        @pl.when(target == 0)
        def _():
            pl.semaphore_wait(credit.at[1, index], 1)
            pl.semaphore_wait(credit.at[2, index], 1)

        when(shared, lambda: to_y(index, target, None).start())
        when(otherwise(shared), lambda: to_x(index, target).start())

    def stage_x(unit):
        index, target = order(unit)

        @pl.when(otherwise(shared_reduce(index, target)))
        def _():
            to_x(index, target).wait_recv()
            add(grad_ref, (index, 2 * c + x, target), w_ref[index, 2 * c, target])
            to_y(index, target, 1).start()

    def stage_y(unit):
        index, target = order(unit)

        def make(span):
            to_y(index, target, span).wait_recv()
            add(grad_ref, (index, local(span), target, y), w_ref[index, 2 * c + 1, target, near(span)])
            pl.when(jnp.logical_and(target != z, jnp.logical_not(passes_on(target))))(lambda: to_z(index, target, span).start())

        both(shared_reduce(index, target), make)

    def stage_r(unit):
        index, target = order(unit)

        def make(span):
            from_z(index, z, span)
            add(grad_ref, (index, local(span), target, y), z_buf[index, near(span), z])
            to_z(index, target, span).start()

        pl.when(passes_on(target))(lambda: both(shared_reduce(index, target), make))

    def final_shared(index):
        return remote(f_buf.at[index, 0], f_buf.at[index, 1], fx_ss.at[index], fx_rs.at[index], x_side)

    def final_split(index):
        mine = out_ref.at[index, 2 * c + x]
        return remote(mine, mine, fx_ss.at[index], fx_rs.at[index], x_side)

    def final_c(index):
        pair = out_ref.at[index, pl.ds(2 * c, 2)]
        return remote(pair, pair, fc_ss.at[index], fc_rs.at[index], c_side)

    def stage_z(step):
        index = mats - 1 - step

        def make(span):
            def sends(source):
                far = jnp.logical_and(relays, jnp.abs(source - z) == z_count - 1)
                return jnp.logical_and(source != z, jnp.logical_not(far))

            def one(source):
                pl.when(sends(source))(lambda: from_z(index, source, span))

            loop(0, z_count, one)
            part_ref[near(span)] = grad_ref[index, local(span), z, y].astype(single)

            def more(source):
                @pl.when(sends(source))
                def _():
                    part_ref[near(span)] = part_ref[near(span)] + z_buf[index, near(span), source].astype(single)

            loop(0, z_count, more)

        shared = shared_reduce(index, z)
        both(shared, make)

        @pl.when(shared)
        def _():
            f_buf[index, 0] = part_ref[...].astype(bfloat)
            final_shared(index).start()

        @pl.when(otherwise(shared))
        def _():
            out_ref[index, pl.ds(2 * c + x, 1)] = part_ref[pl.ds(x, 1)].astype(bfloat)
            final_split(index).start()

    def stage_f(step):
        index = mats - 1 - step
        shared = shared_reduce(index, z)

        @pl.when(shared)
        def _():
            final_shared(index).wait_recv()
            total = f_buf[index, 0].astype(single) + f_buf[index, 1].astype(single)
            out_ref[index, pl.ds(2 * c, 2)] = total.astype(bfloat)

        @pl.when(otherwise(shared))
        def _():
            final_split(index).wait_recv()

        final_c(index).start()
        values = out_ref[index, pl.ds(2 * c, 2)].astype(single)
        sum_ref[...] += jnp.sum((values * values).reshape(-1, 8, width), axis=0)

    def reduce_tick(step):
        for lag, stage in reversed(list(zip(REDUCE, (stage_c, stage_x, stage_y, stage_r)))):
            unit = step - lag
            pl.when(jnp.logical_and(unit >= 0, unit < units))(functools.partial(stage, unit))
        for lag, stage in zip(REDUCE[4:], (stage_z, stage_f)):
            turn = step - lag
            whole = lax.div(turn, z_count)
            pl.when(jnp.logical_and(jnp.logical_and(turn >= 0, turn < units), turn == whole * z_count + z_count - 1))(
                functools.partial(stage, whole)
            )

    def spread_ticks(first, count, turn, turns):
        each = -(-count // turns)

        def one(step):
            mine = turn * each + step
            pl.when(mine < count)(lambda: reduce_tick(first + mine))

        loop(0, each, one)

    def small_step(stage):
        if stage == 0:
            remote(small_ref, s_c, s_ss.at[0], s_rs.at[0], c_side).start()
        elif stage == 1:
            remote(small_ref, s_c, s_ss.at[0], s_rs.at[0], c_side).wait_recv()
            s_cur[0] = small_ref[...] + s_c[...]
            remote(s_cur.at[0], s_x, s_ss.at[1], s_rs.at[1], x_side).start()
        elif stage == 2:
            remote(s_cur.at[0], s_x, s_ss.at[1], s_rs.at[1], x_side).wait_recv()
            s_cur[1] = s_cur[0] + s_x[...]
            remote(s_cur.at[1], s_y, s_ss.at[2], s_rs.at[2], y_side).start()
        elif stage == 3:
            remote(s_cur.at[1], s_y, s_ss.at[2], s_rs.at[2], y_side).wait_recv()
            s_z[z] = s_cur[1] + s_y[...]

            def send(step, carry):
                other = lax.rem(z + step, z_count)
                remote(s_z.at[z], s_z.at[z], s_ss.at[3 + other], s_rs.at[3 + z], device(other, y, x, c)).start()
                return carry

            lax.fori_loop(1, z_count, send, 0)
        else:

            def wait(step, carry):
                other = lax.rem(z + step, z_count)
                remote(s_z.at[other], s_z.at[other], s_ss.at[3 + other], s_rs.at[3 + other], device(other, y, x, c)).wait_recv()
                return carry

            lax.fori_loop(1, z_count, wait, 0)

            def gather(step, carry):
                return carry + s_z[step]

            total_ref[...] = lax.fori_loop(0, z_count, gather, jnp.zeros(total_ref.shape, single))


    for first in range(AHEAD):
        own(matrix_at(first))
    for copy in inputs:
        copy.wait()
    sum_ref[...] = jnp.zeros_like(sum_ref)

    def upright(row):
        down = lax.broadcasted_iota(jnp.int32, (entries, entries), 0)
        along = lax.broadcasted_iota(jnp.int32, (entries, entries), 1)
        return jnp.sum(jnp.where(down == along, row, 0.0), axis=1, keepdims=True)

    def half_of(values, part):
        return values[part * group : (part + 1) * group]

    def spread_slots(values):
        return jnp.concatenate([half_of(values, part) for part in range(2) for _ in range(SLOTS)], axis=0)

    def sum_slots(values):
        sums = []
        for part in range(2):
            total = values[part * half : part * half + group]
            for slot in range(1, SLOTS):
                at = part * half + slot * group
                total = total + values[at : at + group]
            sums.append(total)
        return jnp.concatenate(sums, axis=0)

    tags_row = tags_ref[...].astype(single)
    counts_col = upright(counts_ref[...].astype(single))
    group_col = lax.broadcasted_iota(jnp.int32, (entries, groups), 1).astype(single)
    onehot = (group_col == upright(tags_row)).astype(single)
    table_rows = lax.dot_general(
        onehot, table_ref[...], (((1,), (0,)), ((), ())), precision=highest, preferred_element_type=single
    )
    for part in range(2):
        mine = half_of(table_rows, part)
        for slot in range(SLOTS):
            at = part * half + slot * group
            if slot < PIECES:
                x_ref[at : at + group, :] = mine + pieces_ref[slot, part * group : (part + 1) * group, :].astype(single)
            else:
                x_ref[at : at + group, :] = mine

    row_at = lax.broadcasted_iota(jnp.int32, (half, 2 * half), 0)
    key_at = lax.rem(lax.broadcasted_iota(jnp.int32, (half, 2 * half), 1), half)
    same = lax.rem(row_at, group) == lax.rem(key_at, group)
    key_slot = lax.div(key_at, group).astype(single)
    low_lane = lax.broadcasted_iota(jnp.int32, (half, 128), 1) < HD

    def key_mask(part):
        counts_here = jnp.concatenate([half_of(counts_col, part)] * SLOTS, axis=0)
        return jnp.logical_and(same, key_slot < counts_here)

    def split_pair(values):
        zero = jnp.zeros_like(values)
        return jnp.concatenate([jnp.where(low_lane, values, zero), jnp.where(low_lane, zero, values)], axis=0)

    def gain_at(norm):
        return gain_ref[pl.ds(norm, 1), :]

    def bias_at(norm):
        return bias_ref[pl.ds(norm, 1), :]

    def front(layer):
        values = x_ref[...]
        unit, scale = normalize(values)
        unit_ref[2 * layer] = unit
        scale_ref[2 * layer] = scale
        a = (unit * gain_at(2 * layer) + bias_at(2 * layer)).astype(bfloat)
        a_ref[layer] = a
        for part in range(3):
            qkv_ref[layer, part] = dot_nn(a, block_of(3 * layer, part)).astype(bfloat)
        for part in range(2):
            mask = key_mask(part)
            here = slice(part * half, (part + 1) * half)
            for pair in range(pairs):
                lanes = slice(pair * 128, (pair + 1) * 128)
                q = qkv_ref[layer, 0, here, lanes]
                keys = split_pair(qkv_ref[layer, 1, here, lanes])
                vals = split_pair(qkv_ref[layer, 2, here, lanes])
                scores = dot_nt(q, keys) * HD ** (-0.5)
                scores = jnp.where(mask, scores, masked_score)
                probs = []
                for head in range(2):
                    mine = scores[:, head * half : (head + 1) * half]
                    top = jnp.max(mine, axis=-1, keepdims=True)
                    raised = jnp.exp(mine - top)
                    probs.append(raised / jnp.sum(raised, axis=-1, keepdims=True))
                prob = jnp.concatenate(probs, axis=1)
                prob_ref[layer, part * pairs + pair] = prob
                o_ref[layer, here, lanes] = dot_nn(prob.astype(bfloat), vals).astype(bfloat)
        middle = values + dot_nt(o_ref[layer], block_of(3 * layer, 3))
        unit, scale = normalize(middle)
        unit_ref[2 * layer + 1] = unit
        scale_ref[2 * layer + 1] = scale
        b_ref[layer] = (unit * gain_at(2 * layer + 1) + bias_at(2 * layer + 1)).astype(bfloat)
        x_ref[...] = middle

    def rise(layer):
        def hidden(block, carry):
            u = dot_nn(b_ref[layer], block_of(3 * layer + 1, block))
            gate = 0.5 * (1.0 + lax.erf(u * math.sqrt(0.5)))
            g_ref[layer, block] = (u * gate).astype(bfloat)
            slope_ref[layer, block] = gate + u * (jnp.exp(-0.5 * u * u) * (1.0 / math.sqrt(2.0 * math.pi)))
            return carry

        lax.fori_loop(0, BLOCKS, hidden, 0)

    def fall(layer):
        def hidden(block, carry):
            x_ref[...] += dot_nt(g_ref[layer, block], block_of(3 * layer + 2, block))
            return carry

        lax.fori_loop(0, BLOCKS, hidden, 0)

    def project():
        total = jnp.zeros((entries, width), single)
        for block in range(BLOCKS):
            total += dot_nt(cot_ref[:, block * width : (block + 1) * width], block_of(proj, block))
        dpool_ref[...] = total

    depth = LAGS[-1]

    def gather_tick(step, carry):
        @pl.when(step + AHEAD < mats)
        def _():
            own(matrix_at(step + AHEAD))

        for lag, stage in [list(zip((0, *LAGS), (line, beside, opposite, finish)))[q] for q in (2, 1, 0, 3)]:
            turn = step - lag
            pl.when(jnp.logical_and(turn >= 0, turn < mats))(lambda: stage(matrix_at(turn)))
        index = matrix_at(step - depth)
        layer = lax.div(index, 3)
        ready = jnp.logical_and(step >= depth, index < proj)
        for kind, work in enumerate((front, rise, fall)):
            pl.when(jnp.logical_and(ready, lax.rem(index, 3) == kind))(lambda: work(layer))
        pl.when(jnp.logical_and(step >= depth, index == proj))(project)
        return carry

    lax.fori_loop(0, mats + depth, gather_tick, 0)


    unit, scale = normalize(x_ref[...])
    normed = unit * gain_at(final) + bias_at(final)
    slot_col = lax.div(lax.rem(lax.broadcasted_iota(jnp.int32, (rows, 1), 0), half), group).astype(single)
    used_col = (slot_col < spread_slots(counts_col)).astype(single)
    pooled_low = (sum_slots(normed * used_col) / counts_col).astype(bfloat)
    for block in range(BLOCKS):
        lanes = slice(block * width, (block + 1) * width)
        emb_ref[:, lanes] = dot_nn(pooled_low, block_of(proj, block))
        put_grad(proj, block, dot_tn(pooled_low, cot_ref[:, lanes]))
    lax.fori_loop(0, mats, lambda index, carry: (gather_sent(index), carry)[1], 0)
    start_matrix(proj)
    give_credit(proj, (1, 2))
    emb_out = pltpu.make_async_copy(emb_ref, emb_hbm, store_sem.at[0])
    emb_out.start()
    grad_normed = spread_slots(dpool_ref[...] / counts_col) * used_col
    small_ref[...] = jnp.zeros_like(small_ref)
    small_ref[pl.ds(final, 1), :] = jnp.sum(grad_normed * unit, axis=0, keepdims=True)
    small_ref[pl.ds(SLOTS + final, 1), :] = jnp.sum(grad_normed, axis=0, keepdims=True)
    acc_ref[...] = normalize_back(grad_normed, unit, scale, gain_at(final))

    def backward(step, carry):
        layer = layers - 1 - step
        tick = 3 * z_count * step
        grad_next = acc_ref[...]
        do_ref[...] = grad_next.astype(bfloat)
        turn_ref[0] = grad_next.T.astype(bfloat)
        turn_ref[1] = b_ref[layer].astype(single).T.astype(bfloat)
        x_ref[...] = jnp.zeros_like(x_ref)

        def hidden(turn, carry):
            block = lax.rem(turn + 2 * (1 - c), BLOCKS)
            spread_ticks(tick - SHIFT, z_count, turn, BLOCKS)
            put_grad(3 * layer + 2, block, dot_nn(turn_ref[0], g_ref[layer, block]))
            grad_act = dot_nn(do_ref[...], block_of(3 * layer + 2, block))
            du = (grad_act * slope_ref[layer, block]).astype(bfloat)
            put_grad(3 * layer + 1, block, dot_nn(turn_ref[1], du))
            x_ref[...] += dot_nt(du, block_of(3 * layer + 1, block))

            @pl.when(turn == 1)
            def _():
                start_matrix(3 * layer + 2)
                start_matrix(3 * layer + 1)

            return carry

        lax.fori_loop(0, BLOCKS, hidden, 0)
        give_credit(3 * layer + 2, (1, 2))
        give_credit(3 * layer + 1, (1, 2))
        grad_b = x_ref[...]
        unit = unit_ref[2 * layer + 1]
        small_ref[pl.ds(2 * layer + 1, 1), :] = jnp.sum(grad_b * unit, axis=0, keepdims=True)
        small_ref[pl.ds(SLOTS + 2 * layer + 1, 1), :] = jnp.sum(grad_b, axis=0, keepdims=True)
        grad_middle = grad_next + normalize_back(grad_b, unit, scale_ref[2 * layer + 1], gain_at(2 * layer + 1))
        acc_ref[...] = grad_middle
        dy = grad_middle.astype(bfloat)
        put_grad(3 * layer, 3, dot_nn(grad_middle.T.astype(bfloat), o_ref[layer]))
        do_ref[...] = dot_nn(dy, block_of(3 * layer, 3)).astype(bfloat)

        def attend(pair, carry):
            lanes = pl.ds(pl.multiple_of(pair * 128, 128), 128)
            spread_ticks(tick + z_count - SHIFT, 2 * z_count, pair, pairs)
            for part in range(2):
                here = slice(part * half, (part + 1) * half)
                q = qkv_ref[layer, 0, here, lanes]
                keys = split_pair(qkv_ref[layer, 1, here, lanes])
                vals = split_pair(qkv_ref[layer, 2, here, lanes])
                do = do_ref[here, lanes]
                prob = prob_ref[layer, part * pairs + pair]
                grad_prob = dot_nt(do, vals)
                product = grad_prob * prob
                scored = []
                for head in range(2):
                    spans = slice(head * half, (head + 1) * half)
                    total = jnp.sum(product[:, spans], axis=-1, keepdims=True)
                    scored.append(product[:, spans] - prob[:, spans] * total)
                ds_low = jnp.concatenate(scored, axis=1).astype(bfloat)
                dv = dot_tn(prob.astype(bfloat), do)
                dk = dot_tn(ds_low, q)
                dq = dot_nn(ds_low, keys)
                dqkv_ref[0, here, lanes] = (dq * HD ** (-0.5)).astype(bfloat)
                dqkv_ref[1, here, lanes] = (jnp.where(low_lane, dk[:half], dk[half:]) * HD ** (-0.5)).astype(bfloat)
                dqkv_ref[2, here, lanes] = jnp.where(low_lane, dv[:half], dv[half:]).astype(bfloat)
            return carry

        lax.fori_loop(0, pairs, attend, 0)
        turned = a_ref[layer].astype(single).T.astype(bfloat)
        grad_a = jnp.zeros((rows, width), single)
        for part in range(3):
            put_grad(3 * layer, part, dot_nn(turned, dqkv_ref[part]))
            grad_a += dot_nt(dqkv_ref[part], block_of(3 * layer, part))
        start_matrix(3 * layer)
        give_credit(3 * layer, (1, 2))
        unit = unit_ref[2 * layer]
        small_ref[pl.ds(2 * layer, 1), :] = jnp.sum(grad_a * unit, axis=0, keepdims=True)
        small_ref[pl.ds(SLOTS + 2 * layer, 1), :] = jnp.sum(grad_a, axis=0, keepdims=True)
        acc_ref[...] += normalize_back(grad_a, unit, scale_ref[2 * layer], gain_at(2 * layer))
        return carry

    lax.fori_loop(0, layers, backward, 0)
    group_row = lax.broadcasted_iota(jnp.int32, (groups, entries), 0).astype(single)
    spread = (group_row == tags_row).astype(single)
    small_ref[2 * SLOTS : 2 * SLOTS + groups, :] = lax.dot_general(
        spread, sum_slots(acc_ref[...]), (((1,), (0,)), ((), ())), precision=highest, preferred_element_type=single
    )
    small_step(0)
    for part in range(2):
        for slot in range(PIECES):
            at = part * half + slot * group
            dx_ref[slot, part * group : (part + 1) * group, :] = acc_ref[at : at + group, :]
    dx_out = pltpu.make_async_copy(dx_ref, dx_hbm, store_sem.at[1])
    dx_out.start()

    def tail_tick(step, carry):
        reduce_tick(step)
        return carry

    first, end = units - z_count - SHIFT, units + REDUCE[-1]
    marks = [first, *(min(first + mark, end) for mark in MARKS), end]
    for stage in range(4):
        lax.fori_loop(marks[stage], marks[stage + 1], tail_tick, 0)
        small_step(stage + 1)
    lax.fori_loop(marks[4], marks[5], tail_tick, 0)

    place_here = me * 2 + c
    n_buf[place_here] = functools.reduce(jnp.add, [sum_ref[:, at * 128 : (at + 1) * 128] for at in range(width // 128)])

    def send_norm(step):
        other = lax.rem(place_here + step, 2 * dp)
        return remote(
            n_buf.at[place_here], n_buf.at[place_here], n_ss.at[other], n_rs.at[place_here],
            (lax.div(other, 2), x * 2 + lax.rem(other, 2)),
        )

    def take_norm(step):
        other = lax.rem(place_here + step, 2 * dp)
        await_arrival(n_buf.at[other], n_ss.at[other], n_rs.at[other], (lax.div(other, 2), x * 2 + lax.rem(other, 2)))

    def out_copy(index):
        return pltpu.make_async_copy(out_ref.at[index], out_hbm.at[index], out_sem.at[index])

    def arrive(index):
        pair = out_ref.at[index, pl.ds(2 * (1 - c), 2)]
        await_arrival(pair, fc_ss.at[index], fc_rs.at[index], c_side)
        out_copy(index).start()

    def many(low, high, body):
        lax.fori_loop(low, high, lambda step, carry: (body(step), carry)[1], 0)

    many(1, 2 * dp, lambda step: send_norm(step).start())
    many(0, mats, arrive)
    many(1, 2 * dp, take_norm)

    def sum_norm(step, carry):
        return carry + n_buf[step]

    spread = lax.fori_loop(0, 2 * dp, sum_norm, jnp.zeros(n_buf.shape[1:], single))
    smalls = total_ref[...]
    norm_ref[...] = jnp.broadcast_to(
        jnp.sum(jnp.sum(spread, axis=0, keepdims=True), axis=1, keepdims=True)
        + jnp.sum(jnp.sum(smalls * smalls, axis=0, keepdims=True), axis=1, keepdims=True),
        norm_ref.shape,
    )

    def done_unit(unit, carry):
        index, target = order(unit)
        to_c(index, target).wait_send()
        shared = shared_reduce(index, target)
        when(otherwise(shared), lambda: to_x(index, target).wait_send())

        def make(span):
            to_y(index, target, span).wait_send()
            pl.when(target != z)(lambda: to_z(index, target, span).wait_send())

        both(shared, make)
        return carry

    lax.fori_loop(0, units, done_unit, 0)

    def done_mat(index, carry):
        shared = shared_reduce(index, z)
        when(shared, lambda: final_shared(index).wait_send())
        when(otherwise(shared), lambda: final_split(index).wait_send())
        final_c(index).wait_send()
        return carry

    lax.fori_loop(0, mats, done_mat, 0)
    remote(small_ref, s_c, s_ss.at[0], s_rs.at[0], c_side).wait_send()
    remote(s_cur.at[0], s_x, s_ss.at[1], s_rs.at[1], x_side).wait_send()
    remote(s_cur.at[1], s_y, s_ss.at[2], s_rs.at[2], y_side).wait_send()

    def done_z(step, carry):
        other = lax.rem(z + step, z_count)
        remote(s_z.at[z], s_z.at[z], s_ss.at[3 + other], s_rs.at[3 + z], device(other, y, x, c)).wait_send()
        return carry

    lax.fori_loop(1, z_count, done_z, 0)

    many(1, 2 * dp, lambda step: send_norm(step).wait_send())
    emb_out.wait()
    dx_out.wait()
    many(0, mats, lambda index: out_copy(index).wait())


def train_step(pieces, tags, counts, cotangent, weights, gain, bias, table, layers, dp):
    _, entries, width = pieces.shape
    shard_rows = weights[0].shape[2]
    mats = 3 * layers + 1
    rows = entries * SLOTS
    pairs = width // 128
    z_count = dp // 2
    small = (SMALL_ROWS, width)
    vmem = pl.BlockSpec(memory_space=VMEM)
    where_it_is = pl.BlockSpec(memory_space=pltpu.HBM)
    dma = pltpu.SemaphoreType.DMA
    whole = (mats, BLOCKS, z_count, 2, shard_rows, width)
    return pl.pallas_call(
        functools.partial(step_kernel, layers, z_count),
        out_shape=(
            jax.ShapeDtypeStruct(cotangent.shape, single),
            jax.ShapeDtypeStruct(pieces.shape, single),
            jax.ShapeDtypeStruct((mats, BLOCKS, shard_rows, width), bfloat),
            jax.ShapeDtypeStruct(small, single),
            jax.ShapeDtypeStruct((8, 128), single),
        ),
        in_specs=[where_it_is] * 12,
        out_specs=(where_it_is, where_it_is, where_it_is, vmem, vmem),
        scratch_shapes=[
            VMEM((mats, BLOCKS, shard_rows, width), bfloat),
            VMEM(pieces.shape, bfloat),
            VMEM(tags.shape, jnp.int32),
            VMEM(counts.shape, jnp.int32),
            VMEM(cotangent.shape, bfloat),
            VMEM(gain.shape, single),
            VMEM(bias.shape, single),
            VMEM(table.shape, single),
            VMEM(cotangent.shape, single),
            VMEM(pieces.shape, single),
            VMEM((8, width), single),
            VMEM(whole, bfloat),
            VMEM(whole, bfloat),
            VMEM((mats, 2, z_count, shard_rows, width), bfloat),
            VMEM((mats, 2, 2, shard_rows, width), bfloat),
            VMEM((2, shard_rows, width), single),
            VMEM((rows, width), single),
            VMEM((2 * layers, rows, width), single),
            VMEM((2 * layers, rows, 1), single),
            VMEM((layers, rows, width), bfloat),
            VMEM((layers, rows, width), bfloat),
            VMEM((layers, 3, rows, width), bfloat),
            VMEM((layers, 2 * pairs, rows // 2, rows), single),
            VMEM((layers, rows, width), bfloat),
            VMEM((layers, BLOCKS, rows, width), bfloat),
            VMEM((layers, BLOCKS, rows, width), single),
            VMEM((3, rows, width), bfloat),
            VMEM((rows, width), bfloat),
            VMEM((rows, width), single),
            VMEM((2, width, rows), bfloat),
            VMEM((entries, width), single),
            VMEM(small, single),
            VMEM(small, single),
            VMEM(small, single),
            VMEM(small, single),
            VMEM((z_count, *small), single),
            VMEM((2, *small), single),
            VMEM((2 * dp, 8, 128), single),
            dma((mats, z_count, 2)),
            dma((mats,)),
            dma((mats, 2, z_count, 2)),
            dma((mats,)),
            *[dma((mats, z_count))] * 8,
            *[dma((mats,))] * 4,
            dma((3 + z_count,)),
            dma((3 + z_count,)),
            dma((2 * dp,)),
            dma((2 * dp,)),
            pltpu.SemaphoreType.REGULAR((3, mats)),
            dma((7,)),
            dma((mats, 2)),
            dma((2,)),
            dma((mats,)),
        ],
        compiler_params=pltpu.CompilerParams(collective_id=1, has_side_effects=True, vmem_limit_bytes=60 * 2**20),
        name="train_step",
    )(pieces, tags, counts, cotangent, *weights, gain, bias, table)


def update_kernel(layers, norms, *refs):
    norm_ref, grad_in, small_ref, emb_in, dx_in = refs[:5]
    state_in, (emb_out, dx_out, root_ref), state_out = refs[5:29], refs[29:32], refs[32:56]
    held, (emb_ref, dx_ref, grad_ref, load_sem, store_sem, pass_sem) = refs[56:80], refs[80:]
    passing = [pltpu.make_async_copy(emb_in, emb_ref, pass_sem.at[0]), pltpu.make_async_copy(dx_in, dx_ref, pass_sem.at[1])]
    passed = [pltpu.make_async_copy(emb_ref, emb_out, pass_sem.at[2]), pltpu.make_async_copy(dx_ref, dx_out, pass_sem.at[3])]
    loads = [pltpu.make_async_copy(state_in[at], held[at], load_sem.at[at]) for at in range(24)]
    stores = [pltpu.make_async_copy(held[at], state_out[at], store_sem.at[at]) for at in range(24)]
    grads = pltpu.make_async_copy(grad_in, grad_ref, pass_sem.at[4])
    grads.start()
    for copy in loads[:9]:
        copy.start()
    root = jnp.sqrt(norm_ref[0:1, 0:1])
    root_ref[...] = root
    clip_scale = jnp.minimum(1.0, clip_level / (root + 1e-06))
    width = grad_ref.shape[3]
    proj = 3 * layers

    def piece(base, at, gradient, decay, rate):
        weight, first, second = (held[3 * base + kind] for kind in range(3))
        new = adam_update(weight[at], first[at], second[at], gradient.astype(single), clip_scale, decay, rate)
        weight[at], first[at], second[at] = new

    def group(base, work, ahead=()):
        for copy in loads[3 * base : 3 * base + 3]:
            copy.wait()
        for copy in ahead:
            copy.start()
        work()
        for copy in stores[3 * base : 3 * base + 3]:
            copy.start()

    def each_layer(body):
        def wrapped(layer, carry):
            body(layer)
            return carry

        return lambda: lax.fori_loop(0, layers, wrapped, 0)

    def lanes(block):
        return slice(block * width, (block + 1) * width)

    def front(layer):
        for part in range(3):
            piece(0, (layer, part), grad_ref[3 * layer, part], decay_rate, learn_rate)

    def outward(layer):
        piece(1, (layer,), grad_ref[3 * layer, 3], decay_rate, learn_rate)

    def rise(layer):
        for block in range(BLOCKS):
            piece(2, (layer, slice(None), lanes(block)), grad_ref[3 * layer + 1, block], decay_rate, learn_rate)

    def fall(layer):
        for block in range(BLOCKS):
            piece(3, (layer, slice(None), lanes(block)), grad_ref[3 * layer + 2, block], decay_rate, learn_rate)

    def project():
        for block in range(BLOCKS):
            piece(4, (slice(None), lanes(block)), grad_ref[proj, block], decay_rate, learn_rate)

    grads.wait()
    group(0, each_layer(front), loads[9:12])
    group(1, each_layer(outward), loads[12:15])
    group(2, each_layer(rise), passing + loads[15:])
    group(3, each_layer(fall))
    for arrived, copy in zip(passing, passed):
        arrived.wait()
        copy.start()
    group(4, project)
    whole = (slice(None), slice(None))
    group(5, lambda: piece(5, whole, small_ref[:norms], 0.0, small_rate))
    group(6, lambda: piece(6, whole, small_ref[SLOTS : SLOTS + norms], 0.0, small_rate))
    group(7, lambda: piece(7, whole, small_ref[2 * SLOTS : 2 * SLOTS + held[21].shape[0]], 0.0, small_rate))
    for copy in stores + passed:
        copy.wait()


def update(square_total, reduced, small_total, embeddings, input_grad, state, layers, norms):
    vmem = pl.BlockSpec(memory_space=VMEM)
    where_it_is = pl.BlockSpec(memory_space=pltpu.HBM)
    dma = pltpu.SemaphoreType.DMA
    like = lambda array: jax.ShapeDtypeStruct(array.shape, single)
    return pl.pallas_call(
        functools.partial(update_kernel, layers, norms),
        out_shape=(like(embeddings), like(input_grad), jax.ShapeDtypeStruct((1, 1), single), *map(like, state)),
        in_specs=[vmem, where_it_is, vmem] + [where_it_is] * 26,
        out_specs=(where_it_is, where_it_is, vmem) + (where_it_is,) * 24,
        scratch_shapes=[*[VMEM(array.shape, single) for array in (*state, embeddings, input_grad)], VMEM(reduced.shape, bfloat), dma((24,)), dma((24,)), dma((5,))],
        compiler_params=pltpu.CompilerParams(vmem_limit_bytes=60 * 2**20),
        name="update",
    )(square_total, reduced, small_total, embeddings, input_grad, *state)


def adam_update(weight, first, second, gradient, clip_scale, decay, step_rate):
    clipped = gradient * clip_scale
    first_new = beta_first * first + (1.0 - beta_first) * clipped
    second_new = beta_second * second + (1.0 - beta_second) * clipped * clipped
    first_hat = first_new / (1.0 - beta_first**STEP)
    second_hat = second_new / (1.0 - beta_second**STEP)
    weight_new = weight - step_rate * (first_hat / (jnp.sqrt(second_hat) + adam_eps) + decay * weight)
    return (weight_new, first_new, second_new)


def per_device(
    pieces, script_tags, counts, cotangent,
    qkv_weight, qkv_first, qkv_second,
    out_weight, out_first, out_second,
    up_weight, up_first, up_second,
    down_weight, down_first, down_second,
    proj_weight, proj_first, proj_second,
    norm_gain, gain_first, gain_second,
    norm_bias, bias_first, bias_second,
    group_table, table_first, table_second,
):
    layers = qkv_weight.shape[0]
    dp = lax.axis_size("dp")
    norms = norm_gain.shape[0]

    def turn(array):
        return jnp.swapaxes(array, 1, 2)

    state = (
        qkv_weight, qkv_first, qkv_second,
        turn(out_weight), turn(out_first), turn(out_second),
        up_weight, up_first, up_second,
        turn(down_weight), turn(down_first), turn(down_second),
        proj_weight, proj_first, proj_second,
        norm_gain, gain_first, gain_second,
        norm_bias, bias_first, bias_second,
        group_table, table_first, table_second,
    )
    embeddings, input_grad, reduced, small_total, square_total = train_step(
        jnp.swapaxes(pieces, 0, 1), script_tags.reshape(1, -1), counts.reshape(1, -1), cotangent, state[0:15:3],
        norm_gain, norm_bias, group_table, layers, dp,
    )
    embeddings, input_grad, grad_norm, *state = update(
        square_total, reduced, small_total, embeddings, input_grad, state, layers, norms
    )
    state[3:6] = map(turn, state[3:6])
    state[9:12] = map(turn, state[9:12])
    return (embeddings, jnp.swapaxes(input_grad, 0, 1), grad_norm.reshape(()), *state)


def solution(mesh):
    entry_split = ("dp", "mp")
    weight_specs = (P(None, None, "dp", None), P(None, None, "dp"), P(None, "dp", None), P(None, None, "dp"), P("dp", None))
    state = tuple(spec for spec in weight_specs for _ in range(3)) + (P(),) * 9
    return jax.shard_map(
        per_device,
        mesh=mesh,
        in_specs=(P(entry_split, None, None), P(entry_split), P(entry_split), P(entry_split, None)) + state,
        out_specs=(P(entry_split, None), P(entry_split, None, None), P()) + state,
        check_vma=False,
    )
```
